32 devices in a mesh: groups: 2 (over x), outp: 8 (over z, y), inp: 2 (over core).
Axes of the slice: x: 2, y: 2, z: 4, core: 2. Of those that a mesh axis runs over, the one named last changes fastest.
Arguments:
- inputs: bfloat16 [1024, 8192], P(('groups', 'outp'), 'inp'), parts along dimension 0, may hold values from -6 to 6
- cotangent: bfloat16 [1024, 28672], P(('groups', 'inp'), 'outp'), parts along dimension 0, may hold values from -6 to 6
- weight: bfloat16 [8192, 28672], P('inp', 'outp'), may hold values from -0.0625 to 0.0625
- in_sketch: bfloat16 [64, 8192], P(None, 'inp'), may hold values from -0.0625 to 0.0625
- out_sketch: bfloat16 [64, 28672], P(None, 'outp'), may hold values from -0.03125 to 0.03125
Outputs:
- outputs: bfloat16 [1024, 28672], P(('groups', 'inp'), 'outp'), parts along dimension 0
- input_grad: bfloat16 [1024, 8192], P(('groups', 'outp'), 'inp'), parts along dimension 0
- sketches: float32 [8, 4096], P('groups'), parts along dimension 0
The draws below stay inside these ranges and needn't reach their ends.
There are 2 independent parts, one for each index of `groups`. The reference program is written for one: setup_inputs(seed, part) draws one part's arguments, and reference() takes and returns one part's arrays. A program takes and returns all parts, laid end to end along the dimension named above; an argument that names none is the same for every part. Nothing has to cross between parts.
All inputs are finite; a program needn't handle non-finite values.
Results may differ from the reference program's by a relative error of at most 0.001.
Values may be sent and summed in bfloat16 or wider, within the bound.
No kernel may reach another device: no remote copies, remote signals or barrier semaphores. Data moves between devices by JAX's collectives and lax.ppermute only.
A program may use at most 128 MiB of HBM per device.

```python
import jax
import jax.numpy as jnp
from jax import lax

D = 8192
FF = 28672
R = 64
LEN = 128
SEQS = 4
TOKENS = 512


def with_spikes(entries, own_key, source, target, blocks, factor):
    def block_of(position):
        return (jnp.arange(entries.shape[position]) // (entries.shape[position] // blocks)).reshape((-1,) + (1,) * (entries.ndim - 1 - position))

    near = jax.random.permutation(own_key, blocks)[block_of(target)]
    other_side = (block_of(target) + blocks // 2) % blocks
    return jnp.where((block_of(source) == near) | (block_of(source) == other_side), factor * entries, entries)


def steps_of(own_key, extent, split, smallest, top_value):
    def one(axis_at, shards_of):
        draws = jax.random.uniform(jax.random.fold_in(jax.random.fold_in(own_key, 6), axis_at), (shards_of,), jnp.float32, smallest / len(split), top_value / len(split))
        return jnp.repeat(jnp.exp(draws), extent[axis_at] // shards_of).reshape((-1,) + (1,) * (len(extent) - axis_at - 1))

    level = one(*split[0])
    for cut in split[1:]:
        level = level * one(*cut)
    return level


def scatter_about(own_key, shape, width, limit, shards=(), kind=jnp.bfloat16):
    values = width * jax.random.normal(own_key, shape, jnp.float32)
    if shards:
        values = values * steps_of(own_key, shape, shards, -0.22, 0.18)
    return jnp.clip(values, -limit, limit).astype(kind)


def heavy_noise(key, extent, scale, bound, cuts, heavy, held_as=jnp.bfloat16):
    result = scale * jax.random.normal(key, extent, jnp.float32)
    if cuts:
        result = result * steps_of(key, extent, cuts, -0.22, 0.18)
    return jnp.clip(with_spikes(result, jax.random.fold_in(key, 3), *heavy), -bound, bound).astype(held_as)


def setup_inputs(seed: int = 0, part: int = 0) -> dict:
    arg_keys = jax.random.split(jax.random.key(seed), 6)
    part_splits = jax.random.split(jax.random.fold_in(arg_keys[5], part), 6)
    return {
        "inputs": scatter_about(part_splits[0], (TOKENS, D), 1.0, 6.0, ((0, 8), (1, 2))),
        "cotangent": heavy_noise(part_splits[1], (TOKENS, FF), 1.0, 6.0, ((0, 2), (1, 8)), (1, 0, 8, 2.0)),
        "weight": scatter_about(arg_keys[2], (D, FF), D ** -0.5, 0.0625, ((0, 2), (1, 8))),
        "in_sketch": scatter_about(arg_keys[3], (R, D), D ** -0.5, 0.0625, ((1, 2),)),
        "out_sketch": scatter_about(arg_keys[4], (R, FF), FF ** -0.5, 0.03125, ((1, 8),)),
    }


def reference(inputs, cotangent, weight, in_sketch, out_sketch):
    outputs = jnp.dot(inputs, weight, preferred_element_type=jnp.float32).astype(jnp.bfloat16)
    input_grad = lax.dot_general(cotangent, weight, (((1,), (1,)), ((), ())), preferred_element_type=jnp.float32).astype(jnp.bfloat16)
    left = lax.dot_general(inputs, in_sketch, (((1,), (1,)), ((), ())), preferred_element_type=jnp.float32)
    right = lax.dot_general(cotangent, out_sketch, (((1,), (1,)), ((), ())), preferred_element_type=jnp.float32)
    left = left.reshape(SEQS, LEN, R)
    right = right.reshape(SEQS, LEN, R)
    sketches = jnp.einsum("stj,stk->sjk", left, right, precision=lax.Precision.HIGHEST)
    sketches = (sketches * (1.0 / (LEN ** 0.5))).reshape(SEQS, R * R)
    return outputs, input_grad, sketches
```

```python
import jax
import jax.numpy as jnp
from jax import lax
from jax.sharding import PartitionSpec as P

LEN = 128
FWD_PIECES = 7


def contract_last(left_side, right_side):
    return lax.dot_general(
        left_side, right_side, (((1,), (1,)), ((), ())), preferred_element_type=jnp.float32
    )


def body(inputs, cotangent, weight, in_sketch, out_sketch):
    n = lax.axis_size("outp")
    rows, feats = inputs.shape
    half = feats // 2
    me = lax.axis_index("outp")
    core = lax.axis_index("inp")
    ring = [k for k in range(n) if k % 2 == 0] + [k for k in reversed(range(n)) if k % 2 == 1]
    place = [ring.index(k) for k in range(n)]
    ring_arr = jnp.array(ring, jnp.int32)
    p = jnp.array(place, jnp.int32)[me]
    up = [(ring[k], ring[(k + 1) % n]) for k in range(n)]
    down = [(ring[(k + 1) % n], ring[k]) for k in range(n)]
    swap = [(0, 1), (1, 0)]

    def slot(offset):
        owner = ring_arr[lax.rem(p + offset + 2 * n, n)]
        return lax.rem(owner - core * (n // 2) + n, n) * rows

    grad_other = lax.ppermute(cotangent, "inp", swap)

    buf = jnp.zeros((n * rows, feats), inputs.dtype)
    buf = lax.dynamic_update_slice(buf, inputs, (slot(0), 0))
    a, b = inputs[:, :half], inputs[:, half:]
    for s in range(1, n):
        a = lax.ppermute(a, "outp", up)
        b = lax.ppermute(b, "outp", down)
        buf = lax.dynamic_update_slice(buf, a, (slot(-s), 0))
        buf = lax.dynamic_update_slice(buf, b, (slot(s), half))

    grad = jnp.concatenate([cotangent, grad_other], axis=0)
    right = lax.psum(contract_last(grad, out_sketch), "outp")
    g_up = contract_last(grad, weight[:half])
    g_down = contract_last(grad, weight[half:])

    a = lax.dynamic_slice(g_up, (slot(-1), 0), (rows, half))
    b = lax.dynamic_slice(g_down, (slot(1), 0), (rows, half))
    for s in range(2, n + 1):
        a = lax.ppermute(a, "outp", up)
        b = lax.ppermute(b, "outp", down)
        a = a + lax.dynamic_slice(g_up, (slot(-s), 0), (rows, half))
        b = b + lax.dynamic_slice(g_down, (slot(s), 0), (rows, half))
    input_grad = jnp.concatenate([a, b], axis=1).astype(jnp.bfloat16)

    mine = n * rows // 2
    cols = weight.shape[1] // FWD_PIECES
    outs = []
    for k in range(FWD_PIECES):
        w = weight[:, k * cols : (k + 1) * cols]
        send = jnp.dot(buf[mine:], w, preferred_element_type=jnp.float32)
        got = lax.ppermute(send, "inp", swap)
        own = jnp.dot(buf[:mine], w, preferred_element_type=jnp.float32)
        outs.append((own + got).astype(jnp.bfloat16))
    outputs = jnp.concatenate(outs, axis=1)

    width = in_sketch.shape[0]
    left = contract_last(buf, in_sketch)
    examples = n * rows // LEN
    left = left.reshape(examples, LEN, width)
    right = right.reshape(examples, LEN, width)
    part = jnp.einsum("stj,stk->sjk", left, right, precision=lax.Precision.HIGHEST)
    got = lax.ppermute(part, "inp", swap)
    total = part + jnp.roll(got, examples // 2, axis=0)
    total = jnp.where(core == 0, total, jnp.roll(total, examples // 2, axis=0))
    sketches = (total * (1.0 / LEN**0.5)).reshape(examples, width * width)
    return (outputs, input_grad, sketches)


def solution(mesh):
    placed = (
        P(("groups", "outp"), "inp"),
        P(("groups", "inp"), "outp"),
        P("inp", "outp"),
        P(None, "inp"),
        P(None, "outp"),
    )
    return jax.shard_map(
        body,
        mesh=mesh,
        in_specs=placed,
        out_specs=(P(("groups", "inp"), "outp"), P(("groups", "outp"), "inp"), P("groups", None)),
        check_vma=False,
    )
```

```python
import functools

import jax
import jax.numpy as jnp
from jax import lax
from jax.experimental import pallas as pl
from jax.experimental.pallas import tpu as pltpu
from jax.sharding import PartitionSpec as P

LEN = 128
LANES = 128
BLK = 16
SPAN = 248.0
SHIFT = 124.0
Y_FIRST = 2048
F_TILE = 512
H_TILE = 512
MIB = 1 << 20


def pick(extent, cap):
    best = LANES
    for t in range(LANES, min(cap, extent) + 1, LANES):
        if extent % t == 0:
            best = t
    return best


def contract_last(a, b):
    return lax.dot_general(a, b, (((1,), (1,)), ((), ())), preferred_element_type=jnp.float32)


def params(mib):
    return pltpu.CompilerParams(vmem_limit_bytes=mib * MIB)


def cost(flops, nbytes):
    return pl.CostEstimate(flops=flops, bytes_accessed=nbytes, transcendentals=0)


def encode_rows(tiles, msg, at):
    top = jnp.max(jnp.abs(tiles[0]), axis=1, keepdims=True)
    for v in tiles[1:]:
        top = jnp.maximum(top, jnp.max(jnp.abs(v), axis=1, keepdims=True))
    scale = jnp.maximum(top * 1.004, 2.0**-110).astype(jnp.bfloat16).astype(jnp.float32)
    gain = SPAN / scale
    col = 0
    for v in tiles:
        w = jnp.exp2(jnp.abs(v) * gain - SHIFT)
        msg[at, col : col + v.shape[1]] = jnp.where(v < 0, -w, w).astype(jnp.bfloat16)
        col += v.shape[1]
    msg[at, col : col + LANES] = jnp.broadcast_to(scale, (BLK, LANES)).astype(jnp.bfloat16)


def decode_rows(msg, at, tile, count):
    scale = msg[at, tile * count : tile * count + LANES].astype(jnp.float32)[:, :1] * (1.0 / SPAN)
    out = []
    for t in range(count):
        w = msg[at, t * tile : (t + 1) * tile].astype(jnp.float32)
        a = (jnp.log2(jnp.maximum(jnp.abs(w), 2.0**-SHIFT)) + SHIFT) * scale
        out.append(jnp.where(w < 0, -a, a))
    return out


def backward(idx, own, oth, w, count, tile, first, sketch, rows, nz, y_first):
    half, hidden = own.shape
    zh = nz // 2
    grown = rows if y_first else 2 * rows
    width = count * tile

    def kernel(idx, own, oth, w, *rest):
        if y_first:
            sk, msg, keep, right, total = rest
        else:
            total, up, down = rest
        j = pl.program_id(0)
        z, y, core = idx[0], idx[1], idx[2]
        total[j, core] = contract_last(own[...], w[...])
        total[j, 1 - core] = contract_last(oth[...], w[...])
        if y_first:

            @pl.when(j == 0)
            def _():
                right[core] = contract_last(own[...], sk[...])
                right[1 - core] = contract_last(oth[...], sk[...])

            @pl.when(j == count - 1)
            def _():
                @pl.loop(0, nz * rows // BLK)
                def _(b):
                    zz, off = b // (rows // BLK), (b % (rows // BLK)) * BLK
                    base = (zz % zh) * 2 * rows + off
                    away = pl.ds(pl.multiple_of(base + (1 - y) * rows, BLK), BLK)
                    here = pl.ds(pl.multiple_of(base + y * rows, BLK), BLK)
                    at = pl.ds(pl.multiple_of(b * BLK, BLK), BLK)
                    encode_rows([total[t, zz // zh, away, :] for t in range(count)], msg, at)
                    for t in range(count):
                        keep[t, zz, pl.ds(pl.multiple_of(off, BLK), BLK), :] = total[
                            t, zz // zh, here, :
                        ]

        else:

            @pl.when(j == count - 1)
            def _():
                for msg, far in ((up, z + nz - 1), (down, z - nz + 1)):
                    zz = jnp.clip(far, 0, nz - 1)

                    @pl.loop(0, grown // BLK)
                    def _(b):
                        at = pl.ds(pl.multiple_of(b * BLK, BLK), BLK)
                        src = pl.ds(pl.multiple_of((zz % zh) * grown + b * BLK, BLK), BLK)
                        encode_rows([total[t, zz // zh, src, :] for t in range(count)], msg, at)

    once = pl.Buffered(1)
    whole = lambda *shape: pl.BlockSpec(shape, lambda j, s: (0,) * len(shape))
    in_specs = [
        pl.BlockSpec((half, hidden), lambda j, s: (0, 0), pipeline_mode=once),
        pl.BlockSpec((half, hidden), lambda j, s: (0, 0), pipeline_mode=once),
        pl.BlockSpec((tile, hidden), lambda j, s: (first + j, 0)),
    ]
    total_shape = (count, 2, half, tile)
    msg_shape = lambda r: jax.ShapeDtypeStruct((r, width + LANES), jnp.bfloat16)
    args = [idx, own, oth, w]
    if y_first:
        in_specs.append(whole(*sketch.shape))
        args.append(sketch)
        out_shape = [
            msg_shape(nz * rows),
            jax.ShapeDtypeStruct((count, nz, rows, tile), jnp.float32),
            jax.ShapeDtypeStruct((2, half, sketch.shape[0]), jnp.float32),
        ]
        scratch = [pltpu.VMEM(total_shape, jnp.float32)]
    else:
        out_shape = [
            jax.ShapeDtypeStruct(total_shape, jnp.float32),
            msg_shape(grown),
            msg_shape(grown),
        ]
        scratch = []
    return pl.pallas_call(
        kernel,
        out_shape=out_shape,
        grid_spec=pltpu.PrefetchScalarGridSpec(
            num_scalar_prefetch=1,
            grid=(count,),
            in_specs=in_specs,
            out_specs=[whole(*o.shape) for o in out_shape],
            scratch_shapes=scratch,
        ),
        compiler_params=params(40),
        cost_estimate=cost(4 * half * hidden * width, 2 * hidden * width + 16 * half * width),
        name="backward_y" if y_first else "backward_z",
    )(*args)


def local_call(kernel, idx, args, out_shape, name, specs=None, mib=16):
    whole = lambda shape: pl.BlockSpec(shape, lambda i, s: (0,) * len(shape))
    specs = specs or [whole(a.shape) for a in args]
    nbytes = sum(a.size * a.dtype.itemsize for a in args) + sum(
        o.size * o.dtype.itemsize for o in out_shape
    )
    return pl.pallas_call(
        kernel,
        out_shape=out_shape,
        grid_spec=pltpu.PrefetchScalarGridSpec(
            num_scalar_prefetch=1,
            grid=(1,),
            in_specs=specs,
            out_specs=[whole(o.shape) for o in out_shape],
        ),
        compiler_params=params(mib),
        cost_estimate=cost(0, nbytes),
        name=name,
    )(idx, *args)


def after_y(idx, keep, got):
    count, nz, rows, tile = keep.shape

    def kernel(idx, keep, got, total, up, down):
        z = idx[0]

        @pl.loop(0, nz * rows // BLK)
        def _(b):
            zz = b // (rows // BLK)
            off = pl.ds(pl.multiple_of((b % (rows // BLK)) * BLK, BLK), BLK)
            plus = decode_rows(got, pl.ds(pl.multiple_of(b * BLK, BLK), BLK), tile, count)
            for t in range(count):
                total[t, zz, off, :] = keep[t, zz, off, :] + plus[t]

        for msg, far in ((up, z + nz - 1), (down, z - nz + 1)):
            zz = jnp.clip(far, 0, nz - 1)

            @pl.loop(0, rows // BLK)
            def _(b):
                at = pl.ds(pl.multiple_of(b * BLK, BLK), BLK)
                encode_rows([total[t, zz, at, :] for t in range(count)], msg, at)

    msg = jax.ShapeDtypeStruct((rows, count * tile + LANES), jnp.bfloat16)
    out = [jax.ShapeDtypeStruct(keep.shape, jnp.float32), msg, msg]
    return local_call(kernel, idx, [keep, got], out, "after_y", mib=24)


def line_step(idx, total, up_got, down_got, reach):
    count, nz, rows, tile = total.shape

    def kernel(idx, up_total, down_total, up_got, down_got, up, down):
        for part, got, msg in ((up_total, up_got, up), (down_total, down_got, down)):

            @pl.loop(0, rows // BLK)
            def _(b):
                at = pl.ds(pl.multiple_of(b * BLK, BLK), BLK)
                plus = decode_rows(got, at, tile, count)
                encode_rows([part[t, 0, at, :] + plus[t] for t in range(count)], msg, at)

    def far(step):
        return pl.BlockSpec(
            (count, 1, rows, tile), lambda i, s: (0, jnp.clip(s[0] + step, 0, nz - 1), 0, 0)
        )

    full = pl.BlockSpec(up_got.shape, lambda i, s: (0, 0))
    msg = jax.ShapeDtypeStruct(up_got.shape, jnp.bfloat16)
    return local_call(
        kernel,
        idx,
        [total, total, up_got, down_got],
        [msg, msg],
        "line_step",
        specs=[far(reach), far(-reach), full, full],
    )


def line_end(idx, total, up_got, down_got, split):
    count, nz, rows, tile = total.shape
    width = count * tile
    mine = rows // 2 if split else rows

    def kernel(idx, part, up_got, down_got, *outs):
        y = idx[1]

        def summed(at):
            a = decode_rows(up_got, at, tile, count)
            b = decode_rows(down_got, at, tile, count)
            return [part[t, 0, at, :] + a[t] + b[t] for t in range(count)]

        @pl.loop(0, mine // BLK)
        def _(b):
            at = pl.ds(pl.multiple_of(b * BLK, BLK), BLK)
            if split:
                msg, keep = outs
                away = pl.ds(pl.multiple_of((1 - y) * mine + b * BLK, BLK), BLK)
                here = pl.ds(pl.multiple_of(y * mine + b * BLK, BLK), BLK)
                encode_rows(summed(away), msg, at)
                for t, v in enumerate(summed(here)):
                    keep[at, t * tile : (t + 1) * tile] = v
            else:
                for t, v in enumerate(summed(at)):
                    outs[0][at, t * tile : (t + 1) * tile] = v.astype(jnp.bfloat16)

    if split:
        out = [
            jax.ShapeDtypeStruct((mine, width + LANES), jnp.bfloat16),
            jax.ShapeDtypeStruct((mine, width), jnp.float32),
        ]
    else:
        out = [jax.ShapeDtypeStruct((mine, width), jnp.bfloat16)]
    own = pl.BlockSpec((count, 1, rows, tile), lambda i, s: (0, s[0], 0, 0))
    full = pl.BlockSpec(up_got.shape, lambda i, s: (0, 0))
    return local_call(
        kernel, idx, [total, up_got, down_got], out, "line_end", specs=[own, full, full]
    )


def finish_grad(idx, done, keep, got):
    rows, first = done.shape
    width = keep.shape[1]
    tile = pick(width, F_TILE)

    def kernel(idx, done, keep, got, out):
        out[:, :first] = done[...]

        @pl.loop(0, rows // BLK)
        def _(b):
            at = pl.ds(pl.multiple_of(b * BLK, BLK), BLK)
            for t, v in enumerate(decode_rows(got, at, tile, width // tile)):
                lo = t * tile
                out[at, first + lo : first + lo + tile] = (
                    keep[at, lo : lo + tile] + v
                ).astype(jnp.bfloat16)

    out = [jax.ShapeDtypeStruct((rows, first + width), jnp.bfloat16)]
    return local_call(kernel, idx, [done, keep, got], out, "finish_grad")[0]


def forward(idx, blocks, w, sketch):
    feats, hidden = w.shape
    part = [b.shape[0] // 2 for b in blocks]
    send_rows = sum(part)
    tile = pick(hidden, H_TILE)
    width = sketch.shape[0]

    def kernel(idx, *refs):
        k = 2 * len(blocks)
        xs = refs[:k]
        w, sk, send, keep, left, x = refs[k:]

        @pl.when(pl.program_id(0) == 0)
        def _():
            row = 0
            for ref in xs:
                x[row : row + ref.shape[0], :] = ref[...]
                row += ref.shape[0]
            left[...] = contract_last(x[...], sk[...])

        t = jnp.dot(x[...], w[...], preferred_element_type=jnp.float32)
        send[...] = t[:send_rows]
        keep[...] = t[send_rows:]

    once = pl.Buffered(1)
    specs = [
        pl.BlockSpec((r, feats), lambda j, s: (1 - s[2], 0), pipeline_mode=once) for r in part
    ] + [pl.BlockSpec((r, feats), lambda j, s: (s[2], 0), pipeline_mode=once) for r in part]
    specs += [
        pl.BlockSpec((feats, tile), lambda j, s: (0, j)),
        pl.BlockSpec((width, feats), lambda j, s: (0, 0), pipeline_mode=once),
    ]
    out = jax.ShapeDtypeStruct((send_rows, hidden), jnp.float32)
    column = pl.BlockSpec((send_rows, tile), lambda j, s: (0, j))
    return pl.pallas_call(
        kernel,
        out_shape=[out, out, jax.ShapeDtypeStruct((2 * send_rows, width), jnp.float32)],
        grid_spec=pltpu.PrefetchScalarGridSpec(
            num_scalar_prefetch=1,
            grid=(hidden // tile,),
            in_specs=specs,
            out_specs=[
                column,
                column,
                pl.BlockSpec((2 * send_rows, width), lambda j, s: (0, 0)),
            ],
            scratch_shapes=[pltpu.VMEM((2 * send_rows, feats), jnp.bfloat16)],
        ),
        compiler_params=params(32),
        cost_estimate=cost(
            4 * send_rows * feats * hidden, 2 * feats * hidden + 8 * send_rows * hidden
        ),
        name="forward",
    )(idx, *blocks, *blocks, w, sketch)


def places(rows, a_rows, nz):
    out = []
    zh, b_rows = nz // 2, rows - a_rows
    if a_rows:
        for same in (True, False):
            for zz in range(zh):
                out.append((0, ((0 if same else zh) + zz) * a_rows, zz, same, 0, a_rows))
    last = 1 if a_rows else 0
    for zz in range(zh):
        for same in (True, False):
            at = (2 * zz + (0 if same else 1)) * b_rows
            out.append((last, at, zz, same, a_rows, b_rows))
    return out


def combine(idx, pairs, rows, a_rows, nz):
    hidden = pairs[0][0].shape[1]
    tile = pick(hidden, H_TILE)
    half = nz * rows

    def kernel(idx, *refs):
        out = refs[-1]
        y = idx[1]
        for piece, at, zz, same, off, count in places(rows, a_rows, nz):
            yy = y if same else 1 - y
            keep, got = refs[2 * piece], refs[2 * piece + 1]
            to = pl.ds(pl.multiple_of(zz * 2 * rows + yy * rows + off, BLK), count)
            out[to, :] = (keep[at : at + count, :] + got[at : at + count, :]).astype(jnp.bfloat16)

    flat = [a for pair in pairs for a in pair]
    return pl.pallas_call(
        kernel,
        out_shape=jax.ShapeDtypeStruct((half, hidden), jnp.bfloat16),
        grid_spec=pltpu.PrefetchScalarGridSpec(
            num_scalar_prefetch=1,
            grid=(hidden // tile,),
            in_specs=[pl.BlockSpec((a.shape[0], tile), lambda j, s: (0, j)) for a in flat],
            out_specs=pl.BlockSpec((half, tile), lambda j, s: (0, j)),
        ),
        compiler_params=params(16),
        cost_estimate=cost(0, 10 * half * hidden),
        name="combine",
    )(idx, *flat)


def sketch_part(idx, lefts, right, rows, a_rows, nz):
    width = right.shape[1]
    tokens = right.shape[0]
    half = tokens // 2
    examples = tokens // LEN

    def kernel(idx, *refs):
        right, out, left = refs[-3:]
        y, core = idx[1], idx[2]
        for side in (0, 1):
            base = (1 - core if side == 0 else core) * half
            for piece, at, zz, same, off, count in places(rows, a_rows, nz):
                yy = y if same else 1 - y
                to = pl.ds(pl.multiple_of(base + zz * 2 * rows + yy * rows + off, 8), count)
                src = refs[piece]
                lo = side * (src.shape[0] // 2) + at
                left[to, :] = src[lo : lo + count, :]
        for e in range(examples):
            span = slice(e * LEN, (e + 1) * LEN)
            out[e] = lax.dot_general(
                left[span, :],
                right[span, :],
                (((0,), (0,)), ((), ())),
                precision=lax.Precision.HIGHEST,
                preferred_element_type=jnp.float32,
            )

    args = list(lefts) + [right]
    whole = lambda shape: pl.BlockSpec(shape, lambda i, s: (0,) * len(shape))
    return pl.pallas_call(
        kernel,
        out_shape=jax.ShapeDtypeStruct((examples, width, width), jnp.float32),
        grid_spec=pltpu.PrefetchScalarGridSpec(
            num_scalar_prefetch=1,
            grid=(1,),
            in_specs=[whole(a.shape) for a in args],
            out_specs=whole((examples, width, width)),
            scratch_shapes=[pltpu.VMEM((tokens, width), jnp.float32)],
        ),
        compiler_params=params(16),
        name="sketch_part",
    )(idx, *args)


def body(inputs, cotangent, weight, in_sketch, out_sketch):
    n = lax.axis_size("outp")
    nz = n // 2
    rows, feats = inputs.shape
    me = lax.axis_index("outp")
    idx = jnp.stack([me // 2, me % 2, lax.axis_index("inp")]).astype(jnp.int32)
    swap = [(0, 1), (1, 0)]
    across = [(d, d ^ 1) for d in range(n)]
    lines = [[2 * z + y for z in range(nz)] for y in range(2)]

    def up(reach):
        return [(2 * z + y, 2 * z + 2 + y) for z in range(nz - reach) for y in range(2)]

    def down(reach):
        return [(2 * z + y, 2 * z - 2 + y) for z in range(reach, nz) for y in range(2)]

    def along_z(x):
        return lax.all_gather(x, "outp", axis=0, tiled=True, axis_index_groups=lines)

    a_rows = rows // 2 if (rows // 2) % BLK == 0 else 0
    rest = inputs[a_rows:]
    rest = jnp.concatenate([rest, lax.ppermute(rest, "outp", across)], axis=0)
    grad_other = lax.ppermute(cotangent, "inp", swap)
    groups = []
    if a_rows:
        near = along_z(inputs[:a_rows])
        groups.append([near, lax.ppermute(near, "outp", across)])
    groups.append([along_z(rest)])

    tile = pick(min(Y_FIRST, feats - Y_FIRST), F_TILE)
    c1, c2 = Y_FIRST // tile, (feats - Y_FIRST) // tile
    back = functools.partial(
        backward, idx, cotangent, grad_other, weight, tile=tile, rows=rows, nz=nz
    )
    msg, keep, right = back(count=c1, first=0, sketch=out_sketch, y_first=True)
    got1 = lax.ppermute(msg, "outp", across)
    total2, u2, d2 = back(count=c2, first=c1, sketch=None, y_first=False)
    total2 = total2.reshape(c2, nz, 2 * rows, tile)

    k = 1
    while k < n:
        right = right + lax.ppermute(right, "outp", [(d, d ^ k) for d in range(n)])
        k *= 2

    total1 = None
    for reach in range(nz - 1, 0, -1):
        u2 = lax.ppermute(u2, "outp", up(reach))
        d2 = lax.ppermute(d2, "outp", down(reach))
        if total1 is None:
            total1, u1, d1 = after_y(idx, keep, got1)
        u1 = lax.ppermute(u1, "outp", up(reach))
        d1 = lax.ppermute(d1, "outp", down(reach))
        if reach > 1:
            u2, d2 = line_step(idx, total2, u2, d2, reach - 1)
            u1, d1 = line_step(idx, total1, u1, d1, reach - 1)
    msg2, keep2 = line_end(idx, total2, u2, d2, True)
    got2 = lax.ppermute(msg2, "outp", across)
    (done1,) = line_end(idx, total1, u1, d1, False)
    input_grad = finish_grad(idx, done1, keep2, got2)

    pairs, lefts = [], []
    for blocks in groups:
        send, own, left = forward(idx, blocks, weight, in_sketch)
        pairs.append((own, lax.ppermute(send, "inp", swap)))
        lefts.append(left)
    outputs = combine(idx, pairs, rows, a_rows, nz)
    width = in_sketch.shape[0]
    part = sketch_part(idx, lefts, right.reshape(n * rows, width), rows, a_rows, nz)
    part = (part + lax.ppermute(part, "inp", swap)) * (1.0 / LEN**0.5)
    sketches = part.reshape(n * rows // LEN, width * width)
    return (outputs, input_grad, sketches)


def solution(mesh):
    placed = (
        P(("groups", "outp"), "inp"),
        P(("groups", "inp"), "outp"),
        P("inp", "outp"),
        P(None, "inp"),
        P(None, "outp"),
    )
    return jax.shard_map(
        body,
        mesh=mesh,
        in_specs=placed,
        out_specs=(P(("groups", "inp"), "outp"), P(("groups", "outp"), "inp"), P("groups", None)),
        check_vma=False,
    )
```

```python
import jax
import jax.numpy as jnp
from jax import lax
from jax.experimental import pallas as pl
from jax.experimental.pallas import tpu as pltpu
from jax.sharding import PartitionSpec as P

LEN = 128
LANES = 128
BLK = 16
LN2 = 0.6931471805599453
SPAN = 248.0
SHIFT = 124.0
PIECES = 2
F_TILE = 512
H_TILE = 512
FWD_PIECES = 4
MIB = 1 << 20
ANY = pl.BlockSpec(memory_space=pl.ANY)


def pick(extent, cap):
    best = LANES
    for t in range(LANES, min(cap, extent) + 1, LANES):
        if extent % t == 0:
            best = t
    return best


def contract_last(a, b):
    return lax.dot_general(a, b, (((1,), (1,)), ((), ())), preferred_element_type=jnp.float32)


def whole(shape):
    return pl.BlockSpec(shape, lambda *_: (0,) * len(shape))


def call(kernel, idx, args, specs, out_shape, out_specs, name, grid, mib, work, after, scratch=()):
    token = jax.ShapeDtypeStruct((8, LANES), jnp.float32)
    n_args, n_after, n_out = len(args), len(after), len(out_shape)

    def with_token(idx, *refs):
        ins = refs[:n_args]
        outs = refs[n_args + n_after :]
        outs[n_out][...] = jnp.zeros((8, LANES), jnp.float32)
        kernel(idx, *ins, *outs[:n_out], *outs[n_out + 1 :])

    out = pl.pallas_call(
        with_token,
        out_shape=list(out_shape) + [token],
        grid_spec=pltpu.PrefetchScalarGridSpec(
            num_scalar_prefetch=1,
            grid=grid,
            in_specs=list(specs) + [ANY] * n_after,
            out_specs=list(out_specs) + [whole(token.shape)],
            scratch_shapes=list(scratch),
        ),
        compiler_params=pltpu.CompilerParams(vmem_limit_bytes=mib * MIB),
        cost_estimate=pl.CostEstimate(
            flops=work[0], bytes_accessed=work[1], transcendentals=0
        ),
        name=name,
    )(idx, *args, *after)
    return out[:-1], out[-1]


def encode_rows(tiles, msg, at):
    top = jnp.abs(tiles[0])
    for v in tiles[1:]:
        top = jnp.maximum(top, jnp.abs(v))
    top = jnp.max(top, axis=1, keepdims=True)
    scale = jnp.maximum(top * 1.004, 2.0**-110).astype(jnp.bfloat16).astype(jnp.float32)
    gain = SPAN / scale
    col = 0
    for v in tiles:
        w = jnp.exp2(jnp.abs(v) * gain - SHIFT)
        msg[at, col : col + v.shape[1]] = jnp.where(v < 0, -w, w).astype(jnp.bfloat16)
        col += v.shape[1]
    msg[at, col : col + LANES] = jnp.broadcast_to(scale, (BLK, LANES)).astype(jnp.bfloat16)


def decode_rows(msg, at, tile, count):
    scale = msg[at, tile * count : tile * count + LANES].astype(jnp.float32)[:, :1]
    scale = scale * (1.0 / (SPAN * LN2))
    out = []
    for t in range(count):
        w = msg[at, t * tile : (t + 1) * tile].astype(jnp.float32)
        a = (lax.log(jnp.maximum(jnp.abs(w), 2.0**-SHIFT)) + SHIFT * LN2) * scale
        out.append(jnp.where(w < 0, -a, a))
    return out


def with_bit(c, pos, value):
    low = c & ((1 << pos) - 1)
    return ((c >> pos) << (pos + 1)) + low + value * (1 << pos)


def rows_at(start):
    return pl.ds(pl.multiple_of(start, BLK), BLK)


def backward(idx, own, oth, w, sketch, count, tile, first, rows, bit, after):
    half, hidden = own.shape
    n = 2 * half // rows
    width = count * tile
    with_right = sketch is not None

    def kernel(idx, own, oth, w, *rest):
        if with_right:
            sk, msg, keep, right, x, total, sems = rest
        else:
            msg, keep, x, total, sems = rest
        j = pl.program_id(0)
        me, core = idx[0], idx[1]

        @pl.when(j == 0)
        def _():
            a = pltpu.make_async_copy(own, x.at[core], sems.at[0])
            b = pltpu.make_async_copy(oth, x.at[1 - core], sems.at[1])
            a.start()
            b.start()
            a.wait()
            b.wait()

        xs = x[...].reshape(2 * half, hidden)
        if with_right:

            @pl.when(j == 0)
            def _():
                right[...] = contract_last(xs, sk[...])

        total[j] = contract_last(xs, w[...]).reshape(n, rows, tile)

        @pl.when(j == count - 1)
        def _():
            mine = (me >> bit) & 1
            for c in range(n // 2):
                away, here = with_bit(c, bit, 1 - mine), with_bit(c, bit, mine)

                @pl.loop(0, rows // BLK)
                def _(b):
                    src = rows_at(b * BLK)
                    encode_rows(
                        [total[t, away, src, :] for t in range(count)],
                        msg,
                        rows_at(c * rows + b * BLK),
                    )
                    for t in range(count):
                        keep[t, c, src, :] = total[t, here, src, :]

    args = [own, oth, w]
    specs = [ANY, ANY, pl.BlockSpec((tile, hidden), lambda j, s: (first + j, 0))]
    out = [
        jax.ShapeDtypeStruct((n // 2 * rows, width + LANES), jnp.bfloat16),
        jax.ShapeDtypeStruct((count, n // 2, rows, tile), jnp.float32),
    ]
    if with_right:
        args.append(sketch)
        specs.append(whole(sketch.shape))
        out.append(jax.ShapeDtypeStruct((2 * half, sketch.shape[0]), jnp.float32))
    return call(
        kernel,
        idx,
        args,
        specs,
        out,
        [whole(o.shape) for o in out],
        "backward",
        (count,),
        40,
        (4 * half * hidden * width, 2 * hidden * width + 12 * half * width),
        after,
        [
            pltpu.VMEM((2, half, hidden), jnp.bfloat16),
            pltpu.VMEM((count, n, rows, tile), jnp.float32),
            pltpu.SemaphoreType.DMA((2,)),
        ],
    )


def fold(idx, keep, got, bit, pos, after):
    count, m, rows, tile = keep.shape

    def kernel(idx, keep, got, msg, rest):
        mine = (idx[0] >> bit) & 1
        for c in range(m // 2):
            away, here = with_bit(c, pos, 1 - mine), with_bit(c, pos, mine)

            @pl.loop(0, rows // BLK)
            def _(b):
                src = rows_at(b * BLK)
                plus = decode_rows(got, rows_at(away * rows + b * BLK), tile, count)
                encode_rows(
                    [keep[t, away, src, :] + plus[t] for t in range(count)],
                    msg,
                    rows_at(c * rows + b * BLK),
                )
                plus = decode_rows(got, rows_at(here * rows + b * BLK), tile, count)
                for t in range(count):
                    rest[t, c, src, :] = keep[t, here, src, :] + plus[t]

    out = [
        jax.ShapeDtypeStruct((m // 2 * rows, got.shape[1]), jnp.bfloat16),
        jax.ShapeDtypeStruct((count, m // 2, rows, tile), jnp.float32),
    ]
    return call(
        kernel,
        idx,
        [keep, got],
        [whole(keep.shape), whole(got.shape)],
        out,
        [whole(o.shape) for o in out],
        "fold",
        (1,),
        24,
        (0, 12 * keep.size),
        after,
    )


def finish(idx, keeps, gots, after):
    count, _, rows, tile = keeps[0].shape
    pieces = len(keeps)

    def kernel(idx, *refs):
        out = refs[-1]
        for p in range(pieces):

            @pl.loop(0, rows // BLK)
            def _(b):
                at = rows_at(b * BLK)
                plus = decode_rows(refs[pieces + p], at, tile, count)
                for t in range(count):
                    lo = (p * count + t) * tile
                    out[at, lo : lo + tile] = (refs[p][t, 0, at, :] + plus[t]).astype(
                        jnp.bfloat16
                    )

    args = list(keeps) + list(gots)
    out = [jax.ShapeDtypeStruct((rows, pieces * count * tile), jnp.bfloat16)]
    (grad,), _ = call(
        kernel,
        idx,
        args,
        [whole(a.shape) for a in args],
        out,
        [whole(out[0].shape)],
        "finish",
        (1,),
        16,
        (0, 16 * rows * count * tile),
        after,
    )
    return grad


def bit_reversed(r, bits):
    return sum(((r >> k) & 1) << (bits - 1 - k) for k in range(bits))


def join(idx, a, b, after):
    m = a.shape[0]

    def kernel(idx, a, b, out, sems):
        first = pltpu.make_async_copy(a, out.at[pl.ds(0, m)], sems.at[0])
        second = pltpu.make_async_copy(b, out.at[pl.ds(m, m)], sems.at[1])
        first.start()
        second.start()
        first.wait()
        second.wait()

    out = [jax.ShapeDtypeStruct((2 * m,) + a.shape[1:], a.dtype)]
    work = (0, 8 * a.size)
    dma = [pltpu.SemaphoreType.DMA((2,))]
    (joined,), token = call(
        kernel, idx, [a, b], [ANY, ANY], out, [ANY], "join", (1,), 8, work, after, dma
    )
    return joined, token


def add(idx, a, b, after):
    def kernel(idx, a, b, out):
        out[...] = a[...] + b[...]

    specs = [whole(a.shape)] * 2
    out = [jax.ShapeDtypeStruct(a.shape, a.dtype)]
    work = (a.size, 12 * a.size)
    (total,), token = call(
        kernel, idx, [a, b], specs, out, specs[:1], "add", (1,), 8, work, after
    )
    return total, token


def forward(idx, near, far, w, sketch, rows, first, count, tile, after):
    m, b_rows, feats = far[0].shape
    n = 2 * m
    a_rows = rows - b_rows
    half = n // 2 * rows
    bits = n.bit_length() - 1
    with_left = sketch is not None
    args = ([near] if a_rows else []) + [*far, w] + ([sketch] if with_left else [])
    specs = [ANY] * (3 if a_rows else 2) + [
        pl.BlockSpec((feats, tile), lambda j, s: (0, first + j))
    ]
    if with_left:
        specs.append(whole(sketch.shape))

    def kernel(idx, *refs):
        x, sems = refs[-2:]
        send, keep = refs[len(args) : len(args) + 2]
        *far, w = refs[1:4] if a_rows else refs[:3]
        me, core = idx[0], idx[1]

        def place(d):
            side = 1 - ((d // (n // 2)) ^ core)
            return side * half + (d % (n // 2)) * rows

        @pl.when(pl.program_id(0) == 0)
        def _():
            copies = []
            for r in range(n):
                to = pl.ds(pl.multiple_of(place(me ^ bit_reversed(r, bits)) + a_rows, BLK), b_rows)
                copies.append(pltpu.make_async_copy(far[r // m].at[r % m], x.at[to], sems.at[r]))
                if a_rows:
                    to = pl.ds(pl.multiple_of(place(jnp.int32(r)), BLK), a_rows)
                    copies.append(
                        pltpu.make_async_copy(
                            refs[0].at[pl.ds(r * a_rows, a_rows)], x.at[to], sems.at[n + r]
                        )
                    )
            for c in copies:
                c.start()
            for c in copies:
                c.wait()
            if with_left:
                refs[len(args) + 2][...] = contract_last(x[...], refs[len(args) - 1][...])

        t = jnp.dot(x[...], w[...], preferred_element_type=jnp.float32)
        send[...] = t[:half]
        keep[...] = t[half:]

    width = count * tile
    out = [jax.ShapeDtypeStruct((half, width), jnp.float32)] * 2
    out_specs = [pl.BlockSpec((half, tile), lambda j, s: (0, j))] * 2
    if with_left:
        out.append(jax.ShapeDtypeStruct((2 * half, sketch.shape[0]), jnp.float32))
        out_specs.append(whole(out[-1].shape))
    return call(
        kernel,
        idx,
        args,
        specs,
        out,
        out_specs,
        "forward",
        (count,),
        40,
        (4 * half * feats * width, 2 * feats * width + 8 * half * width),
        after,
        [pltpu.VMEM((2 * half, feats), jnp.bfloat16), pltpu.SemaphoreType.DMA((2 * n,))],
    )


def sketch_part(idx, left, right, after):
    tokens, width = right.shape
    half = tokens // 2
    examples = tokens // LEN

    def kernel(idx, left, right, out):
        core = idx[1]
        for e in range(examples):
            side = 1 - ((2 * e // examples) ^ core)
            at = pl.multiple_of(side * half + (e % (examples // 2)) * LEN, LEN)
            out[e] = lax.dot_general(
                left[pl.ds(at, LEN), :],
                right[e * LEN : (e + 1) * LEN, :],
                (((0,), (0,)), ((), ())),
                precision=lax.Precision.HIGHEST,
                preferred_element_type=jnp.float32,
            )

    out = [jax.ShapeDtypeStruct((examples, width, width), jnp.float32)]
    (part,), token = call(
        kernel,
        idx,
        [left, right],
        [whole(left.shape), whole(right.shape)],
        out,
        [whole(out[0].shape)],
        "sketch_part",
        (1,),
        16,
        (0, 8 * tokens * width),
        after,
    )
    return part, token


def body(inputs, cotangent, weight, in_sketch, out_sketch):
    n = lax.axis_size("outp")
    bits = n.bit_length() - 1
    rows, feats = inputs.shape
    hidden = weight.shape[1]
    idx = jnp.stack([lax.axis_index("outp"), lax.axis_index("inp")]).astype(jnp.int32)

    def partner(x, bit):
        return lax.ppermute(x, "outp", [(d, d ^ (1 << bit)) for d in range(n)])

    def swap(x):
        return lax.ppermute(x, "inp", [(0, 1), (1, 0)])

    a_rows = rows // 2 if (rows // 2) % BLK == 0 else 0
    near = None
    if a_rows:
        near = lax.all_gather(inputs[:a_rows], "outp", axis=0, tiled=True)
    far = inputs[a_rows:][None]
    grad_other = swap(cotangent)

    orders = [list(range(bits)), [1, 0] + list(range(2, bits))]
    tile = pick(feats // PIECES, F_TILE)
    count = feats // PIECES // tile
    msgs, keeps = [], []
    token = []
    far_bits = list(reversed(range(bits)))
    got = partner(far, far_bits.pop(0))
    for p in range(PIECES):
        outs, t = backward(
            idx,
            cotangent,
            grad_other,
            weight,
            out_sketch if p == 0 else None,
            count,
            tile,
            p * count,
            rows,
            orders[p][0],
            token,
        )
        token = [t]
        if p == 0:
            right = outs[2]
            right_got = partner(right, 0)
        msgs.append(partner(outs[0], orders[p][0]))
        keeps.append(outs[1])
        if far_bits:
            far, t = join(idx, far, got, token)
            token = [t]
            got = partner(far, far_bits.pop(0))
    while far_bits:
        far, t = join(idx, far, got, token)
        token = [t]
        got = partner(far, far_bits.pop(0))
    right_bits = list(range(1, bits))

    def right_step(after):
        total, t = add(idx, right, right_got, after)
        if right_bits:
            return total, partner(total, right_bits.pop(0)), [t]
        return total, None, [t]

    def folded(p, step, after):
        done, bit = orders[p][:step], orders[p][step]
        pos = sum(1 for k in range(bit) if k not in done)
        (msg, keeps[p]), t = fold(idx, keeps[p], msgs[p], bit, pos, after)
        msgs[p] = partner(msg, bit)
        return [t]

    h_tile = pick(hidden, H_TILE)
    tiles = hidden // h_tile
    ends = [-(-tiles * k // FWD_PIECES) for k in range(FWD_PIECES + 1)]
    folds = [(p, step) for step in range(1, bits) for p in range(PIECES)]
    columns = []
    right, right_got, token = right_step(token)
    token = folded(*folds.pop(0), token)
    for k in range(FWD_PIECES):
        if right_got is not None:
            right, right_got, token = right_step(token)
        outs, t = forward(
            idx,
            near,
            [far, got],
            weight,
            in_sketch if k == 0 else None,
            rows,
            ends[k],
            ends[k + 1] - ends[k],
            h_tile,
            token,
        )
        token = [t]
        if k == 0:
            left = outs[2]
        columns.append(outs[1] + swap(outs[0]))
        if folds:
            token = folded(*folds.pop(0), token)
    while right_got is not None:
        right, right_got, token = right_step(token)
    for p, step in folds:
        token = folded(p, step, token)
    part, t = sketch_part(idx, left, right, token)
    part = (part + swap(part)) * (1.0 / LEN**0.5)
    sketches = part.reshape(part.shape[0], -1)
    input_grad = finish(idx, keeps, msgs, [t])
    outputs = jnp.concatenate([c.astype(jnp.bfloat16) for c in columns], axis=1)
    return (outputs, input_grad, sketches)


def solution(mesh):
    placed = (
        P(("groups", "outp"), "inp"),
        P(("groups", "inp"), "outp"),
        P("inp", "outp"),
        P(None, "inp"),
        P(None, "outp"),
    )
    return jax.shard_map(
        body,
        mesh=mesh,
        in_specs=placed,
        out_specs=(P(("groups", "inp"), "outp"), P(("groups", "outp"), "inp"), P("groups", None)),
        check_vma=False,
    )
```

```python
import jax
import jax.numpy as jnp
from jax import lax
from jax.experimental import pallas as pl
from jax.experimental.pallas import tpu as pltpu
from jax.sharding import PartitionSpec as P

LEN = 128
LANES = 128
BLK = 16
LN2 = 0.6931471805599453
SPAN = 248.0
SHIFT = 124.0
PIECES = 2
F_TILE = 512
H_TILE = 512
VMEM_MIB = {"backward": 32, "forward": 24}
MIB = 1 << 20
TIMES = {"fold": 0, "combine": 1 << 25, "sketch_part": 1 << 25}
ANY = pl.BlockSpec(memory_space=pl.ANY)


def pick(extent, cap):
    best = LANES
    for t in range(LANES, min(cap, extent) + 1, LANES):
        if extent % t == 0:
            best = t
    return best


def contract_last(a, b):
    return lax.dot_general(a, b, (((1,), (1,)), ((), ())), preferred_element_type=jnp.float32)


def whole(shape):
    return pl.BlockSpec(shape, lambda *_: (0,) * len(shape))


def call(
    kernel, idx, args, specs, out_shape, out_specs, name, grid, work, after, scratch=(), aliases=None
):
    token = jax.ShapeDtypeStruct((8, LANES), jnp.float32)
    n_args, n_after, n_out = len(args), len(after), len(out_shape)

    def with_token(idx, *refs):
        ins = refs[:n_args]
        outs = refs[n_args + n_after :]
        outs[n_out][...] = jnp.zeros((8, LANES), jnp.float32)
        kernel(idx, *ins, *outs[:n_out], *outs[n_out + 1 :])

    out = pl.pallas_call(
        with_token,
        out_shape=list(out_shape) + [token],
        grid_spec=pltpu.PrefetchScalarGridSpec(
            num_scalar_prefetch=1,
            grid=grid,
            in_specs=list(specs) + [ANY] * n_after,
            out_specs=list(out_specs) + [whole(token.shape)],
            scratch_shapes=list(scratch),
        ),
        compiler_params=pltpu.CompilerParams(vmem_limit_bytes=VMEM_MIB.get(name, 12) * MIB),
        cost_estimate=pl.CostEstimate(
            flops=TIMES.get(name, work[0]), bytes_accessed=work[1], transcendentals=0
        ),
        input_output_aliases=aliases or {},
        name=name,
    )(idx, *args, *after)
    return out[:-1], out[-1]


def encode_rows(tiles, msg, at):
    top = jnp.abs(tiles[0])
    for v in tiles[1:]:
        top = jnp.maximum(top, jnp.abs(v))
    top = jnp.max(top, axis=1, keepdims=True)
    scale = jnp.maximum(top * 1.004, 2.0**-110).astype(jnp.bfloat16).astype(jnp.float32)
    gain = SPAN / scale
    col = 0
    for v in tiles:
        w = jnp.exp2(jnp.abs(v) * gain - SHIFT)
        msg[at, col : col + v.shape[1]] = jnp.where(v < 0, -w, w).astype(jnp.bfloat16)
        col += v.shape[1]
    msg[at, col : col + LANES] = jnp.broadcast_to(scale, (BLK, LANES)).astype(jnp.bfloat16)


def decode_rows(msg, at, tile, count):
    scale = msg[at, tile * count : tile * count + LANES].astype(jnp.float32)[:, :1]
    scale = scale * (1.0 / (SPAN * LN2))
    out = []
    for t in range(count):
        w = msg[at, t * tile : (t + 1) * tile].astype(jnp.float32)
        a = (lax.log(jnp.maximum(jnp.abs(w), 2.0**-SHIFT)) + SHIFT * LN2) * scale
        out.append(jnp.where(w < 0, -a, a))
    return out


def with_bit(c, pos, value):
    low = c & ((1 << pos) - 1)
    return ((c >> pos) << (pos + 1)) + low + value * (1 << pos)


def rows_at(start):
    return pl.ds(pl.multiple_of(start, BLK), BLK)


def backward(idx, own, oth, w, count, tile, first, rows, bit, after):
    half, hidden = own.shape
    n = 2 * half // rows
    width = count * tile

    def kernel(idx, own, oth, w, msg, keep, x, total, sems):
        j = pl.program_id(0)
        me, core = idx[0], idx[1]

        @pl.when(j == 0)
        def _():
            a = pltpu.make_async_copy(own, x.at[core], sems.at[0])
            b = pltpu.make_async_copy(oth, x.at[1 - core], sems.at[1])
            a.start()
            b.start()
            a.wait()
            b.wait()

        xs = x[...].reshape(2 * half, hidden)
        total[j] = contract_last(xs, w[...]).reshape(n, rows, tile)

        @pl.when(j == count - 1)
        def _():
            mine = (me >> bit) & 1
            for c in range(n // 2):
                away, here = with_bit(c, bit, 1 - mine), with_bit(c, bit, mine)

                @pl.loop(0, rows // BLK)
                def _(b):
                    src = rows_at(b * BLK)
                    encode_rows(
                        [total[t, away, src, :] for t in range(count)],
                        msg,
                        rows_at(c * rows + b * BLK),
                    )
                    for t in range(count):
                        keep[t, c, src, :] = total[t, here, src, :]

    out = [
        jax.ShapeDtypeStruct((n // 2 * rows, width + LANES), jnp.bfloat16),
        jax.ShapeDtypeStruct((count, n // 2, rows, tile), jnp.float32),
    ]
    return call(
        kernel,
        idx,
        [own, oth, w],
        [ANY, ANY, pl.BlockSpec((tile, hidden), lambda j, s: (first + j, 0))],
        out,
        [whole(o.shape) for o in out],
        "backward",
        (count,),
        (4 * half * hidden * width, 2 * hidden * width + 12 * half * width),
        after,
        [
            pltpu.VMEM((2, half, hidden), jnp.bfloat16),
            pltpu.VMEM((count, n, rows, tile), jnp.float32),
            pltpu.SemaphoreType.DMA((2,)),
        ],
    )


def right_part(idx, own, oth, sketch):
    half, hidden = own.shape
    width = sketch.shape[0]

    def kernel(idx, own, oth, sk, out):
        core = idx[1]
        out[core] = contract_last(own[...], sk[...])
        out[1 - core] = contract_last(oth[...], sk[...])

    args = [own, oth, sketch]
    out = [jax.ShapeDtypeStruct((2, half, width), jnp.float32)]
    specs = [whole(a.shape) for a in args]
    work = (4 * half * hidden * width, 4 * half * hidden)
    (part,), token = call(
        kernel, idx, args, specs, out, [whole(out[0].shape)], "right", (1,), work, []
    )
    return part.reshape(2 * half, width), token


def fold(idx, keep, got, bit, pos, after):
    count, m, rows, tile = keep.shape

    def kernel(idx, keep, got, msg, rest):
        mine = (idx[0] >> bit) & 1
        for c in range(m // 2):
            away, here = with_bit(c, pos, 1 - mine), with_bit(c, pos, mine)

            @pl.loop(0, rows // BLK)
            def _(b):
                src = rows_at(b * BLK)
                plus = decode_rows(got, rows_at(away * rows + b * BLK), tile, count)
                encode_rows(
                    [keep[t, away, src, :] + plus[t] for t in range(count)],
                    msg,
                    rows_at(c * rows + b * BLK),
                )
                plus = decode_rows(got, rows_at(here * rows + b * BLK), tile, count)
                for t in range(count):
                    rest[t, c, src, :] = keep[t, here, src, :] + plus[t]

    out = [
        jax.ShapeDtypeStruct((m // 2 * rows, got.shape[1]), jnp.bfloat16),
        jax.ShapeDtypeStruct((count, m // 2, rows, tile), jnp.float32),
    ]
    return call(
        kernel,
        idx,
        [keep, got],
        [whole(keep.shape), whole(got.shape)],
        out,
        [whole(o.shape) for o in out],
        "fold",
        (1,),
        (0, 12 * keep.size),
        after,
    )


def finish(idx, keeps, gots, after):
    count, _, rows, tile = keeps[0].shape
    pieces = len(keeps)

    def kernel(idx, *refs):
        out = refs[-1]
        for p in range(pieces):

            @pl.loop(0, rows // BLK)
            def _(b):
                at = rows_at(b * BLK)
                plus = decode_rows(refs[pieces + p], at, tile, count)
                for t in range(count):
                    lo = (p * count + t) * tile
                    out[at, lo : lo + tile] = (refs[p][t, 0, at, :] + plus[t]).astype(
                        jnp.bfloat16
                    )

    args = list(keeps) + list(gots)
    out = [jax.ShapeDtypeStruct((rows, pieces * count * tile), jnp.bfloat16)]
    (grad,), _ = call(
        kernel,
        idx,
        args,
        [whole(a.shape) for a in args],
        out,
        [whole(out[0].shape)],
        "finish",
        (1,),
        (0, 16 * rows * count * tile),
        after,
    )
    return grad


def gate(idx, arrays, after):
    k = len(arrays)

    def kernel(idx, *refs):
        pass

    out, token = call(
        kernel,
        idx,
        arrays,
        [ANY] * k,
        [jax.ShapeDtypeStruct(a.shape, a.dtype) for a in arrays],
        [ANY] * k,
        "gate",
        (1,),
        (0, 0),
        after,
        aliases={1 + i: i for i in range(k)},
    )
    return list(out), [token]


def add(idx, a, b, after):
    def kernel(idx, a, b, out):
        out[...] = a[...] + b[...]

    specs = [whole(a.shape)] * 2
    out = [jax.ShapeDtypeStruct(a.shape, a.dtype)]
    work = (a.size, 12 * a.size)
    (total,), token = call(kernel, idx, [a, b], specs, out, specs[:1], "add", (1,), work, after)
    return total, [token]


def forward(idx, chunks, w, sketch, lo, hi, after):
    rows, feats = chunks[0][1].shape
    m = len(chunks)
    tile = pick(w.shape[1], H_TILE)
    hidden = (hi - lo) * tile
    part = m // 2 * rows

    def kernel(idx, *refs):
        w, sk, send, keep, left, x, sems = refs[m:]
        me, core = idx[0], idx[1]

        @pl.when(pl.program_id(0) == 0)
        def _():
            copies = []
            for i, (mask, _) in enumerate(chunks):
                d = me ^ mask
                side = 1 - ((d // m) ^ core)
                to = pl.ds(pl.multiple_of(side * part + (d % (m // 2)) * rows, BLK), rows)
                copies.append(pltpu.make_async_copy(refs[i], x.at[to], sems.at[i]))
            for c in copies:
                c.start()
            for c in copies:
                c.wait()
            left[...] = contract_last(x[...], sk[...])

        t = jnp.dot(x[...], w[...], preferred_element_type=jnp.float32)
        send[...] = t[:part]
        keep[...] = t[part:]

    out = [jax.ShapeDtypeStruct((part, hidden), jnp.float32)] * 2
    out.append(jax.ShapeDtypeStruct((2 * part, sketch.shape[0]), jnp.float32))
    column = pl.BlockSpec((part, tile), lambda j, s: (0, j))
    return call(
        kernel,
        idx,
        [c[1] for c in chunks] + [w, sketch],
        [ANY] * m + [pl.BlockSpec((feats, tile), lambda j, s: (0, lo + j)), whole(sketch.shape)],
        out,
        [column, column, whole(out[2].shape)],
        "forward",
        (hidden // tile,),
        (4 * part * feats * hidden, 2 * feats * hidden + 8 * part * hidden),
        after,
        [pltpu.VMEM((2 * part, feats), jnp.bfloat16), pltpu.SemaphoreType.DMA((m,))],
    )


def combine(idx, keep, got, lo, total, batch, bit, before, after):
    part, hidden = keep.shape
    tile = pick(total, H_TILE)
    block = pl.BlockSpec((part, tile), lambda j, s: (0, j))

    def kernel(idx, keep, got, *refs):
        refs[-1][...] = (keep[...] + got[...]).astype(jnp.bfloat16)

    (out,), token = call(
        kernel,
        idx,
        [keep, got] + before,
        [block, block] + [ANY] * len(before),
        [jax.ShapeDtypeStruct((2 * part, total), jnp.bfloat16)],
        [pl.BlockSpec((part, tile), lambda j, s: (((s[0] >> bit) & 1) ^ batch, lo + j))],
        "combine",
        (hidden // tile,),
        (0, 10 * part * hidden),
        after,
        aliases={3: 0} if before else None,
    )
    return out, [token]


def sketch_part(idx, lefts, right, bit, after):
    tokens, width = right.shape
    part = tokens // 4
    examples = part // LEN

    def kernel(idx, first, second, right, out):
        me, core = idx[0], idx[1]
        for batch, left in enumerate((first, second)):
            block = ((me >> bit) & 1) ^ batch
            for side in (0, 1):
                owner = 1 - (side ^ core)
                for e in range(examples):
                    at = (2 * owner + block) * examples + e
                    lo = side * part + e * LEN
                    out[at] = lax.dot_general(
                        left[lo : lo + LEN, :],
                        right[pl.ds(pl.multiple_of(at * LEN, LEN), LEN), :],
                        (((0,), (0,)), ((), ())),
                        precision=lax.Precision.HIGHEST,
                        preferred_element_type=jnp.float32,
                    )

    args = [*lefts, right]
    out = [jax.ShapeDtypeStruct((tokens // LEN, width, width), jnp.float32)]
    (sketch,), token = call(
        kernel,
        idx,
        args,
        [whole(a.shape) for a in args],
        out,
        [whole(out[0].shape)],
        "sketch_part",
        (1,),
        (0, 8 * tokens * width),
        after,
    )
    return sketch, [token]


def body(inputs, cotangent, weight, in_sketch, out_sketch):
    n = lax.axis_size("outp")
    bits = n.bit_length() - 1
    rows, feats = inputs.shape
    hidden = weight.shape[1]
    idx = jnp.stack([lax.axis_index("outp"), lax.axis_index("inp")]).astype(jnp.int32)

    def partner(x, bit):
        return lax.ppermute(x, "outp", [(d, d ^ (1 << bit)) for d in range(n)])

    def swap(x):
        return lax.ppermute(x, "inp", [(0, 1), (1, 0)])

    chunks = {0: inputs}

    def last_bit(mask):
        if mask.bit_count() == 2 and mask & 2:
            return 1
        return (mask & -mask).bit_length() - 1

    def wave(size):
        for mask in sorted(range(n), reverse=True):
            if mask.bit_count() == size:
                bit = last_bit(mask)
                chunks[mask] = partner(chunks[mask ^ (1 << bit)], bit)

    def hold(size, after):
        masks = [m for m in chunks if m.bit_count() == size]
        held, token = gate(idx, [chunks[m] for m in masks], after)
        chunks.update(zip(masks, held))
        return token

    grad_other = swap(cotangent)
    wave(1)
    right, t = right_part(idx, cotangent, grad_other, out_sketch)
    token = [t]
    right_got = partner(right, 0)

    orders = [list(range(bits)), [1, 0] + list(range(2, bits))]
    tile = pick(feats // PIECES, F_TILE)
    count = feats // PIECES // tile
    msgs, keeps = [], []
    for p in range(PIECES):
        outs, t = backward(
            idx, cotangent, grad_other, weight, count, tile, p * count, rows, orders[p][0], token
        )
        right, token = add(idx, right, right_got, [t])
        right_got = partner(right, 1 + p)
        token = hold(1 + p, token)
        wave(2 + p)
        msgs.append(partner(outs[0], orders[p][0]))
        keeps.append(outs[1])
    for k in range(1 + PIECES, bits):
        right, token = add(idx, right, right_got, token)
        right_got = partner(right, k)
        token = hold(k, token)
        wave(k + 1)

    def folded(p, step, after):
        done, bit = orders[p][:step], orders[p][step]
        pos = sum(1 for k in range(bit) if k not in done)
        (msg, keeps[p]), t = fold(idx, keeps[p], msgs[p], bit, pos, after)
        msgs[p] = partner(msg, bit)
        return [t]

    tiles = hidden // pick(hidden, H_TILE)

    def batch_forward(batch, lo, hi, after):
        masks = [m for m in range(n) if (m >> (bits - 2)) & 1 == batch]
        parts = [(m, chunks[m]) for m in masks]
        outs, t = forward(idx, parts, weight, in_sketch, lo, hi, after)
        return (outs[1], swap(outs[0]), lo, hidden, batch, bits - 2), outs[2], [t]

    cut = -(-tiles // 2)
    first, left1, token = batch_forward(0, 0, tiles, token)
    token = folded(0, 1, token)
    token = folded(1, 1, token)
    right, token = add(idx, right, right_got, token)
    second, left2, token = batch_forward(1, 0, cut, token)
    token = folded(0, 2, token)
    third, _, token = batch_forward(1, cut, tiles, token)
    token = folded(1, 2, token)
    for step in range(3, bits):
        for p in range(PIECES):
            token = folded(p, step, token)
    outputs, token = combine(idx, *first, [], token)
    part, token = sketch_part(idx, [left1, left2], right, bits - 2, token)
    outputs, token = combine(idx, *second, [outputs], token)
    outputs, token = combine(idx, *third, [outputs], token)
    part = (part + swap(part)) * (1.0 / LEN**0.5)
    sketches = part.reshape(part.shape[0], -1)
    input_grad = finish(idx, keeps, msgs, token)
    return (outputs, input_grad, sketches)


def solution(mesh):
    placed = (
        P(("groups", "outp"), "inp"),
        P(("groups", "inp"), "outp"),
        P("inp", "outp"),
        P(None, "inp"),
        P(None, "outp"),
    )
    return jax.shard_map(
        body,
        mesh=mesh,
        in_specs=placed,
        out_specs=(P(("groups", "inp"), "outp"), P(("groups", "outp"), "inp"), P("groups", None)),
        check_vma=False,
    )
```

```python
import jax
import jax.numpy as jnp
from jax import lax
from jax.experimental import pallas as pl
from jax.experimental.pallas import tpu as pltpu
from jax.sharding import PartitionSpec as P

LEN = 128
LANES = 128
BLK = 16
LN2 = 0.6931471805599453
SPAN = 248.0
SHIFT = 124.0
PIECES = 2
F_TILE = 512
H_TILE = 512
VMEM_MIB = {"backward": 32, "forward": 24}
MIB = 1 << 20
TIMES = {"forward": 1 << 34, "fold": 0, "combine": 1 << 34, "sketch_part": 1 << 34}
ANY = pl.BlockSpec(memory_space=pl.ANY)
HBM = pl.BlockSpec(memory_space=pltpu.HBM)


def pick(extent, cap):
    best = LANES
    for t in range(LANES, min(cap, extent) + 1, LANES):
        if extent % t == 0:
            best = t
    return best


def contract_last(a, b):
    return lax.dot_general(a, b, (((1,), (1,)), ((), ())), preferred_element_type=jnp.float32)


def whole(shape):
    return pl.BlockSpec(shape, lambda *_: (0,) * len(shape))


def call(
    kernel, idx, args, specs, out_shape, out_specs, name, grid, work, after, scratch=(), aliases=None
):
    token = jax.ShapeDtypeStruct((8, LANES), jnp.float32)
    n_args, n_after, n_out = len(args), len(after), len(out_shape)

    def with_token(idx, *refs):
        ins = refs[:n_args]
        outs = refs[n_args + n_after :]
        outs[n_out][...] = jnp.zeros((8, LANES), jnp.float32)
        kernel(idx, *ins, *outs[:n_out], *outs[n_out + 1 :])

    out = pl.pallas_call(
        with_token,
        out_shape=list(out_shape) + [token],
        grid_spec=pltpu.PrefetchScalarGridSpec(
            num_scalar_prefetch=1,
            grid=grid,
            in_specs=list(specs) + [ANY] * n_after,
            out_specs=list(out_specs) + [whole(token.shape)],
            scratch_shapes=list(scratch),
        ),
        compiler_params=pltpu.CompilerParams(vmem_limit_bytes=VMEM_MIB.get(name, 14) * MIB),
        cost_estimate=pl.CostEstimate(
            flops=TIMES.get(name, work[0]), bytes_accessed=work[1], transcendentals=0
        ),
        input_output_aliases=aliases or {},
        name=name,
    )(idx, *args, *after)
    return out[:-1], out[-1]


def encode_rows(tiles, msg, at):
    top = jnp.abs(tiles[0])
    for v in tiles[1:]:
        top = jnp.maximum(top, jnp.abs(v))
    top = jnp.max(top, axis=1, keepdims=True)
    scale = jnp.maximum(top * 1.004, 2.0**-110).astype(jnp.bfloat16).astype(jnp.float32)
    gain = SPAN / scale
    col = 0
    for v in tiles:
        w = jnp.exp2(jnp.abs(v) * gain - SHIFT)
        msg[at, col : col + v.shape[1]] = jnp.where(v < 0, -w, w).astype(jnp.bfloat16)
        col += v.shape[1]
    msg[at, col : col + LANES] = jnp.broadcast_to(scale, (BLK, LANES)).astype(jnp.bfloat16)


def decode_rows(msg, at, tile, count):
    scale = msg[at, tile * count : tile * count + LANES].astype(jnp.float32)[:, :1]
    scale = scale * (1.0 / (SPAN * LN2))
    out = []
    for t in range(count):
        w = msg[at, t * tile : (t + 1) * tile].astype(jnp.float32)
        a = (lax.log(jnp.maximum(jnp.abs(w), 2.0**-SHIFT)) + SHIFT * LN2) * scale
        out.append(jnp.where(w < 0, -a, a))
    return out


def with_bit(c, pos, value):
    low = c & ((1 << pos) - 1)
    return ((c >> pos) << (pos + 1)) + low + value * (1 << pos)


def rows_at(start):
    return pl.ds(pl.multiple_of(start, BLK), BLK)


def backward(idx, own, oth, w, sketch, count, tile, first, rows, bit, after):
    half, hidden = own.shape
    n = 2 * half // rows
    width = count * tile

    def kernel(idx, own, oth, w, *rest):
        if sketch is None:
            msg, keep, x, total, sems = rest
        else:
            sk, msg, keep, right, x, total, sems, sk_here = rest
        j = pl.program_id(0)
        me, core = idx[0], idx[1]

        @pl.when(j == 0)
        def _():
            a = pltpu.make_async_copy(own, x.at[core], sems.at[0])
            b = pltpu.make_async_copy(oth, x.at[1 - core], sems.at[1])
            a.start()
            b.start()
            if sketch is not None:
                c = pltpu.make_async_copy(sk, sk_here, sems.at[2])
                c.start()
                c.wait()
            a.wait()
            b.wait()
            if sketch is not None:
                right[...] = contract_last(x[...].reshape(2 * half, hidden), sk_here[...])

        xs = x[...].reshape(2 * half, hidden)
        total[j] = contract_last(xs, w[...]).reshape(n, rows, tile)

        @pl.when(j == count - 1)
        def _():
            mine = (me >> bit) & 1
            for c in range(n // 2):
                away, here = with_bit(c, bit, 1 - mine), with_bit(c, bit, mine)

                @pl.loop(0, rows // BLK)
                def _(b):
                    src = rows_at(b * BLK)
                    encode_rows(
                        [total[t, away, src, :] for t in range(count)],
                        msg,
                        rows_at(c * rows + b * BLK),
                    )
                    for t in range(count):
                        keep[t, c, src, :] = total[t, here, src, :]

    out = [
        jax.ShapeDtypeStruct((n // 2 * rows, width + LANES), jnp.bfloat16),
        jax.ShapeDtypeStruct((count, n // 2, rows, tile), jnp.float32),
    ]
    args = [own, oth, w]
    specs = [HBM, ANY, pl.BlockSpec((tile, hidden), lambda j, s: (first + j, 0))]
    scratch = [
        pltpu.VMEM((2, half, hidden), jnp.bfloat16),
        pltpu.VMEM((count, n, rows, tile), jnp.float32),
        pltpu.SemaphoreType.DMA((3,)),
    ]
    if sketch is not None:
        args.append(sketch)
        specs.append(HBM)
        out.append(jax.ShapeDtypeStruct((2 * half, sketch.shape[0]), jnp.float32))
        scratch.append(pltpu.VMEM(sketch.shape, sketch.dtype))
    return call(
        kernel,
        idx,
        args,
        specs,
        out,
        [whole(o.shape) for o in out],
        "backward",
        (count,),
        (4 * half * hidden * width, 2 * hidden * width + 12 * half * width),
        after,
        scratch,
    )


def fold(idx, keep, got, bit, pos, after):
    count, m, rows, tile = keep.shape

    def kernel(idx, keep, got, msg, rest):
        mine = (idx[0] >> bit) & 1
        for c in range(m // 2):
            away, here = with_bit(c, pos, 1 - mine), with_bit(c, pos, mine)

            @pl.loop(0, rows // BLK)
            def _(b):
                src = rows_at(b * BLK)
                plus = decode_rows(got, rows_at(away * rows + b * BLK), tile, count)
                encode_rows(
                    [keep[t, away, src, :] + plus[t] for t in range(count)],
                    msg,
                    rows_at(c * rows + b * BLK),
                )
                plus = decode_rows(got, rows_at(here * rows + b * BLK), tile, count)
                for t in range(count):
                    rest[t, c, src, :] = keep[t, here, src, :] + plus[t]

    out = [
        jax.ShapeDtypeStruct((m // 2 * rows, got.shape[1]), jnp.bfloat16),
        jax.ShapeDtypeStruct((count, m // 2, rows, tile), jnp.float32),
    ]
    return call(
        kernel,
        idx,
        [keep, got],
        [whole(keep.shape), whole(got.shape)],
        out,
        [whole(o.shape) for o in out],
        "fold",
        (1,),
        (0, 12 * keep.size),
        after,
    )


def finish(idx, keeps, gots, after):
    count, _, rows, tile = keeps[0].shape
    pieces = len(keeps)

    def kernel(idx, *refs):
        out = refs[-1]
        for p in range(pieces):

            @pl.loop(0, rows // BLK)
            def _(b):
                at = rows_at(b * BLK)
                plus = decode_rows(refs[pieces + p], at, tile, count)
                for t in range(count):
                    lo = (p * count + t) * tile
                    out[at, lo : lo + tile] = (refs[p][t, 0, at, :] + plus[t]).astype(
                        jnp.bfloat16
                    )

    args = list(keeps) + list(gots)
    out = [jax.ShapeDtypeStruct((rows, pieces * count * tile), jnp.bfloat16)]
    (grad,), _ = call(
        kernel,
        idx,
        args,
        [whole(a.shape) for a in args],
        out,
        [whole(out[0].shape)],
        "finish",
        (1,),
        (0, 16 * rows * count * tile),
        after,
    )
    return grad


def gate(idx, arrays, after):
    k = len(arrays)

    def kernel(idx, *refs):
        pass

    out, token = call(
        kernel,
        idx,
        arrays,
        [ANY] * k,
        [jax.ShapeDtypeStruct(a.shape, a.dtype) for a in arrays],
        [ANY] * k,
        "gate",
        (1,),
        (0, 0),
        after,
        aliases={1 + i: i for i in range(k)},
    )
    return list(out), [token]


def add(idx, a, b, after):
    def kernel(idx, a, b, out):
        out[...] = a[...] + b[...]

    specs = [whole(a.shape)] * 2
    out = [jax.ShapeDtypeStruct(a.shape, a.dtype)]
    work = (a.size, 12 * a.size)
    (total,), token = call(kernel, idx, [a, b], specs, out, specs[:1], "add", (1,), work, after)
    return total, [token]


def forward(idx, chunks, w, sketch, lo, hi, after):
    rows, feats = chunks[0][1].shape
    m = len(chunks)
    tile = pick(w.shape[1], H_TILE)
    hidden = (hi - lo) * tile
    part = m // 2 * rows

    def kernel(idx, *refs):
        w, sk, send, keep, left, x, sems = refs[m:]
        me, core = idx[0], idx[1]

        @pl.when(pl.program_id(0) == 0)
        def _():
            copies = []
            for i, (mask, _) in enumerate(chunks):
                d = me ^ mask
                side = 1 - ((d // m) ^ core)
                to = pl.ds(pl.multiple_of(side * part + ((d % m) >> 1) * rows, BLK), rows)
                copies.append(pltpu.make_async_copy(refs[i], x.at[to], sems.at[i]))
            for c in copies:
                c.start()
            for c in copies:
                c.wait()
            left[...] = contract_last(x[...], sk[...])

        t = jnp.dot(x[...], w[...], preferred_element_type=jnp.float32)
        send[...] = t[:part]
        keep[...] = t[part:]

    out = [jax.ShapeDtypeStruct((part, hidden), jnp.float32)] * 2
    out.append(jax.ShapeDtypeStruct((2 * part, sketch.shape[0]), jnp.float32))
    column = pl.BlockSpec((part, tile), lambda j, s: (0, j))
    return call(
        kernel,
        idx,
        [c[1] for c in chunks] + [w, sketch],
        [ANY] * m + [pl.BlockSpec((feats, tile), lambda j, s: (0, lo + j)), whole(sketch.shape)],
        out,
        [column, column, whole(out[2].shape)],
        "forward",
        (hidden // tile,),
        (4 * part * feats * hidden, 2 * feats * hidden + 8 * part * hidden),
        after,
        [pltpu.VMEM((2 * part, feats), jnp.bfloat16), pltpu.SemaphoreType.DMA((m,))],
    )


def combine(idx, keep, got, lo, total, batch, rows, before, after):
    part, width = keep.shape
    m = part // rows

    def kernel(idx, keep, got, *refs):
        out, x, sems = refs[-3:]
        mine = (idx[0] & 1) ^ batch
        x[...] = (keep[...] + got[...]).astype(jnp.bfloat16)
        copies = []
        for i in range(m):
            to = pl.ds(pl.multiple_of((2 * i + mine) * rows, BLK), rows)
            copies.append(
                pltpu.make_async_copy(
                    x.at[pl.ds(i * rows, rows)], out.at[to, pl.ds(lo, width)], sems.at[i]
                )
            )
        for c in copies:
            c.start()
        for c in copies:
            c.wait()

    (out,), token = call(
        kernel,
        idx,
        [keep, got] + before,
        [whole(keep.shape)] * 2 + [HBM] * len(before),
        [jax.ShapeDtypeStruct((2 * part, total), jnp.bfloat16)],
        [HBM],
        "combine",
        (1,),
        (0, 10 * part * width),
        after,
        [pltpu.VMEM((part, width), jnp.bfloat16), pltpu.SemaphoreType.DMA((m,))],
        aliases={3: 0} if before else None,
    )
    return out, [token]


def sketch_part(idx, lefts, right, rows, after):
    tokens, width = right.shape
    half = tokens // 2
    part = half // 2
    examples = half // LEN

    def kernel(idx, first, second, right, out):
        me, core = idx[0], idx[1]
        for side in (0, 1):
            owner = 1 - (side ^ core)
            for e in range(examples):
                total = jnp.zeros((width, width), jnp.float32)
                for i in range(part // rows):
                    if 2 * i * rows // LEN != e:
                        continue
                    for batch, left in enumerate((first, second)):
                        at = owner * half + (2 * i + ((me & 1) ^ batch)) * rows
                        lo = side * part + i * rows
                        total += lax.dot_general(
                            left[lo : lo + rows, :],
                            right[pl.ds(pl.multiple_of(at, BLK), rows), :],
                            (((0,), (0,)), ((), ())),
                            precision=lax.Precision.HIGHEST,
                            preferred_element_type=jnp.float32,
                        )
                out[owner * examples + e] = total

    args = [*lefts, right]
    out = [jax.ShapeDtypeStruct((tokens // LEN, width, width), jnp.float32)]
    (sketch,), token = call(
        kernel,
        idx,
        args,
        [whole(a.shape) for a in args],
        out,
        [whole(out[0].shape)],
        "sketch_part",
        (1,),
        (0, 8 * tokens * width),
        after,
    )
    return sketch, [token]


def body(inputs, cotangent, weight, in_sketch, out_sketch):
    n = lax.axis_size("outp")
    bits = n.bit_length() - 1
    rows, feats = inputs.shape
    hidden = weight.shape[1]
    idx = jnp.stack([lax.axis_index("outp"), lax.axis_index("inp")]).astype(jnp.int32)

    def partner(x, bit):
        return lax.ppermute(x, "outp", [(d, d ^ (1 << bit)) for d in range(n)])

    def swap(x):
        return lax.ppermute(x, "inp", [(0, 1), (1, 0)])

    chunks = {0: inputs}

    def wave_of(mask):
        if mask & 1 and mask > 3:
            return max(3, mask.bit_count())
        return 2 if mask == 3 else mask.bit_count()

    def step_of(mask):
        if mask == 3:
            return 1
        return 0 if mask & 1 else (mask & -mask).bit_length() - 1

    def wave(k):
        for mask in sorted(range(1, n), reverse=True):
            if wave_of(mask) == k:
                bit = step_of(mask)
                chunks[mask] = partner(chunks[mask ^ (1 << bit)], bit)

    def hold(k, after):
        masks = [m for m in range(1, n) if wave_of(m) == k]
        held, token = gate(idx, [chunks[m] for m in masks], after)
        chunks.update(zip(masks, held))
        return token

    grad_other = swap(cotangent)
    wave(1)

    orders = [list(range(bits)), [1, 0] + list(range(2, bits))]
    tile = pick(feats // PIECES, F_TILE)
    count = feats // PIECES // tile
    msgs, keeps = [], []
    token = []
    for p in range(PIECES):
        outs, t = backward(
            idx,
            cotangent,
            grad_other,
            weight,
            out_sketch if p == 0 else None,
            count,
            tile,
            p * count,
            rows,
            orders[p][0],
            token,
        )
        token = [t]
        msgs.append(partner(outs[0], orders[p][0]))
        keeps.append(outs[1])
        if p == 0:
            right = outs[2]
        else:
            right, token = add(idx, right, right_got, token)
        right_got = partner(right, p)
        token = hold(1 + p, token)
        wave(2 + p)
    for k in range(PIECES, bits - 1):
        right, token = add(idx, right, right_got, token)
        right_got = partner(right, k)
    last = max(wave_of(m) for m in range(1, n))
    for k in range(PIECES + 1, last):
        token = hold(k, token)
        wave(k + 1)

    def folded(p, step, after):
        done, bit = orders[p][:step], orders[p][step]
        pos = sum(1 for k in range(bit) if k not in done)
        (msg, keeps[p]), t = fold(idx, keeps[p], msgs[p], bit, pos, after)
        msgs[p] = partner(msg, bit)
        return [t]

    tiles = hidden // pick(hidden, H_TILE)

    def batch_forward(batch, lo, hi, after):
        parts = [(m, chunks[m]) for m in range(n) if m & 1 == batch]
        outs, t = forward(idx, parts, weight, in_sketch, lo, hi, after)
        start = lo * (hidden // tiles)
        return (outs[1], swap(outs[0]), start, hidden, batch, rows), outs[2], [t]

    cut = -(-tiles // 2)
    token = folded(0, 1, token)
    first, left1, token = batch_forward(0, 0, tiles, token)
    token = hold(last, token)
    token = folded(1, 1, token)
    right, token = add(idx, right, right_got, token)
    right_got = partner(right, bits - 1)
    second, left2, token = batch_forward(1, 0, cut, token)
    token = folded(0, 2, token)
    third, _, token = batch_forward(1, cut, tiles, token)
    token = folded(1, 2, token)
    for step in range(3, bits):
        for p in range(PIECES):
            token = folded(p, step, token)
    outputs, token = combine(idx, *first, [], token + [msgs[0]])
    right, token = add(idx, right, right_got, token)
    part, token = sketch_part(idx, [left1, left2], right, rows, token)
    outputs, token = combine(idx, *second, [outputs], token)
    outputs, token = combine(idx, *third, [outputs], token)
    part = (part + swap(part)) * (1.0 / LEN**0.5)
    sketches = part.reshape(part.shape[0], -1)
    input_grad = finish(idx, keeps, msgs, token)
    return (outputs, input_grad, sketches)


def solution(mesh):
    placed = (
        P(("groups", "outp"), "inp"),
        P(("groups", "inp"), "outp"),
        P("inp", "outp"),
        P(None, "inp"),
        P(None, "outp"),
    )
    return jax.shard_map(
        body,
        mesh=mesh,
        in_specs=placed,
        out_specs=(P(("groups", "inp"), "outp"), P(("groups", "outp"), "inp"), P("groups", None)),
        check_vma=False,
    )
```

```python
import jax
import jax.numpy as jnp
from jax import lax
from jax.experimental import pallas as pl
from jax.experimental.pallas import tpu as pltpu
from jax.sharding import PartitionSpec as P

LEN = 128
LANES = 128
BLK = 16
LN2 = 0.6931471805599453
SPAN = 248.0
SHIFT = 124.0
PIECES = 2
F_TILE = 512
H_TILE = 512
VMEM_MIB = {"backward": 32, "forward": 24}
MIB = 1 << 20
TIMES = {"forward": 1 << 34, "fold": 0, "combine": 1 << 34, "sketch_part": 1 << 34}
ANY = pl.BlockSpec(memory_space=pl.ANY)
HBM = pl.BlockSpec(memory_space=pltpu.HBM)


def pick(extent, cap):
    best = LANES
    for t in range(LANES, min(cap, extent) + 1, LANES):
        if extent % t == 0:
            best = t
    return best


def contract_last(a, b):
    return lax.dot_general(a, b, (((1,), (1,)), ((), ())), preferred_element_type=jnp.float32)


def whole(shape):
    return pl.BlockSpec(shape, lambda *_: (0,) * len(shape))


def call(
    kernel, idx, args, specs, out_shape, out_specs, name, grid, work, after, scratch=(), aliases=None
):
    token = jax.ShapeDtypeStruct((8, LANES), jnp.float32)
    n_args, n_after, n_out = len(args), len(after), len(out_shape)

    def with_token(idx, *refs):
        ins = refs[:n_args]
        outs = refs[n_args + n_after :]
        outs[n_out][...] = jnp.zeros((8, LANES), jnp.float32)
        kernel(idx, *ins, *outs[:n_out], *outs[n_out + 1 :])

    out = pl.pallas_call(
        with_token,
        out_shape=list(out_shape) + [token],
        grid_spec=pltpu.PrefetchScalarGridSpec(
            num_scalar_prefetch=1,
            grid=grid,
            in_specs=list(specs) + [ANY] * n_after,
            out_specs=list(out_specs) + [whole(token.shape)],
            scratch_shapes=list(scratch),
        ),
        compiler_params=pltpu.CompilerParams(vmem_limit_bytes=VMEM_MIB.get(name, 14) * MIB),
        cost_estimate=pl.CostEstimate(
            flops=TIMES.get(name, work[0]), bytes_accessed=work[1], transcendentals=0
        ),
        input_output_aliases=aliases or {},
        name=name,
    )(idx, *args, *after)
    return out[:-1], out[-1]


def encode_rows(tiles, msg, at):
    top = jnp.abs(tiles[0])
    for v in tiles[1:]:
        top = jnp.maximum(top, jnp.abs(v))
    top = jnp.max(top, axis=1, keepdims=True)
    scale = jnp.maximum(top * 1.004, 2.0**-110).astype(jnp.bfloat16).astype(jnp.float32)
    gain = SPAN / scale
    col = 0
    for v in tiles:
        w = jnp.exp2(jnp.abs(v) * gain - SHIFT)
        msg[at, col : col + v.shape[1]] = jnp.where(v < 0, -w, w).astype(jnp.bfloat16)
        col += v.shape[1]
    msg[at, col : col + LANES] = jnp.broadcast_to(scale, (BLK, LANES)).astype(jnp.bfloat16)


def decode_rows(msg, at, tile, count):
    scale = msg[at, tile * count : tile * count + LANES].astype(jnp.float32)[:, :1]
    scale = scale * (1.0 / (SPAN * LN2))
    out = []
    for t in range(count):
        w = msg[at, t * tile : (t + 1) * tile].astype(jnp.float32)
        a = (lax.log(jnp.maximum(jnp.abs(w), 2.0**-SHIFT)) + SHIFT * LN2) * scale
        out.append(jnp.where(w < 0, -a, a))
    return out


def with_bit(c, pos, value):
    low = c & ((1 << pos) - 1)
    return ((c >> pos) << (pos + 1)) + low + value * (1 << pos)


def rows_at(start):
    return pl.ds(pl.multiple_of(start, BLK), BLK)


def backward(idx, own, oth, w, sketch, count, tile, first, rows, bit, after):
    half, hidden = own.shape
    n = 2 * half // rows
    width = count * tile

    def kernel(idx, own, oth, w, *rest):
        if sketch is None:
            msg, keep, x, total, sems = rest
        else:
            sk, msg, keep, right, x, total, sems, sk_here = rest
        j = pl.program_id(0)
        me, core = idx[0], idx[1]

        @pl.when(j == 0)
        def _():
            a = pltpu.make_async_copy(own, x.at[core], sems.at[0])
            b = pltpu.make_async_copy(oth, x.at[1 - core], sems.at[1])
            a.start()
            b.start()
            if sketch is not None:
                c = pltpu.make_async_copy(sk, sk_here, sems.at[2])
                c.start()
                c.wait()
            a.wait()
            b.wait()
            if sketch is not None:
                right[...] = contract_last(x[...].reshape(2 * half, hidden), sk_here[...])

        xs = x[...].reshape(2 * half, hidden)
        total[j] = contract_last(xs, w[...]).reshape(n, rows, tile)

        @pl.when(j == count - 1)
        def _():
            mine = (me >> bit) & 1
            for c in range(n // 2):
                away, here = with_bit(c, bit, 1 - mine), with_bit(c, bit, mine)

                @pl.loop(0, rows // BLK)
                def _(b):
                    src = rows_at(b * BLK)
                    encode_rows(
                        [total[t, away, src, :] for t in range(count)],
                        msg,
                        rows_at(c * rows + b * BLK),
                    )
                    for t in range(count):
                        keep[t, c, src, :] = total[t, here, src, :]

    out = [
        jax.ShapeDtypeStruct((n // 2 * rows, width + LANES), jnp.bfloat16),
        jax.ShapeDtypeStruct((count, n // 2, rows, tile), jnp.float32),
    ]
    args = [own, oth, w]
    specs = [HBM, ANY, pl.BlockSpec((tile, hidden), lambda j, s: (first + j, 0))]
    scratch = [
        pltpu.VMEM((2, half, hidden), jnp.bfloat16),
        pltpu.VMEM((count, n, rows, tile), jnp.float32),
        pltpu.SemaphoreType.DMA((3,)),
    ]
    if sketch is not None:
        args.append(sketch)
        specs.append(HBM)
        out.append(jax.ShapeDtypeStruct((2 * half, sketch.shape[0]), jnp.float32))
        scratch.append(pltpu.VMEM(sketch.shape, sketch.dtype))
    return call(
        kernel,
        idx,
        args,
        specs,
        out,
        [whole(o.shape) for o in out],
        "backward",
        (count,),
        (4 * half * hidden * width, 2 * hidden * width + 12 * half * width),
        after,
        scratch,
    )


def fold(idx, keep, got, bit, pos, after):
    count, m, rows, tile = keep.shape

    def kernel(idx, keep, got, msg, rest):
        mine = (idx[0] >> bit) & 1
        for c in range(m // 2):
            away, here = with_bit(c, pos, 1 - mine), with_bit(c, pos, mine)

            @pl.loop(0, rows // BLK)
            def _(b):
                src = rows_at(b * BLK)
                plus = decode_rows(got, rows_at(away * rows + b * BLK), tile, count)
                encode_rows(
                    [keep[t, away, src, :] + plus[t] for t in range(count)],
                    msg,
                    rows_at(c * rows + b * BLK),
                )
                plus = decode_rows(got, rows_at(here * rows + b * BLK), tile, count)
                for t in range(count):
                    rest[t, c, src, :] = keep[t, here, src, :] + plus[t]

    out = [
        jax.ShapeDtypeStruct((m // 2 * rows, got.shape[1]), jnp.bfloat16),
        jax.ShapeDtypeStruct((count, m // 2, rows, tile), jnp.float32),
    ]
    return call(
        kernel,
        idx,
        [keep, got],
        [whole(keep.shape), whole(got.shape)],
        out,
        [whole(o.shape) for o in out],
        "fold",
        (1,),
        (0, 12 * keep.size),
        after,
    )


def finish(idx, keeps, gots, after):
    count, _, rows, tile = keeps[0].shape
    pieces = len(keeps)

    def kernel(idx, *refs):
        out = refs[-1]
        for p in range(pieces):

            @pl.loop(0, rows // BLK)
            def _(b):
                at = rows_at(b * BLK)
                plus = decode_rows(refs[pieces + p], at, tile, count)
                for t in range(count):
                    lo = (p * count + t) * tile
                    out[at, lo : lo + tile] = (refs[p][t, 0, at, :] + plus[t]).astype(
                        jnp.bfloat16
                    )

    args = list(keeps) + list(gots)
    out = [jax.ShapeDtypeStruct((rows, pieces * count * tile), jnp.bfloat16)]
    (grad,), _ = call(
        kernel,
        idx,
        args,
        [whole(a.shape) for a in args],
        out,
        [whole(out[0].shape)],
        "finish",
        (1,),
        (0, 16 * rows * count * tile),
        after,
    )
    return grad


def gate(idx, arrays, after):
    k = len(arrays)

    def kernel(idx, *refs):
        pass

    out, token = call(
        kernel,
        idx,
        arrays,
        [ANY] * k,
        [jax.ShapeDtypeStruct(a.shape, a.dtype) for a in arrays],
        [ANY] * k,
        "gate",
        (1,),
        (0, 0),
        after,
        aliases={1 + i: i for i in range(k)},
    )
    return list(out), [token]


def add(idx, a, b, after):
    def kernel(idx, a, b, out):
        out[...] = a[...] + b[...]

    specs = [whole(a.shape)] * 2
    out = [jax.ShapeDtypeStruct(a.shape, a.dtype)]
    work = (a.size, 12 * a.size)
    (total,), token = call(kernel, idx, [a, b], specs, out, specs[:1], "add", (1,), work, after)
    return total, [token]


def forward(idx, chunks, w, sketch, lo, hi, after):
    rows, feats = chunks[0][1].shape
    m = len(chunks)
    tile = pick(w.shape[1], H_TILE)
    hidden = (hi - lo) * tile
    part = m // 2 * rows

    def kernel(idx, *refs):
        w, sk, send, keep, left, x, sems = refs[m:]
        me, core = idx[0], idx[1]

        @pl.when(pl.program_id(0) == 0)
        def _():
            copies = []
            for i, (mask, _) in enumerate(chunks):
                d = me ^ mask
                side = 1 - ((d // m) ^ core)
                to = pl.ds(pl.multiple_of(side * part + ((d % m) >> 1) * rows, BLK), rows)
                copies.append(pltpu.make_async_copy(refs[i], x.at[to], sems.at[i]))
            for c in copies:
                c.start()
            for c in copies:
                c.wait()
            left[...] = contract_last(x[...], sk[...])

        t = jnp.dot(x[...], w[...], preferred_element_type=jnp.float32)
        send[...] = t[:part]
        keep[...] = t[part:]

    out = [jax.ShapeDtypeStruct((part, hidden), jnp.float32)] * 2
    out.append(jax.ShapeDtypeStruct((2 * part, sketch.shape[0]), jnp.float32))
    column = pl.BlockSpec((part, tile), lambda j, s: (0, j))
    return call(
        kernel,
        idx,
        [c[1] for c in chunks] + [w, sketch],
        [ANY] * m + [pl.BlockSpec((feats, tile), lambda j, s: (0, lo + j)), whole(sketch.shape)],
        out,
        [column, column, whole(out[2].shape)],
        "forward",
        (hidden // tile,),
        (4 * part * feats * hidden, 2 * feats * hidden + 8 * part * hidden),
        after,
        [pltpu.VMEM((2 * part, feats), jnp.bfloat16), pltpu.SemaphoreType.DMA((m,))],
    )


def combine(idx, keep, got, lo, total, batch, rows, before, after):
    part, width = keep.shape
    m = part // rows

    def kernel(idx, keep, got, *refs):
        out, x, sems = refs[-3:]
        mine = (idx[0] & 1) ^ batch
        x[...] = (keep[...] + got[...]).astype(jnp.bfloat16)
        copies = []
        for i in range(m):
            to = pl.ds(pl.multiple_of((2 * i + mine) * rows, BLK), rows)
            copies.append(
                pltpu.make_async_copy(
                    x.at[pl.ds(i * rows, rows)], out.at[to, pl.ds(lo, width)], sems.at[i]
                )
            )
        for c in copies:
            c.start()
        for c in copies:
            c.wait()

    (out,), token = call(
        kernel,
        idx,
        [keep, got] + before,
        [whole(keep.shape)] * 2 + [HBM] * len(before),
        [jax.ShapeDtypeStruct((2 * part, total), jnp.bfloat16)],
        [HBM],
        "combine",
        (1,),
        (0, 10 * part * width),
        after,
        [pltpu.VMEM((part, width), jnp.bfloat16), pltpu.SemaphoreType.DMA((m,))],
        aliases={3: 0} if before else None,
    )
    return out, [token]


def sketch_part(idx, lefts, right, rows, after):
    tokens, width = right.shape
    half = tokens // 2
    part = half // 2
    examples = half // LEN

    def kernel(idx, first, second, right, out):
        me, core = idx[0], idx[1]
        for side in (0, 1):
            owner = 1 - (side ^ core)
            for e in range(examples):
                total = jnp.zeros((width, width), jnp.float32)
                for i in range(part // rows):
                    if 2 * i * rows // LEN != e:
                        continue
                    for batch, left in enumerate((first, second)):
                        at = owner * half + (2 * i + ((me & 1) ^ batch)) * rows
                        lo = side * part + i * rows
                        total += lax.dot_general(
                            left[lo : lo + rows, :],
                            right[pl.ds(pl.multiple_of(at, BLK), rows), :],
                            (((0,), (0,)), ((), ())),
                            precision=lax.Precision.HIGHEST,
                            preferred_element_type=jnp.float32,
                        )
                out[owner * examples + e] = total

    args = [*lefts, right]
    out = [jax.ShapeDtypeStruct((tokens // LEN, width, width), jnp.float32)]
    (sketch,), token = call(
        kernel,
        idx,
        args,
        [whole(a.shape) for a in args],
        out,
        [whole(out[0].shape)],
        "sketch_part",
        (1,),
        (0, 8 * tokens * width),
        after,
    )
    return sketch, [token]


def body(inputs, cotangent, weight, in_sketch, out_sketch):
    n = lax.axis_size("outp")
    bits = n.bit_length() - 1
    rows, feats = inputs.shape
    hidden = weight.shape[1]
    idx = jnp.stack([lax.axis_index("outp"), lax.axis_index("inp")]).astype(jnp.int32)

    def partner(x, bit):
        return lax.ppermute(x, "outp", [(d, d ^ (1 << bit)) for d in range(n)])

    def swap(x):
        return lax.ppermute(x, "inp", [(0, 1), (1, 0)])

    chunks = {0: inputs}

    def wave_of(mask):
        if mask & 1 and mask > 3:
            return max(3, mask.bit_count())
        return 2 if mask == 3 else mask.bit_count()

    def step_of(mask):
        if mask == 3:
            return 1
        return 0 if mask & 1 else (mask & -mask).bit_length() - 1

    def wave(k):
        for mask in sorted(range(1, n), reverse=True):
            if wave_of(mask) == k:
                bit = step_of(mask)
                chunks[mask] = partner(chunks[mask ^ (1 << bit)], bit)

    def hold(k, after):
        masks = [m for m in range(1, n) if wave_of(m) == k]
        held, token = gate(idx, [chunks[m] for m in masks], after)
        chunks.update(zip(masks, held))
        return token

    grad_other = swap(cotangent)
    wave(1)

    orders = [list(range(bits)), [1, 0] + list(range(2, bits))]
    tile = pick(feats // PIECES, F_TILE)
    count = feats // PIECES // tile
    msgs, keeps = [], []
    token = []
    for p in range(PIECES):
        outs, t = backward(
            idx,
            cotangent,
            grad_other,
            weight,
            out_sketch if p == 0 else None,
            count,
            tile,
            p * count,
            rows,
            orders[p][0],
            token,
        )
        token = [t]
        msgs.append(partner(outs[0], orders[p][0]))
        keeps.append(outs[1])
        if p == 0:
            right = outs[2]
            right_got = partner(right, 0)
        token = hold(1 + p, token)
        wave(2 + p)
    last = max(wave_of(m) for m in range(1, n))
    for k in range(PIECES + 1, last):
        token = hold(k, token)
        wave(k + 1)

    def folded(p, step, after):
        done, bit = orders[p][:step], orders[p][step]
        pos = sum(1 for k in range(bit) if k not in done)
        (msg, keeps[p]), t = fold(idx, keeps[p], msgs[p], bit, pos, after)
        msgs[p] = partner(msg, bit)
        return [t]

    tiles = hidden // pick(hidden, H_TILE)

    def batch_forward(batch, lo, hi, after):
        parts = [(m, chunks[m]) for m in range(n) if m & 1 == batch]
        outs, t = forward(idx, parts, weight, in_sketch, lo, hi, after)
        start = lo * (hidden // tiles)
        return (outs[1], swap(outs[0]), start, hidden, batch, rows), outs[2], [t]

    cut = -(-tiles // 2)
    token = folded(0, 1, token)
    first, left1, token = batch_forward(0, 0, tiles, token)
    token = hold(last, token)
    token = folded(1, 1, token)
    right, token = add(idx, right, right_got, token)
    right_got = partner(right, 1)
    second, left2, token = batch_forward(1, 0, cut, token)
    token = folded(0, 2, token)
    right, token = add(idx, right, right_got, token)
    right_got = partner(right, 2)
    third, _, token = batch_forward(1, cut, tiles, token)
    token = folded(1, 2, token)
    for step in range(3, bits):
        for p in range(PIECES):
            token = folded(p, step, token)
    outputs, token = combine(idx, *first, [], token + [msgs[0]])
    right, token = add(idx, right, right_got, token)
    for k in range(3, bits):
        right, token = add(idx, right, partner(right, k), token)
    part, token = sketch_part(idx, [left1, left2], right, rows, token)
    outputs, token = combine(idx, *second, [outputs], token)
    outputs, token = combine(idx, *third, [outputs], token)
    part = (part + swap(part)) * (1.0 / LEN**0.5)
    sketches = part.reshape(part.shape[0], -1)
    input_grad = finish(idx, keeps, msgs, token)
    return (outputs, input_grad, sketches)


def solution(mesh):
    placed = (
        P(("groups", "outp"), "inp"),
        P(("groups", "inp"), "outp"),
        P("inp", "outp"),
        P(None, "inp"),
        P(None, "outp"),
    )
    return jax.shard_map(
        body,
        mesh=mesh,
        in_specs=placed,
        out_specs=(P(("groups", "inp"), "outp"), P(("groups", "outp"), "inp"), P("groups", None)),
        check_vma=False,
    )
```

```python
import jax
import jax.numpy as jnp
from jax import lax
from jax.experimental import pallas as pl
from jax.experimental.pallas import tpu as pltpu
from jax.sharding import PartitionSpec as P

LEN = 128
LANES = 128
BLK = 16
LN2 = 0.6931471805599453
SPAN = 248.0
SHIFT = 124.0
PIECES = 2
F_TILE = 512
H_TILE = 512
VMEM_MIB = {"backward": 32, "forward": 24}
MIB = 1 << 20
RIGHT_ROWS = 32
TIMES = {"backward": 19 * 10**9, "forward": 1 << 34, "fold": 0, "combine": 1 << 34, "sketch_part": 1 << 34}
ANY = pl.BlockSpec(memory_space=pl.ANY)
HBM = pl.BlockSpec(memory_space=pltpu.HBM)


def pick(extent, cap):
    best = LANES
    for t in range(LANES, min(cap, extent) + 1, LANES):
        if extent % t == 0:
            best = t
    return best


def contract_last(a, b):
    return lax.dot_general(a, b, (((1,), (1,)), ((), ())), preferred_element_type=jnp.float32)


def whole(shape):
    return pl.BlockSpec(shape, lambda *_: (0,) * len(shape))


def call(
    kernel, idx, args, specs, out_shape, out_specs, name, grid, work, after, scratch=(), aliases=None
):
    token = jax.ShapeDtypeStruct((8, LANES), jnp.float32)
    n_args, n_after, n_out = len(args), len(after), len(out_shape)

    def with_token(idx, *refs):
        ins = refs[:n_args]
        outs = refs[n_args + n_after :]
        outs[n_out][...] = jnp.zeros((8, LANES), jnp.float32)
        kernel(idx, *ins, *outs[:n_out], *outs[n_out + 1 :])

    out = pl.pallas_call(
        with_token,
        out_shape=list(out_shape) + [token],
        grid_spec=pltpu.PrefetchScalarGridSpec(
            num_scalar_prefetch=1,
            grid=grid,
            in_specs=list(specs) + [ANY] * n_after,
            out_specs=list(out_specs) + [whole(token.shape)],
            scratch_shapes=list(scratch),
        ),
        compiler_params=pltpu.CompilerParams(vmem_limit_bytes=VMEM_MIB.get(name, 14) * MIB),
        cost_estimate=pl.CostEstimate(
            flops=TIMES.get(name, work[0]), bytes_accessed=work[1], transcendentals=0
        ),
        input_output_aliases=aliases or {},
        name=name,
    )(idx, *args, *after)
    return out[:-1], out[-1]


def encode_rows(tiles, msg, at):
    top = jnp.abs(tiles[0])
    for v in tiles[1:]:
        top = jnp.maximum(top, jnp.abs(v))
    top = jnp.max(top, axis=1, keepdims=True)
    scale = jnp.maximum(top * 1.004, 2.0**-110).astype(jnp.bfloat16).astype(jnp.float32)
    gain = SPAN / scale
    col = 0
    for v in tiles:
        w = jnp.exp2(jnp.abs(v) * gain - SHIFT)
        msg[at, col : col + v.shape[1]] = jnp.where(v < 0, -w, w).astype(jnp.bfloat16)
        col += v.shape[1]
    msg[at, col : col + LANES] = jnp.broadcast_to(scale, (BLK, LANES)).astype(jnp.bfloat16)


def decode_rows(msg, at, tile, count):
    scale = msg[at, tile * count : tile * count + LANES].astype(jnp.float32)[:, :1]
    scale = scale * (1.0 / (SPAN * LN2))
    out = []
    for t in range(count):
        w = msg[at, t * tile : (t + 1) * tile].astype(jnp.float32)
        a = (lax.log(jnp.maximum(jnp.abs(w), 2.0**-SHIFT)) + SHIFT * LN2) * scale
        out.append(jnp.where(w < 0, -a, a))
    return out


def put_right(value, msg):
    base = msg.shape[0] - RIGHT_ROWS
    for q in range(value.shape[0] // RIGHT_ROWS):
        left_over = value[q * RIGHT_ROWS : (q + 1) * RIGHT_ROWS, :]
        for k in range(3):
            part = left_over.astype(jnp.bfloat16)
            lo = (3 * q + k) * LANES
            msg[base:, lo : lo + LANES] = part
            left_over = left_over - part.astype(jnp.float32)


def add_right(value, msg):
    base = msg.shape[0] - RIGHT_ROWS
    out = []
    for q in range(value.shape[0] // RIGHT_ROWS):
        lo = 3 * q * LANES
        parts = [
            msg[base:, lo + k * LANES : lo + (k + 1) * LANES].astype(jnp.float32) for k in range(3)
        ]
        got = parts[0] + (parts[1] + parts[2])
        out.append(value[q * RIGHT_ROWS : (q + 1) * RIGHT_ROWS, :] + got)
    return jnp.concatenate(out, axis=0)


def with_bit(c, pos, value):
    low = c & ((1 << pos) - 1)
    return ((c >> pos) << (pos + 1)) + low + value * (1 << pos)


def rows_at(start):
    return pl.ds(pl.multiple_of(start, BLK), BLK)


def backward(idx, own, oth, w, sketch, count, tile, first, rows, bit, after):
    half, hidden = own.shape
    n = 2 * half // rows
    width = count * tile

    def kernel(idx, own, oth, w, *rest):
        if sketch is None:
            msg, keep, x, total, sems = rest
        else:
            sk, msg, keep, right, x, total, sems, sk_here = rest
        j = pl.program_id(0)
        me, core = idx[0], idx[1]

        @pl.when(j == 0)
        def _():
            a = pltpu.make_async_copy(own, x.at[core], sems.at[0])
            b = pltpu.make_async_copy(oth, x.at[1 - core], sems.at[1])
            a.start()
            b.start()
            if sketch is not None:
                c = pltpu.make_async_copy(sk, sk_here, sems.at[2])
                c.start()
                c.wait()
            a.wait()
            b.wait()
            if sketch is not None:
                low, high = jnp.zeros_like(sk_here[...]), sk_here[...]
                first_block = jnp.concatenate([high, low], axis=0)
                second_block = jnp.concatenate([low, high], axis=0)
                right[...] = contract_last(x[core, : half // 2, :], first_block) + contract_last(
                    x[core, half // 2 :, :], second_block
                )
                put_right(right[...], msg)

        xs = x[...].reshape(2 * half, hidden)
        total[j] = contract_last(xs, w[...]).reshape(n, rows, tile)

        @pl.when(j == count - 1)
        def _():
            mine = (me >> bit) & 1
            for c in range(n // 2):
                away, here = with_bit(c, bit, 1 - mine), with_bit(c, bit, mine)

                @pl.loop(0, rows // BLK)
                def _(b):
                    src = rows_at(b * BLK)
                    encode_rows(
                        [total[t, away, src, :] for t in range(count)],
                        msg,
                        rows_at(c * rows + b * BLK),
                    )
                    for t in range(count):
                        keep[t, c, src, :] = total[t, here, src, :]

    extra = 0 if sketch is None else RIGHT_ROWS
    out = [
        jax.ShapeDtypeStruct((n // 2 * rows + extra, width + LANES), jnp.bfloat16),
        jax.ShapeDtypeStruct((count, n // 2, rows, tile), jnp.float32),
    ]
    args = [own, oth, w]
    specs = [HBM, ANY, pl.BlockSpec((tile, hidden), lambda j, s: (first + j, 0))]
    scratch = [
        pltpu.VMEM((2, half, hidden), jnp.bfloat16),
        pltpu.VMEM((count, n, rows, tile), jnp.float32),
        pltpu.SemaphoreType.DMA((3,)),
    ]
    if sketch is not None:
        args.append(sketch)
        specs.append(HBM)
        out.append(jax.ShapeDtypeStruct((half // 2, 2 * sketch.shape[0]), jnp.float32))
        scratch.append(pltpu.VMEM(sketch.shape, sketch.dtype))
    return call(
        kernel,
        idx,
        args,
        specs,
        out,
        [whole(o.shape) for o in out],
        "backward",
        (count,),
        (4 * half * hidden * width, 2 * hidden * width + 12 * half * width),
        after,
        scratch,
    )


def fold(idx, keep, got, right, bit, pos, after):
    count, m, rows, tile = keep.shape
    extra = 0 if right is None else RIGHT_ROWS

    def kernel(idx, keep, got, *refs):
        if extra:
            right, msg, rest, total = refs
            total[...] = add_right(right[...], got)
            put_right(total[...], msg)
        else:
            msg, rest = refs
        mine = (idx[0] >> bit) & 1
        for c in range(m // 2):
            away, here = with_bit(c, pos, 1 - mine), with_bit(c, pos, mine)

            @pl.loop(0, rows // BLK)
            def _(b):
                src = rows_at(b * BLK)
                plus = decode_rows(got, rows_at(away * rows + b * BLK), tile, count)
                encode_rows(
                    [keep[t, away, src, :] + plus[t] for t in range(count)],
                    msg,
                    rows_at(c * rows + b * BLK),
                )
                plus = decode_rows(got, rows_at(here * rows + b * BLK), tile, count)
                for t in range(count):
                    rest[t, c, src, :] = keep[t, here, src, :] + plus[t]

    args = [keep, got] + ([right] if extra else [])
    out = [
        jax.ShapeDtypeStruct((m // 2 * rows + extra, got.shape[1]), jnp.bfloat16),
        jax.ShapeDtypeStruct((count, m // 2, rows, tile), jnp.float32),
    ] + ([jax.ShapeDtypeStruct(right.shape, jnp.float32)] if extra else [])
    return call(
        kernel,
        idx,
        args,
        [whole(a.shape) for a in args],
        out,
        [whole(o.shape) for o in out],
        "fold",
        (1,),
        (0, 12 * keep.size),
        after,
    )


def finish(idx, keeps, gots, after):
    count, _, rows, tile = keeps[0].shape
    pieces = len(keeps)

    def kernel(idx, *refs):
        out = refs[-1]
        for p in range(pieces):

            @pl.loop(0, rows // BLK)
            def _(b):
                at = rows_at(b * BLK)
                plus = decode_rows(refs[pieces + p], at, tile, count)
                for t in range(count):
                    lo = (p * count + t) * tile
                    out[at, lo : lo + tile] = (refs[p][t, 0, at, :] + plus[t]).astype(
                        jnp.bfloat16
                    )

    args = list(keeps) + list(gots)
    out = [jax.ShapeDtypeStruct((rows, pieces * count * tile), jnp.bfloat16)]
    (grad,), _ = call(
        kernel,
        idx,
        args,
        [whole(a.shape) for a in args],
        out,
        [whole(out[0].shape)],
        "finish",
        (1,),
        (0, 16 * rows * count * tile),
        after,
    )
    return grad


def gate(idx, arrays, after):
    k = len(arrays)

    def kernel(idx, *refs):
        pass

    out, token = call(
        kernel,
        idx,
        arrays,
        [ANY] * k,
        [jax.ShapeDtypeStruct(a.shape, a.dtype) for a in arrays],
        [ANY] * k,
        "gate",
        (1,),
        (0, 0),
        after,
        aliases={1 + i: i for i in range(k)},
    )
    return list(out), [token]


def last_right(idx, right, got, after):
    def kernel(idx, right, got, out):
        out[...] = add_right(right[...], got)

    out = [jax.ShapeDtypeStruct(right.shape, jnp.float32)]
    specs = [whole(right.shape), whole(got.shape)]
    work = (0, 2 * got.size)
    (total,), token = call(
        kernel, idx, [right, got], specs, out, specs[:1], "last_right", (1,), work, after
    )
    return total, [token]


def forward(idx, chunks, w, sketch, lo, hi, after):
    rows, feats = chunks[0][1].shape
    m = len(chunks)
    tile = pick(w.shape[1], H_TILE)
    hidden = (hi - lo) * tile
    part = m // 2 * rows

    def kernel(idx, *refs):
        w, sk, send, keep, left, x, sems = refs[m:]
        me, core = idx[0], idx[1]

        @pl.when(pl.program_id(0) == 0)
        def _():
            copies = []
            for i, (mask, _) in enumerate(chunks):
                d = me ^ mask
                side = 1 - ((d // m) ^ core)
                to = pl.ds(pl.multiple_of(side * part + ((d % m) >> 1) * rows, BLK), rows)
                copies.append(pltpu.make_async_copy(refs[i], x.at[to], sems.at[i]))
            for c in copies:
                c.start()
            for c in copies:
                c.wait()
            left[...] = contract_last(x[...], sk[...])

        t = jnp.dot(x[...], w[...], preferred_element_type=jnp.float32)
        send[...] = t[:part]
        keep[...] = t[part:]

    out = [jax.ShapeDtypeStruct((part, hidden), jnp.float32)] * 2
    out.append(jax.ShapeDtypeStruct((2 * part, sketch.shape[0]), jnp.float32))
    column = pl.BlockSpec((part, tile), lambda j, s: (0, j))
    return call(
        kernel,
        idx,
        [c[1] for c in chunks] + [w, sketch],
        [ANY] * m + [pl.BlockSpec((feats, tile), lambda j, s: (0, lo + j)), whole(sketch.shape)],
        out,
        [column, column, whole(out[2].shape)],
        "forward",
        (hidden // tile,),
        (4 * part * feats * hidden, 2 * feats * hidden + 8 * part * hidden),
        after,
        [pltpu.VMEM((2 * part, feats), jnp.bfloat16), pltpu.SemaphoreType.DMA((m,))],
    )


def combine(idx, keep, got, lo, total, batch, rows, before, after):
    part, width = keep.shape
    m = part // rows

    def kernel(idx, keep, got, *refs):
        out, x, sems = refs[-3:]
        mine = (idx[0] & 1) ^ batch
        x[...] = (keep[...] + got[...]).astype(jnp.bfloat16)
        copies = []
        for i in range(m):
            to = pl.ds(pl.multiple_of((2 * i + mine) * rows, BLK), rows)
            copies.append(
                pltpu.make_async_copy(
                    x.at[pl.ds(i * rows, rows)], out.at[to, pl.ds(lo, width)], sems.at[i]
                )
            )
        for c in copies:
            c.start()
        for c in copies:
            c.wait()

    (out,), token = call(
        kernel,
        idx,
        [keep, got] + before,
        [whole(keep.shape)] * 2 + [HBM] * len(before),
        [jax.ShapeDtypeStruct((2 * part, total), jnp.bfloat16)],
        [HBM],
        "combine",
        (1,),
        (0, 10 * part * width),
        after,
        [pltpu.VMEM((part, width), jnp.bfloat16), pltpu.SemaphoreType.DMA((m,))],
        aliases={3: 0} if before else None,
    )
    return out, [token]


def sketch_part(idx, lefts, own, oth, rows, after):
    packed, lanes = own.shape
    width = lanes // 2
    half = 2 * packed
    part = half // 2
    examples = half // LEN

    def kernel(idx, first, second, own, oth, out):
        me, core = idx[0], idx[1]
        for side, right in ((0, oth), (1, own)):
            owner = 1 - (side ^ core)
            for e in range(examples):
                total = jnp.zeros((width, width), jnp.float32)
                for i in range(part // rows):
                    if 2 * i * rows // LEN != e:
                        continue
                    block, start = divmod(2 * i * rows, packed)
                    for batch, left in enumerate((first, second)):
                        at = start + ((me & 1) ^ batch) * rows
                        lo = side * part + i * rows
                        both = right[pl.ds(pl.multiple_of(at, BLK), rows), :]
                        total += lax.dot_general(
                            left[lo : lo + rows, :],
                            both[:, block * width : (block + 1) * width],
                            (((0,), (0,)), ((), ())),
                            precision=lax.Precision.HIGHEST,
                            preferred_element_type=jnp.float32,
                        )
                out[owner * examples + e] = total

    args = [*lefts, own, oth]
    out = [jax.ShapeDtypeStruct((2 * examples, width, width), jnp.float32)]
    (sketch,), token = call(
        kernel,
        idx,
        args,
        [whole(a.shape) for a in args],
        out,
        [whole(out[0].shape)],
        "sketch_part",
        (1,),
        (0, 16 * half * width),
        after,
    )
    return sketch, [token]


def body(inputs, cotangent, weight, in_sketch, out_sketch):
    n = lax.axis_size("outp")
    bits = n.bit_length() - 1
    rows, feats = inputs.shape
    hidden = weight.shape[1]
    idx = jnp.stack([lax.axis_index("outp"), lax.axis_index("inp")]).astype(jnp.int32)

    def partner(x, bit):
        return lax.ppermute(x, "outp", [(d, d ^ (1 << bit)) for d in range(n)])

    def swap(x):
        return lax.ppermute(x, "inp", [(0, 1), (1, 0)])

    chunks = {0: inputs}
    evens = range(2, n, 2)

    def wave(masks):
        for mask in masks:
            bit = (mask & -mask).bit_length() - 1
            chunks[mask] = partner(chunks[mask ^ (1 << bit)], bit)

    def along_z(k):
        return [m for m in reversed(evens) if m.bit_count() == k]

    def hold(masks, after):
        held, token = gate(idx, [chunks[m] for m in masks], after)
        chunks.update(zip(masks, held))
        return token

    grad_other = swap(cotangent)
    wave(along_z(1) + [1])

    orders = [list(range(bits)), [1, 0] + list(range(2, bits))]
    tile = pick(feats // PIECES, F_TILE)
    count = feats // PIECES // tile
    msgs, keeps = [], []
    token = []
    for p in range(PIECES):
        outs, t = backward(
            idx,
            cotangent,
            grad_other,
            weight,
            out_sketch if p == 0 else None,
            count,
            tile,
            p * count,
            rows,
            orders[p][0],
            token,
        )
        token = [t]
        msgs.append(partner(outs[0], orders[p][0]))
        keeps.append(outs[1])
        if p == 0:
            right = outs[2]
        if p == 0:
            token = hold([1] + along_z(1), token)
            wave(along_z(2))
    for k in range(2, bits - 1):
        token = hold(along_z(k), token)
        wave(along_z(k + 1))
    token = hold(list(evens), token)
    wave([m + 1 for m in evens])

    rights = [right] + [None] * (PIECES - 1)

    def folded(p, step, after):
        done, bit = orders[p][:step], orders[p][step]
        pos = sum(1 for k in range(bit) if k not in done)
        outs, t = fold(idx, keeps[p], msgs[p], rights[p], bit, pos, after)
        msgs[p], keeps[p] = partner(outs[0], bit), outs[1]
        if p == 0:
            rights[p] = outs[2]
        return [t]

    tiles = hidden // pick(hidden, H_TILE)

    def batch_forward(batch, lo, hi, after):
        parts = [(m, chunks[m]) for m in range(n) if m & 1 == batch]
        outs, t = forward(idx, parts, weight, in_sketch, lo, hi, after)
        start = lo * (hidden // tiles)
        return (outs[1], swap(outs[0]), start, hidden, batch, rows), outs[2], [t]

    cut = -(-tiles // 2)
    token = folded(0, 1, token)
    first, left1, token = batch_forward(0, 0, tiles, token)
    token = folded(1, 1, token)
    token = folded(0, 2, token)
    token = hold([m + 1 for m in evens], token)
    second, left2, token = batch_forward(1, 0, cut, token)
    token = folded(1, 2, token)
    third, _, token = batch_forward(1, cut, tiles, token)
    for step in range(3, bits):
        for p in range(PIECES):
            token = folded(p, step, token)
    outputs, token = combine(idx, *first, [], token)
    right, token = last_right(idx, rights[0], msgs[0], token)
    right_got = swap(right)
    outputs, token = combine(idx, *second, [outputs], token)
    outputs, token = combine(idx, *third, [outputs], token)
    part, token = sketch_part(idx, [left1, left2], right, right_got, rows, token)
    input_grad = finish(idx, keeps, msgs, token)
    part = (part + swap(part)) * (1.0 / LEN**0.5)
    sketches = part.reshape(part.shape[0], -1)
    return (outputs, input_grad, sketches)


def solution(mesh):
    placed = (
        P(("groups", "outp"), "inp"),
        P(("groups", "inp"), "outp"),
        P("inp", "outp"),
        P(None, "inp"),
        P(None, "outp"),
    )
    return jax.shard_map(
        body,
        mesh=mesh,
        in_specs=placed,
        out_specs=(P(("groups", "inp"), "outp"), P(("groups", "outp"), "inp"), P("groups", None)),
        check_vma=False,
    )
```

```python
import jax
import jax.numpy as jnp
from jax import lax
from jax.experimental import pallas as pl
from jax.experimental.pallas import tpu as pltpu
from jax.sharding import PartitionSpec as P

LEN = 128
LANES = 128
BLK = 16
LN2 = 0.6931471805599453
SPAN = 248.0
SHIFT = 124.0
PIECES = 2
F_TILE = 512
H_TILE = 512
VMEM_MIB = {"backward": 32, "forward": 24}
MIB = 1 << 20
RIGHT_ROWS = 32
TIMES = {"gate": 0, "backward_0": 19 * 10**9, "backward_4": 10 * 10**9, "forward": 1 << 34, "fold": 0, "combine": 1 << 34, "sketch_part": 1 << 34}
ANY = pl.BlockSpec(memory_space=pl.ANY)
HBM = pl.BlockSpec(memory_space=pltpu.HBM)


def pick(extent, cap):
    best = LANES
    for t in range(LANES, min(cap, extent) + 1, LANES):
        if extent % t == 0:
            best = t
    return best


def contract_last(a, b):
    return lax.dot_general(a, b, (((1,), (1,)), ((), ())), preferred_element_type=jnp.float32)


def whole(shape):
    return pl.BlockSpec(shape, lambda *_: (0,) * len(shape))


def call(
    kernel, idx, args, specs, out_shape, out_specs, name, grid, work, after, scratch=(), aliases=None
):
    token = jax.ShapeDtypeStruct((8, LANES), jnp.float32)
    n_args, n_after, n_out = len(args), len(after), len(out_shape)

    def with_token(idx, *refs):
        ins = refs[:n_args]
        outs = refs[n_args + n_after :]
        outs[n_out][...] = jnp.zeros((8, LANES), jnp.float32)
        kernel(idx, *ins, *outs[:n_out], *outs[n_out + 1 :])

    out = pl.pallas_call(
        with_token,
        out_shape=list(out_shape) + [token],
        grid_spec=pltpu.PrefetchScalarGridSpec(
            num_scalar_prefetch=1,
            grid=grid,
            in_specs=list(specs) + [ANY] * n_after,
            out_specs=list(out_specs) + [whole(token.shape)],
            scratch_shapes=list(scratch),
        ),
        compiler_params=pltpu.CompilerParams(vmem_limit_bytes=VMEM_MIB.get(name.split("_")[0], 14) * MIB),
        cost_estimate=pl.CostEstimate(
            flops=TIMES.get(name, work[0]), bytes_accessed=work[1], transcendentals=0
        ),
        input_output_aliases=aliases or {},
        name=name,
    )(idx, *args, *after)
    return out[:-1], out[-1]


def encode_rows(tiles, msg, at):
    top = jnp.abs(tiles[0])
    for v in tiles[1:]:
        top = jnp.maximum(top, jnp.abs(v))
    top = jnp.max(top, axis=1, keepdims=True)
    scale = jnp.maximum(top * 1.004, 2.0**-110).astype(jnp.bfloat16).astype(jnp.float32)
    gain = SPAN / scale
    col = 0
    for v in tiles:
        w = jnp.exp2(jnp.abs(v) * gain - SHIFT)
        msg[at, col : col + v.shape[1]] = jnp.where(v < 0, -w, w).astype(jnp.bfloat16)
        col += v.shape[1]
    msg[at, col : col + LANES] = jnp.broadcast_to(scale, (BLK, LANES)).astype(jnp.bfloat16)


def decode_rows(msg, at, tile, count):
    scale = msg[at, tile * count : tile * count + LANES].astype(jnp.float32)[:, :1]
    scale = scale * (1.0 / (SPAN * LN2))
    out = []
    for t in range(count):
        w = msg[at, t * tile : (t + 1) * tile].astype(jnp.float32)
        a = (lax.log(jnp.maximum(jnp.abs(w), 2.0**-SHIFT)) + SHIFT * LN2) * scale
        out.append(jnp.where(w < 0, -a, a))
    return out


def put_right(value, msg):
    base = msg.shape[0] - RIGHT_ROWS
    for q in range(value.shape[0] // RIGHT_ROWS):
        left_over = value[q * RIGHT_ROWS : (q + 1) * RIGHT_ROWS, :]
        for k in range(3):
            part = left_over.astype(jnp.bfloat16)
            lo = (3 * q + k) * LANES
            msg[base:, lo : lo + LANES] = part
            left_over = left_over - part.astype(jnp.float32)


def add_right(value, msg):
    base = msg.shape[0] - RIGHT_ROWS
    out = []
    for q in range(value.shape[0] // RIGHT_ROWS):
        lo = 3 * q * LANES
        parts = [
            msg[base:, lo + k * LANES : lo + (k + 1) * LANES].astype(jnp.float32) for k in range(3)
        ]
        got = parts[0] + (parts[1] + parts[2])
        out.append(value[q * RIGHT_ROWS : (q + 1) * RIGHT_ROWS, :] + got)
    return jnp.concatenate(out, axis=0)


def with_bit(c, pos, value):
    low = c & ((1 << pos) - 1)
    return ((c >> pos) << (pos + 1)) + low + value * (1 << pos)


def rows_at(start):
    return pl.ds(pl.multiple_of(start, BLK), BLK)


def backward(idx, own, oth, w, sketch, count, tile, first, rows, bit, after):
    half, hidden = own.shape
    n = 2 * half // rows
    width = count * tile

    def kernel(idx, own, oth, w, *rest):
        if sketch is None:
            msg, keep, x, total, sems = rest
        else:
            sk, msg, keep, right, x, total, sems, sk_here = rest
        j = pl.program_id(0)
        me, core = idx[0], idx[1]

        @pl.when(j == 0)
        def _():
            a = pltpu.make_async_copy(own, x.at[core], sems.at[0])
            b = pltpu.make_async_copy(oth, x.at[1 - core], sems.at[1])
            a.start()
            b.start()
            if sketch is not None:
                c = pltpu.make_async_copy(sk, sk_here, sems.at[2])
                c.start()
                c.wait()
            a.wait()
            b.wait()
            if sketch is not None:
                low, high = jnp.zeros_like(sk_here[...]), sk_here[...]
                first_block = jnp.concatenate([high, low], axis=0)
                second_block = jnp.concatenate([low, high], axis=0)
                right[...] = contract_last(x[core, : half // 2, :], first_block) + contract_last(
                    x[core, half // 2 :, :], second_block
                )
                put_right(right[...], msg)

        xs = x[...].reshape(2 * half, hidden)
        total[j] = contract_last(xs, w[...]).reshape(n, rows, tile)

        @pl.when(j == count - 1)
        def _():
            mine = (me >> bit) & 1
            for c in range(n // 2):
                away, here = with_bit(c, bit, 1 - mine), with_bit(c, bit, mine)

                @pl.loop(0, rows // BLK)
                def _(b):
                    src = rows_at(b * BLK)
                    encode_rows(
                        [total[t, away, src, :] for t in range(count)],
                        msg,
                        rows_at(c * rows + b * BLK),
                    )
                    for t in range(count):
                        keep[t, c, src, :] = total[t, here, src, :]

    extra = 0 if sketch is None else RIGHT_ROWS
    out = [
        jax.ShapeDtypeStruct((n // 2 * rows + extra, width + LANES), jnp.bfloat16),
        jax.ShapeDtypeStruct((count, n // 2, rows, tile), jnp.float32),
    ]
    args = [own, oth, w]
    specs = [HBM, ANY, pl.BlockSpec((tile, hidden), lambda j, s: (first + j, 0))]
    scratch = [
        pltpu.VMEM((2, half, hidden), jnp.bfloat16),
        pltpu.VMEM((count, n, rows, tile), jnp.float32),
        pltpu.SemaphoreType.DMA((3,)),
    ]
    if sketch is not None:
        args.append(sketch)
        specs.append(HBM)
        out.append(jax.ShapeDtypeStruct((half // 2, 2 * sketch.shape[0]), jnp.float32))
        scratch.append(pltpu.VMEM(sketch.shape, sketch.dtype))
    return call(
        kernel,
        idx,
        args,
        specs,
        out,
        [whole(o.shape) for o in out],
        f"backward_{first}",
        (count,),
        (4 * half * hidden * width, 2 * hidden * width + 12 * half * width),
        after,
        scratch,
    )


def fold(idx, keep, got, right, bit, pos, after):
    count, m, rows, tile = keep.shape
    extra = 0 if right is None else RIGHT_ROWS

    def kernel(idx, keep, got, *refs):
        if extra:
            right, msg, rest, total = refs
            total[...] = add_right(right[...], got)
            put_right(total[...], msg)
        else:
            msg, rest = refs
        mine = (idx[0] >> bit) & 1
        for c in range(m // 2):
            away, here = with_bit(c, pos, 1 - mine), with_bit(c, pos, mine)

            @pl.loop(0, rows // BLK)
            def _(b):
                src = rows_at(b * BLK)
                plus = decode_rows(got, rows_at(away * rows + b * BLK), tile, count)
                encode_rows(
                    [keep[t, away, src, :] + plus[t] for t in range(count)],
                    msg,
                    rows_at(c * rows + b * BLK),
                )
                plus = decode_rows(got, rows_at(here * rows + b * BLK), tile, count)
                for t in range(count):
                    rest[t, c, src, :] = keep[t, here, src, :] + plus[t]

    args = [keep, got] + ([right] if extra else [])
    out = [
        jax.ShapeDtypeStruct((m // 2 * rows + extra, got.shape[1]), jnp.bfloat16),
        jax.ShapeDtypeStruct((count, m // 2, rows, tile), jnp.float32),
    ] + ([jax.ShapeDtypeStruct(right.shape, jnp.float32)] if extra else [])
    return call(
        kernel,
        idx,
        args,
        [whole(a.shape) for a in args],
        out,
        [whole(o.shape) for o in out],
        "fold",
        (1,),
        (0, 12 * keep.size),
        after,
    )


def finish(idx, keeps, gots, after):
    count, _, rows, tile = keeps[0].shape
    pieces = len(keeps)

    def kernel(idx, *refs):
        out = refs[-1]
        for p in range(pieces):

            @pl.loop(0, rows // BLK)
            def _(b):
                at = rows_at(b * BLK)
                plus = decode_rows(refs[pieces + p], at, tile, count)
                for t in range(count):
                    lo = (p * count + t) * tile
                    out[at, lo : lo + tile] = (refs[p][t, 0, at, :] + plus[t]).astype(
                        jnp.bfloat16
                    )

    args = list(keeps) + list(gots)
    out = [jax.ShapeDtypeStruct((rows, pieces * count * tile), jnp.bfloat16)]
    (grad,), _ = call(
        kernel,
        idx,
        args,
        [whole(a.shape) for a in args],
        out,
        [whole(out[0].shape)],
        "finish",
        (1,),
        (0, 16 * rows * count * tile),
        after,
    )
    return grad


def gate(idx, arrays, after):
    k = len(arrays)

    def kernel(idx, *refs):
        pass

    out, token = call(
        kernel,
        idx,
        arrays,
        [ANY] * k,
        [jax.ShapeDtypeStruct(a.shape, a.dtype) for a in arrays],
        [ANY] * k,
        "gate",
        (1,),
        (0, 0),
        after,
        aliases={1 + i: i for i in range(k)},
    )
    return list(out), [token]


def last_right(idx, right, got, after):
    def kernel(idx, right, got, out):
        out[...] = add_right(right[...], got)

    out = [jax.ShapeDtypeStruct(right.shape, jnp.float32)]
    specs = [whole(right.shape), whole(got.shape)]
    work = (0, 2 * got.size)
    (total,), token = call(
        kernel, idx, [right, got], specs, out, specs[:1], "last_right", (1,), work, after
    )
    return total, [token]


def forward(idx, chunks, w, sketch, lo, hi, after):
    rows, feats = chunks[0][1].shape
    m = len(chunks)
    tile = pick(w.shape[1], H_TILE)
    hidden = (hi - lo) * tile
    part = m // 2 * rows

    def kernel(idx, *refs):
        w, sk, send, keep, left, x, sems = refs[m:]
        me, core = idx[0], idx[1]

        @pl.when(pl.program_id(0) == 0)
        def _():
            copies = []
            for i, (mask, _) in enumerate(chunks):
                d = me ^ mask
                side = 1 - ((d // m) ^ core)
                to = pl.ds(pl.multiple_of(side * part + ((d % m) >> 1) * rows, BLK), rows)
                copies.append(pltpu.make_async_copy(refs[i], x.at[to], sems.at[i]))
            for c in copies:
                c.start()
            for c in copies:
                c.wait()
            left[...] = contract_last(x[...], sk[...])

        t = jnp.dot(x[...], w[...], preferred_element_type=jnp.float32)
        send[...] = t[:part]
        keep[...] = t[part:]

    out = [jax.ShapeDtypeStruct((part, hidden), jnp.float32)] * 2
    out.append(jax.ShapeDtypeStruct((2 * part, sketch.shape[0]), jnp.float32))
    column = pl.BlockSpec((part, tile), lambda j, s: (0, j))
    return call(
        kernel,
        idx,
        [c[1] for c in chunks] + [w, sketch],
        [ANY] * m + [pl.BlockSpec((feats, tile), lambda j, s: (0, lo + j)), whole(sketch.shape)],
        out,
        [column, column, whole(out[2].shape)],
        "forward",
        (hidden // tile,),
        (4 * part * feats * hidden, 2 * feats * hidden + 8 * part * hidden),
        after,
        [pltpu.VMEM((2 * part, feats), jnp.bfloat16), pltpu.SemaphoreType.DMA((m,))],
    )


def combine(idx, keep, got, lo, total, batch, rows, before, after):
    part, width = keep.shape
    m = part // rows

    def kernel(idx, keep, got, *refs):
        out, x, sems = refs[-3:]
        mine = (idx[0] & 1) ^ batch
        x[...] = (keep[...] + got[...]).astype(jnp.bfloat16)
        copies = []
        for i in range(m):
            to = pl.ds(pl.multiple_of((2 * i + mine) * rows, BLK), rows)
            copies.append(
                pltpu.make_async_copy(
                    x.at[pl.ds(i * rows, rows)], out.at[to, pl.ds(lo, width)], sems.at[i]
                )
            )
        for c in copies:
            c.start()
        for c in copies:
            c.wait()

    (out,), token = call(
        kernel,
        idx,
        [keep, got] + before,
        [whole(keep.shape)] * 2 + [HBM] * len(before),
        [jax.ShapeDtypeStruct((2 * part, total), jnp.bfloat16)],
        [HBM],
        "combine",
        (1,),
        (0, 10 * part * width),
        after,
        [pltpu.VMEM((part, width), jnp.bfloat16), pltpu.SemaphoreType.DMA((m,))],
        aliases={3: 0} if before else None,
    )
    return out, [token]


def sketch_part(idx, lefts, own, oth, rows, after):
    packed, lanes = own.shape
    width = lanes // 2
    half = 2 * packed
    part = half // 2
    examples = half // LEN

    def kernel(idx, first, second, own, oth, out):
        me, core = idx[0], idx[1]
        for side, right in ((0, oth), (1, own)):
            owner = 1 - (side ^ core)
            for e in range(examples):
                total = jnp.zeros((width, width), jnp.float32)
                for i in range(part // rows):
                    if 2 * i * rows // LEN != e:
                        continue
                    block, start = divmod(2 * i * rows, packed)
                    for batch, left in enumerate((first, second)):
                        at = start + ((me & 1) ^ batch) * rows
                        lo = side * part + i * rows
                        both = right[pl.ds(pl.multiple_of(at, BLK), rows), :]
                        total += lax.dot_general(
                            left[lo : lo + rows, :],
                            both[:, block * width : (block + 1) * width],
                            (((0,), (0,)), ((), ())),
                            precision=lax.Precision.HIGHEST,
                            preferred_element_type=jnp.float32,
                        )
                out[owner * examples + e] = total

    args = [*lefts, own, oth]
    out = [jax.ShapeDtypeStruct((2 * examples, width, width), jnp.float32)]
    (sketch,), token = call(
        kernel,
        idx,
        args,
        [whole(a.shape) for a in args],
        out,
        [whole(out[0].shape)],
        "sketch_part",
        (1,),
        (0, 16 * half * width),
        after,
    )
    return sketch, [token]


def body(inputs, cotangent, weight, in_sketch, out_sketch):
    n = lax.axis_size("outp")
    bits = n.bit_length() - 1
    rows, feats = inputs.shape
    hidden = weight.shape[1]
    idx = jnp.stack([lax.axis_index("outp"), lax.axis_index("inp")]).astype(jnp.int32)

    def partner(x, bit):
        return lax.ppermute(x, "outp", [(d, d ^ (1 << bit)) for d in range(n)])

    def swap(x):
        return lax.ppermute(x, "inp", [(0, 1), (1, 0)])

    chunks = {0: inputs}
    evens = range(2, n, 2)

    def wave(masks):
        for mask in masks:
            bit = (mask & -mask).bit_length() - 1
            chunks[mask] = partner(chunks[mask ^ (1 << bit)], bit)

    def along_z(k):
        return [m for m in reversed(evens) if m.bit_count() == k]

    def hold(masks, after):
        held, token = gate(idx, [chunks[m] for m in masks], after)
        chunks.update(zip(masks, held))
        return token

    grad_other = swap(cotangent)
    wave(along_z(1) + [1])

    orders = [list(range(bits)), [1, 0] + list(range(2, bits))]
    tile = pick(feats // PIECES, F_TILE)
    count = feats // PIECES // tile
    msgs, keeps = [], []
    token = []
    for p in range(PIECES):
        outs, t = backward(
            idx,
            cotangent,
            grad_other,
            weight,
            out_sketch if p == 0 else None,
            count,
            tile,
            p * count,
            rows,
            orders[p][0],
            token,
        )
        token = [t]
        msgs.append(partner(outs[0], orders[p][0]))
        keeps.append(outs[1])
        if p == 0:
            right = outs[2]
        if p == 0:
            token = hold([1] + along_z(1), token)
            wave(along_z(2))
    for k in range(2, bits - 1):
        token = hold(along_z(k), token)
        wave(along_z(k + 1))
    token = hold(list(evens), token)
    wave([m + 1 for m in evens])

    rights = [right] + [None] * (PIECES - 1)

    def folded(p, step, after):
        done, bit = orders[p][:step], orders[p][step]
        pos = sum(1 for k in range(bit) if k not in done)
        outs, t = fold(idx, keeps[p], msgs[p], rights[p], bit, pos, after)
        msgs[p], keeps[p] = partner(outs[0], bit), outs[1]
        if p == 0:
            rights[p] = outs[2]
        return [t]

    tiles = hidden // pick(hidden, H_TILE)

    def batch_forward(batch, lo, hi, after):
        parts = [(m, chunks[m]) for m in range(n) if m & 1 == batch]
        outs, t = forward(idx, parts, weight, in_sketch, lo, hi, after)
        start = lo * (hidden // tiles)
        return (outs[1], swap(outs[0]), start, hidden, batch, rows), outs[2], [t]

    cut = -(-tiles // 2)
    token = folded(0, 1, token)
    first, left1, token = batch_forward(0, 0, tiles, token)
    token = folded(1, 1, token)
    token = folded(0, 2, token)
    token = hold([m + 1 for m in evens], token)
    second, left2, token = batch_forward(1, 0, cut, token)
    token = folded(1, 2, token)
    outputs, token = combine(idx, *first, [], token)
    third, _, token = batch_forward(1, cut, tiles, token)
    for step in range(3, bits):
        for p in range(PIECES):
            token = folded(p, step, token)
    right, token = last_right(idx, rights[0], msgs[0], token)
    right_got = swap(right)
    outputs, token = combine(idx, *second, [outputs], token)
    outputs, token = combine(idx, *third, [outputs], token)
    part, token = sketch_part(idx, [left1, left2], right, right_got, rows, token)
    input_grad = finish(idx, keeps, msgs, token)
    part = (part + swap(part)) * (1.0 / LEN**0.5)
    sketches = part.reshape(part.shape[0], -1)
    return (outputs, input_grad, sketches)


def solution(mesh):
    placed = (
        P(("groups", "outp"), "inp"),
        P(("groups", "inp"), "outp"),
        P("inp", "outp"),
        P(None, "inp"),
        P(None, "outp"),
    )
    return jax.shard_map(
        body,
        mesh=mesh,
        in_specs=placed,
        out_specs=(P(("groups", "inp"), "outp"), P(("groups", "outp"), "inp"), P("groups", None)),
        check_vma=False,
    )
```

```python
import jax
import jax.numpy as jnp
from jax import lax
from jax.experimental import pallas as pl
from jax.experimental.pallas import tpu as pltpu
from jax.sharding import PartitionSpec as P

LEN = 128
LANES = 128
BLK = 16
LN2 = 0.6931471805599453
SPAN = 248.0
SHIFT = 124.0
PIECES = 2
F_TILE = 512
H_TILE = 512
VMEM_MIB = {"backward": 32, "forward": 24}
MIB = 1 << 20
RIGHT_ROWS = 16
RIGHT_PARTS = 2
TIMES = {"gate": 0, "backward_0": 19 * 10**9, "backward_4": 10 * 10**9, "forward": 1 << 34, "fold": 0, "combine": 1 << 34, "sketch_part": 1 << 34}
ANY = pl.BlockSpec(memory_space=pl.ANY)
HBM = pl.BlockSpec(memory_space=pltpu.HBM)


def pick(extent, cap):
    best = LANES
    for t in range(LANES, min(cap, extent) + 1, LANES):
        if extent % t == 0:
            best = t
    return best


def contract_last(a, b):
    return lax.dot_general(a, b, (((1,), (1,)), ((), ())), preferred_element_type=jnp.float32)


def whole(shape):
    return pl.BlockSpec(shape, lambda *_: (0,) * len(shape))


def call(
    kernel, idx, args, specs, out_shape, out_specs, name, grid, work, after, scratch=(), aliases=None
):
    token = jax.ShapeDtypeStruct((8, LANES), jnp.float32)
    n_args, n_after, n_out = len(args), len(after), len(out_shape)

    def with_token(idx, *refs):
        ins = refs[:n_args]
        outs = refs[n_args + n_after :]
        outs[n_out][...] = jnp.zeros((8, LANES), jnp.float32)
        kernel(idx, *ins, *outs[:n_out], *outs[n_out + 1 :])

    out = pl.pallas_call(
        with_token,
        out_shape=list(out_shape) + [token],
        grid_spec=pltpu.PrefetchScalarGridSpec(
            num_scalar_prefetch=1,
            grid=grid,
            in_specs=list(specs) + [ANY] * n_after,
            out_specs=list(out_specs) + [whole(token.shape)],
            scratch_shapes=list(scratch),
        ),
        compiler_params=pltpu.CompilerParams(vmem_limit_bytes=VMEM_MIB.get(name.split("_")[0], 14) * MIB),
        cost_estimate=pl.CostEstimate(
            flops=TIMES.get(name, work[0]), bytes_accessed=work[1], transcendentals=0
        ),
        input_output_aliases=aliases or {},
        name=name,
    )(idx, *args, *after)
    return out[:-1], out[-1]


def encode_rows(tiles, msg, at):
    top = jnp.abs(tiles[0])
    for v in tiles[1:]:
        top = jnp.maximum(top, jnp.abs(v))
    top = jnp.max(top, axis=1, keepdims=True)
    scale = jnp.maximum(top * 1.004, 2.0**-110).astype(jnp.bfloat16).astype(jnp.float32)
    gain = SPAN / scale
    col = 0
    for v in tiles:
        w = jnp.exp2(jnp.abs(v) * gain - SHIFT)
        msg[at, col : col + v.shape[1]] = jnp.where(v < 0, -w, w).astype(jnp.bfloat16)
        col += v.shape[1]
    msg[at, col : col + LANES] = jnp.broadcast_to(scale, (BLK, LANES)).astype(jnp.bfloat16)


def decode_rows(msg, at, tile, count):
    scale = msg[at, tile * count : tile * count + LANES].astype(jnp.float32)[:, :1]
    scale = scale * (1.0 / (SPAN * LN2))
    out = []
    for t in range(count):
        w = msg[at, t * tile : (t + 1) * tile].astype(jnp.float32)
        a = (lax.log(jnp.maximum(jnp.abs(w), 2.0**-SHIFT)) + SHIFT * LN2) * scale
        out.append(jnp.where(w < 0, -a, a))
    return out


def put_right(value, msg):
    base = msg.shape[0] - RIGHT_ROWS
    for q in range(value.shape[0] // RIGHT_ROWS):
        left_over = value[q * RIGHT_ROWS : (q + 1) * RIGHT_ROWS, :]
        for k in range(RIGHT_PARTS):
            part = left_over.astype(jnp.bfloat16)
            lo = (RIGHT_PARTS * q + k) * LANES
            msg[base:, lo : lo + LANES] = part
            left_over = left_over - part.astype(jnp.float32)


def add_right(value, msg):
    base = msg.shape[0] - RIGHT_ROWS
    out = []
    for q in range(value.shape[0] // RIGHT_ROWS):
        lo = RIGHT_PARTS * q * LANES
        parts = [
            msg[base:, lo + k * LANES : lo + (k + 1) * LANES].astype(jnp.float32)
            for k in range(RIGHT_PARTS)
        ]
        got = sum(parts)
        out.append(value[q * RIGHT_ROWS : (q + 1) * RIGHT_ROWS, :] + got)
    return jnp.concatenate(out, axis=0)


def with_bit(c, pos, value):
    low = c & ((1 << pos) - 1)
    return ((c >> pos) << (pos + 1)) + low + value * (1 << pos)


def rows_at(start):
    return pl.ds(pl.multiple_of(start, BLK), BLK)


def backward(idx, own, oth, w, sketch, count, tile, first, rows, bit, after):
    half, hidden = own.shape
    n = 2 * half // rows
    width = count * tile

    def kernel(idx, own, oth, w, *rest):
        if sketch is None:
            msg, keep, x, total, sems = rest
        else:
            sk, msg, keep, right, x, total, sems, sk_here = rest
        j = pl.program_id(0)
        me, core = idx[0], idx[1]

        @pl.when(j == 0)
        def _():
            a = pltpu.make_async_copy(own, x.at[core], sems.at[0])
            b = pltpu.make_async_copy(oth, x.at[1 - core], sems.at[1])
            a.start()
            b.start()
            if sketch is not None:
                c = pltpu.make_async_copy(sk, sk_here, sems.at[2])
                c.start()
                c.wait()
            a.wait()
            b.wait()
            if sketch is not None:
                low, high = jnp.zeros_like(sk_here[...]), sk_here[...]
                first_block = jnp.concatenate([high, low], axis=0)
                second_block = jnp.concatenate([low, high], axis=0)
                right[...] = contract_last(x[core, : half // 2, :], first_block) + contract_last(
                    x[core, half // 2 :, :], second_block
                )
                put_right(right[...], msg)

        xs = x[...].reshape(2 * half, hidden)
        total[j] = contract_last(xs, w[...]).reshape(n, rows, tile)

        @pl.when(j == count - 1)
        def _():
            mine = (me >> bit) & 1
            for c in range(n // 2):
                away, here = with_bit(c, bit, 1 - mine), with_bit(c, bit, mine)

                @pl.loop(0, rows // BLK)
                def _(b):
                    src = rows_at(b * BLK)
                    encode_rows(
                        [total[t, away, src, :] for t in range(count)],
                        msg,
                        rows_at(c * rows + b * BLK),
                    )
                    for t in range(count):
                        keep[t, c, src, :] = total[t, here, src, :]

    extra = 0 if sketch is None else RIGHT_ROWS
    out = [
        jax.ShapeDtypeStruct((n // 2 * rows + extra, width + LANES), jnp.bfloat16),
        jax.ShapeDtypeStruct((count, n // 2, rows, tile), jnp.float32),
    ]
    args = [own, oth, w]
    specs = [HBM, ANY, pl.BlockSpec((tile, hidden), lambda j, s: (first + j, 0))]
    scratch = [
        pltpu.VMEM((2, half, hidden), jnp.bfloat16),
        pltpu.VMEM((count, n, rows, tile), jnp.float32),
        pltpu.SemaphoreType.DMA((3,)),
    ]
    if sketch is not None:
        args.append(sketch)
        specs.append(HBM)
        out.append(jax.ShapeDtypeStruct((half // 2, 2 * sketch.shape[0]), jnp.float32))
        scratch.append(pltpu.VMEM(sketch.shape, sketch.dtype))
    return call(
        kernel,
        idx,
        args,
        specs,
        out,
        [whole(o.shape) for o in out],
        f"backward_{first}",
        (count,),
        (4 * half * hidden * width, 2 * hidden * width + 12 * half * width),
        after,
        scratch,
    )


def fold(idx, keep, got, right, bit, pos, after):
    count, m, rows, tile = keep.shape
    extra = 0 if right is None else RIGHT_ROWS

    def kernel(idx, keep, got, *refs):
        if extra:
            right, msg, rest, total = refs
            total[...] = add_right(right[...], got)
            put_right(total[...], msg)
        else:
            msg, rest = refs
        mine = (idx[0] >> bit) & 1
        for c in range(m // 2):
            away, here = with_bit(c, pos, 1 - mine), with_bit(c, pos, mine)

            @pl.loop(0, rows // BLK)
            def _(b):
                src = rows_at(b * BLK)
                plus = decode_rows(got, rows_at(away * rows + b * BLK), tile, count)
                encode_rows(
                    [keep[t, away, src, :] + plus[t] for t in range(count)],
                    msg,
                    rows_at(c * rows + b * BLK),
                )
                plus = decode_rows(got, rows_at(here * rows + b * BLK), tile, count)
                for t in range(count):
                    rest[t, c, src, :] = keep[t, here, src, :] + plus[t]

    args = [keep, got] + ([right] if extra else [])
    out = [
        jax.ShapeDtypeStruct((m // 2 * rows + extra, got.shape[1]), jnp.bfloat16),
        jax.ShapeDtypeStruct((count, m // 2, rows, tile), jnp.float32),
    ] + ([jax.ShapeDtypeStruct(right.shape, jnp.float32)] if extra else [])
    return call(
        kernel,
        idx,
        args,
        [whole(a.shape) for a in args],
        out,
        [whole(o.shape) for o in out],
        "fold",
        (1,),
        (0, 12 * keep.size),
        after,
    )


def finish(idx, keeps, gots, after):
    count, _, rows, tile = keeps[0].shape
    pieces = len(keeps)

    def kernel(idx, *refs):
        out = refs[-1]
        for p in range(pieces):

            @pl.loop(0, rows // BLK)
            def _(b):
                at = rows_at(b * BLK)
                plus = decode_rows(refs[pieces + p], at, tile, count)
                for t in range(count):
                    lo = (p * count + t) * tile
                    out[at, lo : lo + tile] = (refs[p][t, 0, at, :] + plus[t]).astype(
                        jnp.bfloat16
                    )

    args = list(keeps) + list(gots)
    out = [jax.ShapeDtypeStruct((rows, pieces * count * tile), jnp.bfloat16)]
    (grad,), _ = call(
        kernel,
        idx,
        args,
        [whole(a.shape) for a in args],
        out,
        [whole(out[0].shape)],
        "finish",
        (1,),
        (0, 16 * rows * count * tile),
        after,
    )
    return grad


def gate(idx, arrays, after):
    k = len(arrays)

    def kernel(idx, *refs):
        pass

    out, token = call(
        kernel,
        idx,
        arrays,
        [ANY] * k,
        [jax.ShapeDtypeStruct(a.shape, a.dtype) for a in arrays],
        [ANY] * k,
        "gate",
        (1,),
        (0, 0),
        after,
        aliases={1 + i: i for i in range(k)},
    )
    return list(out), [token]


def join(idx, arrays, after):
    rows, width = arrays[0].shape
    k = len(arrays)

    def kernel(idx, *refs):
        out, sems = refs[-2:]
        copies = [
            pltpu.make_async_copy(refs[i], out.at[pl.ds(i * rows, rows)], sems.at[i])
            for i in range(k)
        ]
        for c in copies:
            c.start()
        for c in copies:
            c.wait()

    (out,), token = call(
        kernel,
        idx,
        arrays,
        [ANY] * k,
        [jax.ShapeDtypeStruct((k * rows, width), arrays[0].dtype)],
        [ANY],
        "join",
        (1,),
        (0, 0),
        after,
        [pltpu.SemaphoreType.DMA((k,))],
    )
    return out, [token]


def last_right(idx, right, got, after):
    def kernel(idx, right, got, out):
        out[...] = add_right(right[...], got)

    out = [jax.ShapeDtypeStruct(right.shape, jnp.float32)]
    specs = [whole(right.shape), whole(got.shape)]
    work = (0, 2 * got.size)
    (total,), token = call(
        kernel, idx, [right, got], specs, out, specs[:1], "last_right", (1,), work, after
    )
    return total, [token]


def forward(idx, chunks, rows, w, sketch, lo, hi, after):
    feats = w.shape[0]
    m = len(chunks)
    tile = pick(w.shape[1], H_TILE)
    hidden = (hi - lo) * tile
    part = m // 2 * rows

    def kernel(idx, *refs):
        w, sk, send, keep, left, x, sems = refs[m:]
        me, core = idx[0], idx[1]

        @pl.when(pl.program_id(0) == 0)
        def _():
            copies = []
            for i, (mask, _, block) in enumerate(chunks):
                d = me ^ mask
                side = 1 - ((d // m) ^ core)
                to = pl.ds(pl.multiple_of(side * part + ((d % m) >> 1) * rows, BLK), rows)
                src = refs[i].at[pl.ds(block * rows, rows)]
                copies.append(pltpu.make_async_copy(src, x.at[to], sems.at[i]))
            for c in copies:
                c.start()
            for c in copies:
                c.wait()
            left[...] = contract_last(x[...], sk[...])

        t = jnp.dot(x[...], w[...], preferred_element_type=jnp.float32)
        send[...] = t[:part]
        keep[...] = t[part:]

    out = [jax.ShapeDtypeStruct((part, hidden), jnp.float32)] * 2
    out.append(jax.ShapeDtypeStruct((2 * part, sketch.shape[0]), jnp.float32))
    column = pl.BlockSpec((part, tile), lambda j, s: (0, j))
    return call(
        kernel,
        idx,
        [c[1] for c in chunks] + [w, sketch],
        [ANY] * m + [pl.BlockSpec((feats, tile), lambda j, s: (0, lo + j)), whole(sketch.shape)],
        out,
        [column, column, whole(out[2].shape)],
        "forward",
        (hidden // tile,),
        (4 * part * feats * hidden, 2 * feats * hidden + 8 * part * hidden),
        after,
        [pltpu.VMEM((2 * part, feats), jnp.bfloat16), pltpu.SemaphoreType.DMA((m,))],
    )


def combine(idx, keep, got, lo, total, batch, rows, before, after):
    part, width = keep.shape
    m = part // rows

    def kernel(idx, keep, got, *refs):
        out, x, sems = refs[-3:]
        mine = (idx[0] & 1) ^ batch
        x[...] = (keep[...] + got[...]).astype(jnp.bfloat16)
        copies = []
        for i in range(m):
            to = pl.ds(pl.multiple_of((2 * i + mine) * rows, BLK), rows)
            copies.append(
                pltpu.make_async_copy(
                    x.at[pl.ds(i * rows, rows)], out.at[to, pl.ds(lo, width)], sems.at[i]
                )
            )
        for c in copies:
            c.start()
        for c in copies:
            c.wait()

    (out,), token = call(
        kernel,
        idx,
        [keep, got] + before,
        [whole(keep.shape)] * 2 + [HBM] * len(before),
        [jax.ShapeDtypeStruct((2 * part, total), jnp.bfloat16)],
        [HBM],
        "combine",
        (1,),
        (0, 10 * part * width),
        after,
        [pltpu.VMEM((part, width), jnp.bfloat16), pltpu.SemaphoreType.DMA((m,))],
        aliases={3: 0} if before else None,
    )
    return out, [token]


def sketch_part(idx, lefts, own, oth, rows, after):
    packed, lanes = own.shape
    width = lanes // 2
    half = 2 * packed
    part = half // 2
    examples = half // LEN

    def kernel(idx, first, second, own, oth, out):
        me, core = idx[0], idx[1]
        for side, right in ((0, oth), (1, own)):
            owner = 1 - (side ^ core)
            for e in range(examples):
                total = jnp.zeros((width, width), jnp.float32)
                for i in range(part // rows):
                    if 2 * i * rows // LEN != e:
                        continue
                    block, start = divmod(2 * i * rows, packed)
                    for batch, left in enumerate((first, second)):
                        at = start + ((me & 1) ^ batch) * rows
                        lo = side * part + i * rows
                        both = right[pl.ds(pl.multiple_of(at, BLK), rows), :]
                        total += lax.dot_general(
                            left[lo : lo + rows, :],
                            both[:, block * width : (block + 1) * width],
                            (((0,), (0,)), ((), ())),
                            precision=lax.Precision.HIGHEST,
                            preferred_element_type=jnp.float32,
                        )
                out[owner * examples + e] = total

    args = [*lefts, own, oth]
    out = [jax.ShapeDtypeStruct((2 * examples, width, width), jnp.float32)]
    (sketch,), token = call(
        kernel,
        idx,
        args,
        [whole(a.shape) for a in args],
        out,
        [whole(out[0].shape)],
        "sketch_part",
        (1,),
        (0, 16 * half * width),
        after,
    )
    return sketch, [token]


def body(inputs, cotangent, weight, in_sketch, out_sketch):
    n = lax.axis_size("outp")
    bits = n.bit_length() - 1
    rows, feats = inputs.shape
    hidden = weight.shape[1]
    idx = jnp.stack([lax.axis_index("outp"), lax.axis_index("inp")]).astype(jnp.int32)

    def partner(x, bit):
        return lax.ppermute(x, "outp", [(d, d ^ (1 << bit)) for d in range(n)])

    def swap(x):
        return lax.ppermute(x, "inp", [(0, 1), (1, 0)])

    evens = list(range(2, n, 2))
    far = n // 2
    chunks = {0: inputs}

    def fetch(masks):
        for mask in masks:
            bit = (mask & -mask).bit_length() - 1
            chunks[mask] = partner(chunks[mask ^ (1 << bit)], bit)

    def hold(masks, after):
        held, token = gate(idx, [chunks[m] for m in masks], after)
        chunks.update(zip(masks, held))
        return token

    grad_other = swap(cotangent)
    fetch([far, 1])

    orders = [list(range(bits)), [1, 0] + list(range(2, bits))]
    tile = pick(feats // PIECES, F_TILE)
    count = feats // PIECES // tile
    msgs, keeps = [], []
    token = []
    for p in range(PIECES):
        outs, t = backward(
            idx,
            cotangent,
            grad_other,
            weight,
            out_sketch if p == 0 else None,
            count,
            tile,
            p * count,
            rows,
            orders[p][0],
            token,
        )
        token = [t]
        msgs.append(partner(outs[0], orders[p][0]))
        keeps.append(outs[1])
        if p == 0:
            right = outs[2]
        if p == 0:
            token = hold([far, 1], token)
            fetch([m for m in evens if m != far and (m & ~far).bit_count() == 1][::-1])
    ready = [m for m in evens if m in chunks]
    while len(ready) < len(evens):
        token = hold(ready, token)
        fetch([m for m in evens if m not in chunks and m & (m - 1) in chunks])
        ready = [m for m in evens if m in chunks]
    crossed, token = join(idx, [chunks[m] for m in evens], token)
    crossed = partner(crossed, 0)

    rights = [right] + [None] * (PIECES - 1)

    def folded(p, step, after):
        done, bit = orders[p][:step], orders[p][step]
        pos = sum(1 for k in range(bit) if k not in done)
        outs, t = fold(idx, keeps[p], msgs[p], rights[p], bit, pos, after)
        msgs[p], keeps[p] = partner(outs[0], bit), outs[1]
        if p == 0:
            rights[p] = outs[2]
        return [t]

    tiles = hidden // pick(hidden, H_TILE)

    def batch_forward(batch, lo, hi, after):
        if batch:
            parts = [(1, chunks[1], 0)] + [(m + 1, crossed, i) for i, m in enumerate(evens)]
        else:
            parts = [(m, chunks[m], 0) for m in [0] + evens]
        outs, t = forward(idx, parts, rows, weight, in_sketch, lo, hi, after)
        start = lo * (hidden // tiles)
        return (outs[1], swap(outs[0]), start, hidden, batch, rows), outs[2], [t]

    cut = -(-tiles // 2)
    token = folded(0, 1, token)
    first, left1, token = batch_forward(0, 0, tiles, token)
    token = folded(1, 1, token)
    token = folded(0, 2, token)
    (crossed,), token = gate(idx, [crossed], token)
    second, left2, token = batch_forward(1, 0, cut, token)
    token = folded(1, 2, token)
    outputs, token = combine(idx, *first, [], token)
    third, _, token = batch_forward(1, cut, tiles, token)
    for step in range(3, bits):
        for p in range(PIECES):
            token = folded(p, step, token)
    right, token = last_right(idx, rights[0], msgs[0], token)
    right_got = swap(right)
    outputs, token = combine(idx, *second, [outputs], token)
    outputs, token = combine(idx, *third, [outputs], token)
    part, token = sketch_part(idx, [left1, left2], right, right_got, rows, token)
    input_grad = finish(idx, keeps, msgs, token)
    part = (part + swap(part)) * (1.0 / LEN**0.5)
    sketches = part.reshape(part.shape[0], -1)
    return (outputs, input_grad, sketches)


def solution(mesh):
    placed = (
        P(("groups", "outp"), "inp"),
        P(("groups", "inp"), "outp"),
        P("inp", "outp"),
        P(None, "inp"),
        P(None, "outp"),
    )
    return jax.shard_map(
        body,
        mesh=mesh,
        in_specs=placed,
        out_specs=(P(("groups", "inp"), "outp"), P(("groups", "outp"), "inp"), P("groups", None)),
        check_vma=False,
    )
```

```python
import jax
import jax.numpy as jnp
from jax import lax
from jax.experimental import pallas as pl
from jax.experimental.pallas import tpu as pltpu
from jax.sharding import PartitionSpec as P

LEN = 128
LANES = 128
BLK = 16
LN2 = 0.6931471805599453
SPAN = 248.0
SHIFT = 124.0
PIECES = 2
F_TILE = 512
H_TILE = 512
VMEM_MIB = {"backward": 32, "forward": 24}
MIB = 1 << 20
RIGHT_ROWS = 16
RIGHT_PARTS = 2
TIMES = {"gate": 0, "backward_0": 19 * 10**9, "backward_4": 10 * 10**9, "forward": 1 << 34, "fold": 0, "combine": 1 << 34, "sketch_part": 1 << 34}
ANY = pl.BlockSpec(memory_space=pl.ANY)
HBM = pl.BlockSpec(memory_space=pltpu.HBM)


def pick(extent, cap):
    best = LANES
    for t in range(LANES, min(cap, extent) + 1, LANES):
        if extent % t == 0:
            best = t
    return best


def contract_last(a, b):
    return lax.dot_general(a, b, (((1,), (1,)), ((), ())), preferred_element_type=jnp.float32)


def whole(shape):
    return pl.BlockSpec(shape, lambda *_: (0,) * len(shape))


def call(
    kernel, idx, args, specs, out_shape, out_specs, name, grid, work, after, scratch=(), aliases=None
):
    token = jax.ShapeDtypeStruct((8, LANES), jnp.float32)
    n_args, n_after, n_out = len(args), len(after), len(out_shape)

    def with_token(idx, *refs):
        ins = refs[:n_args]
        outs = refs[n_args + n_after :]
        outs[n_out][...] = jnp.zeros((8, LANES), jnp.float32)
        kernel(idx, *ins, *outs[:n_out], *outs[n_out + 1 :])

    out = pl.pallas_call(
        with_token,
        out_shape=list(out_shape) + [token],
        grid_spec=pltpu.PrefetchScalarGridSpec(
            num_scalar_prefetch=1,
            grid=grid,
            in_specs=list(specs) + [ANY] * n_after,
            out_specs=list(out_specs) + [whole(token.shape)],
            scratch_shapes=list(scratch),
        ),
        compiler_params=pltpu.CompilerParams(vmem_limit_bytes=VMEM_MIB.get(name.split("_")[0], 14) * MIB),
        cost_estimate=pl.CostEstimate(
            flops=TIMES.get(name, work[0]), bytes_accessed=work[1], transcendentals=0
        ),
        input_output_aliases=aliases or {},
        name=name,
    )(idx, *args, *after)
    return out[:-1], out[-1]


def encode_rows(tiles, msg, at):
    top = jnp.abs(tiles[0])
    for v in tiles[1:]:
        top = jnp.maximum(top, jnp.abs(v))
    top = jnp.max(top, axis=1, keepdims=True)
    scale = jnp.maximum(top * 1.004, 2.0**-110).astype(jnp.bfloat16).astype(jnp.float32)
    gain = SPAN / scale
    col = 0
    for v in tiles:
        w = jnp.exp2(jnp.abs(v) * gain - SHIFT)
        msg[at, col : col + v.shape[1]] = jnp.where(v < 0, -w, w).astype(jnp.bfloat16)
        col += v.shape[1]
    msg[at, col : col + LANES] = jnp.broadcast_to(scale, (BLK, LANES)).astype(jnp.bfloat16)


def decode_rows(msg, at, tile, count):
    scale = msg[at, tile * count : tile * count + LANES].astype(jnp.float32)[:, :1]
    scale = scale * (1.0 / (SPAN * LN2))
    out = []
    for t in range(count):
        w = msg[at, t * tile : (t + 1) * tile].astype(jnp.float32)
        a = (lax.log(jnp.maximum(jnp.abs(w), 2.0**-SHIFT)) + SHIFT * LN2) * scale
        out.append(jnp.where(w < 0, -a, a))
    return out


def put_right(value, msg):
    base = msg.shape[0] - RIGHT_ROWS
    for q in range(value.shape[0] // RIGHT_ROWS):
        left_over = value[q * RIGHT_ROWS : (q + 1) * RIGHT_ROWS, :]
        for k in range(RIGHT_PARTS):
            part = left_over.astype(jnp.bfloat16)
            lo = (RIGHT_PARTS * q + k) * LANES
            msg[base:, lo : lo + LANES] = part
            left_over = left_over - part.astype(jnp.float32)


def add_right(value, msg):
    base = msg.shape[0] - RIGHT_ROWS
    out = []
    for q in range(value.shape[0] // RIGHT_ROWS):
        lo = RIGHT_PARTS * q * LANES
        parts = [
            msg[base:, lo + k * LANES : lo + (k + 1) * LANES].astype(jnp.float32)
            for k in range(RIGHT_PARTS)
        ]
        got = sum(parts)
        out.append(value[q * RIGHT_ROWS : (q + 1) * RIGHT_ROWS, :] + got)
    return jnp.concatenate(out, axis=0)


def with_bit(c, pos, value):
    low = c & ((1 << pos) - 1)
    return ((c >> pos) << (pos + 1)) + low + value * (1 << pos)


def rows_at(start):
    return pl.ds(pl.multiple_of(start, BLK), BLK)


def backward(idx, own, oth, w, sketch, count, tile, first, rows, bit, after):
    half, hidden = own.shape
    n = 2 * half // rows
    width = count * tile

    def kernel(idx, own, oth, w, *rest):
        if sketch is None:
            msg, keep, x, total, sems = rest
        else:
            sk, msg, keep, right, x, total, sems, sk_here = rest
        j = pl.program_id(0)
        me, core = idx[0], idx[1]

        @pl.when(j == 0)
        def _():
            a = pltpu.make_async_copy(own, x.at[core], sems.at[0])
            b = pltpu.make_async_copy(oth, x.at[1 - core], sems.at[1])
            a.start()
            b.start()
            if sketch is not None:
                c = pltpu.make_async_copy(sk, sk_here, sems.at[2])
                c.start()
                c.wait()
            a.wait()
            b.wait()
            if sketch is not None:
                low, high = jnp.zeros_like(sk_here[...]), sk_here[...]
                first_block = jnp.concatenate([high, low], axis=0)
                second_block = jnp.concatenate([low, high], axis=0)
                right[...] = contract_last(x[core, : half // 2, :], first_block) + contract_last(
                    x[core, half // 2 :, :], second_block
                )
                put_right(right[...], msg)

        xs = x[...].reshape(2 * half, hidden)
        total[j] = contract_last(xs, w[...]).reshape(n, rows, tile)

        @pl.when(j == count - 1)
        def _():
            mine = (me >> bit) & 1
            for c in range(n // 2):
                away, here = with_bit(c, bit, 1 - mine), with_bit(c, bit, mine)

                @pl.loop(0, rows // BLK)
                def _(b):
                    src = rows_at(b * BLK)
                    encode_rows(
                        [total[t, away, src, :] for t in range(count)],
                        msg,
                        rows_at(c * rows + b * BLK),
                    )
                    for t in range(count):
                        keep[t, c, src, :] = total[t, here, src, :]

    extra = 0 if sketch is None else RIGHT_ROWS
    out = [
        jax.ShapeDtypeStruct((n // 2 * rows + extra, width + LANES), jnp.bfloat16),
        jax.ShapeDtypeStruct((count, n // 2, rows, tile), jnp.float32),
    ]
    args = [own, oth, w]
    specs = [HBM, ANY, pl.BlockSpec((tile, hidden), lambda j, s: (first + j, 0))]
    scratch = [
        pltpu.VMEM((2, half, hidden), jnp.bfloat16),
        pltpu.VMEM((count, n, rows, tile), jnp.float32),
        pltpu.SemaphoreType.DMA((3,)),
    ]
    if sketch is not None:
        args.append(sketch)
        specs.append(HBM)
        out.append(jax.ShapeDtypeStruct((half // 2, 2 * sketch.shape[0]), jnp.float32))
        scratch.append(pltpu.VMEM(sketch.shape, sketch.dtype))
    return call(
        kernel,
        idx,
        args,
        specs,
        out,
        [whole(o.shape) for o in out],
        f"backward_{first}",
        (count,),
        (4 * half * hidden * width, 2 * hidden * width + 12 * half * width),
        after,
        scratch,
    )


def fold(idx, keep, got, right, bit, pos, after):
    count, m, rows, tile = keep.shape
    extra = 0 if right is None else RIGHT_ROWS

    def kernel(idx, keep, got, *refs):
        if extra:
            right, msg, rest, total = refs
            total[...] = add_right(right[...], got)
            put_right(total[...], msg)
        else:
            msg, rest = refs
        mine = (idx[0] >> bit) & 1
        for c in range(m // 2):
            away, here = with_bit(c, pos, 1 - mine), with_bit(c, pos, mine)

            @pl.loop(0, rows // BLK)
            def _(b):
                src = rows_at(b * BLK)
                plus = decode_rows(got, rows_at(away * rows + b * BLK), tile, count)
                encode_rows(
                    [keep[t, away, src, :] + plus[t] for t in range(count)],
                    msg,
                    rows_at(c * rows + b * BLK),
                )
                plus = decode_rows(got, rows_at(here * rows + b * BLK), tile, count)
                for t in range(count):
                    rest[t, c, src, :] = keep[t, here, src, :] + plus[t]

    args = [keep, got] + ([right] if extra else [])
    out = [
        jax.ShapeDtypeStruct((m // 2 * rows + extra, got.shape[1]), jnp.bfloat16),
        jax.ShapeDtypeStruct((count, m // 2, rows, tile), jnp.float32),
    ] + ([jax.ShapeDtypeStruct(right.shape, jnp.float32)] if extra else [])
    return call(
        kernel,
        idx,
        args,
        [whole(a.shape) for a in args],
        out,
        [whole(o.shape) for o in out],
        "fold",
        (1,),
        (0, 12 * keep.size),
        after,
    )


def finish(idx, keeps, gots, after):
    count, _, rows, tile = keeps[0].shape
    pieces = len(keeps)

    def kernel(idx, *refs):
        out = refs[-1]
        for p in range(pieces):

            @pl.loop(0, rows // BLK)
            def _(b):
                at = rows_at(b * BLK)
                plus = decode_rows(refs[pieces + p], at, tile, count)
                for t in range(count):
                    lo = (p * count + t) * tile
                    out[at, lo : lo + tile] = (refs[p][t, 0, at, :] + plus[t]).astype(
                        jnp.bfloat16
                    )

    args = list(keeps) + list(gots)
    out = [jax.ShapeDtypeStruct((rows, pieces * count * tile), jnp.bfloat16)]
    (grad,), _ = call(
        kernel,
        idx,
        args,
        [whole(a.shape) for a in args],
        out,
        [whole(out[0].shape)],
        "finish",
        (1,),
        (0, 16 * rows * count * tile),
        after,
    )
    return grad


def gate(idx, arrays, after):
    k = len(arrays)

    def kernel(idx, *refs):
        pass

    out, token = call(
        kernel,
        idx,
        arrays,
        [ANY] * k,
        [jax.ShapeDtypeStruct(a.shape, a.dtype) for a in arrays],
        [ANY] * k,
        "gate",
        (1,),
        (0, 0),
        after,
        aliases={1 + i: i for i in range(k)},
    )
    return list(out), [token]


def join(idx, arrays, after):
    rows, width = arrays[0].shape
    k = len(arrays)

    def kernel(idx, *refs):
        out, sems = refs[-2:]
        copies = [
            pltpu.make_async_copy(refs[i], out.at[pl.ds(i * rows, rows)], sems.at[i])
            for i in range(k)
        ]
        for c in copies:
            c.start()
        for c in copies:
            c.wait()

    (out,), token = call(
        kernel,
        idx,
        arrays,
        [ANY] * k,
        [jax.ShapeDtypeStruct((k * rows, width), arrays[0].dtype)],
        [ANY],
        "join",
        (1,),
        (0, 0),
        after,
        [pltpu.SemaphoreType.DMA((k,))],
    )
    return out, [token]


def last_right(idx, right, got, after):
    def kernel(idx, right, got, out):
        out[...] = add_right(right[...], got)

    out = [jax.ShapeDtypeStruct(right.shape, jnp.float32)]
    specs = [whole(right.shape), whole(got.shape)]
    work = (0, 2 * got.size)
    (total,), token = call(
        kernel, idx, [right, got], specs, out, specs[:1], "last_right", (1,), work, after
    )
    return total, [token]


def forward(idx, chunks, rows, w, sketch, lo, hi, after):
    feats = w.shape[0]
    m = len(chunks)
    tile = pick(w.shape[1], H_TILE)
    hidden = (hi - lo) * tile
    part = m // 2 * rows

    def kernel(idx, *refs):
        w, sk, send, keep, left, x, sems = refs[m:]
        me, core = idx[0], idx[1]

        @pl.when(pl.program_id(0) == 0)
        def _():
            copies = []
            for i, (mask, _, block) in enumerate(chunks):
                d = me ^ mask
                side = 1 - ((d // m) ^ core)
                to = pl.ds(pl.multiple_of(side * part + ((d % m) >> 1) * rows, BLK), rows)
                src = refs[i].at[pl.ds(block * rows, rows)]
                copies.append(pltpu.make_async_copy(src, x.at[to], sems.at[i]))
            for c in copies:
                c.start()
            for c in copies:
                c.wait()
            left[...] = contract_last(x[...], sk[...])

        t = jnp.dot(x[...], w[...], preferred_element_type=jnp.float32)
        send[...] = t[:part]
        keep[...] = t[part:]

    out = [jax.ShapeDtypeStruct((part, hidden), jnp.float32)] * 2
    out.append(jax.ShapeDtypeStruct((2 * part, sketch.shape[0]), jnp.float32))
    column = pl.BlockSpec((part, tile), lambda j, s: (0, j))
    return call(
        kernel,
        idx,
        [c[1] for c in chunks] + [w, sketch],
        [ANY] * m + [pl.BlockSpec((feats, tile), lambda j, s: (0, lo + j)), whole(sketch.shape)],
        out,
        [column, column, whole(out[2].shape)],
        "forward",
        (hidden // tile,),
        (4 * part * feats * hidden, 2 * feats * hidden + 8 * part * hidden),
        after,
        [pltpu.VMEM((2 * part, feats), jnp.bfloat16), pltpu.SemaphoreType.DMA((m,))],
    )


def combine(idx, keep, got, lo, total, batch, rows, before, after):
    part, width = keep.shape
    m = part // rows

    def kernel(idx, keep, got, *refs):
        out, x, sems = refs[-3:]
        mine = (idx[0] & 1) ^ batch
        x[...] = (keep[...] + got[...]).astype(jnp.bfloat16)
        copies = []
        for i in range(m):
            to = pl.ds(pl.multiple_of((2 * i + mine) * rows, BLK), rows)
            copies.append(
                pltpu.make_async_copy(
                    x.at[pl.ds(i * rows, rows)], out.at[to, pl.ds(lo, width)], sems.at[i]
                )
            )
        for c in copies:
            c.start()
        for c in copies:
            c.wait()

    (out,), token = call(
        kernel,
        idx,
        [keep, got] + before,
        [whole(keep.shape)] * 2 + [HBM] * len(before),
        [jax.ShapeDtypeStruct((2 * part, total), jnp.bfloat16)],
        [HBM],
        "combine",
        (1,),
        (0, 10 * part * width),
        after,
        [pltpu.VMEM((part, width), jnp.bfloat16), pltpu.SemaphoreType.DMA((m,))],
        aliases={3: 0} if before else None,
    )
    return out, [token]


def sketch_part(idx, lefts, own, oth, rows, after):
    packed, lanes = own.shape
    width = lanes // 2
    half = 2 * packed
    part = half // 2
    examples = half // LEN

    def kernel(idx, first, second, own, oth, out):
        me, core = idx[0], idx[1]
        for side, right in ((0, oth), (1, own)):
            owner = 1 - (side ^ core)
            for e in range(examples):
                total = jnp.zeros((width, width), jnp.float32)
                for i in range(part // rows):
                    if 2 * i * rows // LEN != e:
                        continue
                    block, start = divmod(2 * i * rows, packed)
                    for batch, left in enumerate((first, second)):
                        at = start + ((me & 1) ^ batch) * rows
                        lo = side * part + i * rows
                        both = right[pl.ds(pl.multiple_of(at, BLK), rows), :]
                        total += lax.dot_general(
                            left[lo : lo + rows, :],
                            both[:, block * width : (block + 1) * width],
                            (((0,), (0,)), ((), ())),
                            precision=lax.Precision.HIGHEST,
                            preferred_element_type=jnp.float32,
                        )
                out[owner * examples + e] = total

    args = [*lefts, own, oth]
    out = [jax.ShapeDtypeStruct((2 * examples, width, width), jnp.float32)]
    (sketch,), token = call(
        kernel,
        idx,
        args,
        [whole(a.shape) for a in args],
        out,
        [whole(out[0].shape)],
        "sketch_part",
        (1,),
        (0, 16 * half * width),
        after,
    )
    return sketch, [token]


def body(inputs, cotangent, weight, in_sketch, out_sketch):
    n = lax.axis_size("outp")
    bits = n.bit_length() - 1
    rows, feats = inputs.shape
    hidden = weight.shape[1]
    idx = jnp.stack([lax.axis_index("outp"), lax.axis_index("inp")]).astype(jnp.int32)

    def partner(x, bit):
        return lax.ppermute(x, "outp", [(d, d ^ (1 << bit)) for d in range(n)])

    def swap(x):
        return lax.ppermute(x, "inp", [(0, 1), (1, 0)])

    evens = list(range(2, n, 2))
    chunks = {0: inputs}

    def fetch(masks):
        for mask in masks:
            bit = (mask & -mask).bit_length() - 1
            chunks[mask] = partner(chunks[mask ^ (1 << bit)], bit)

    def hold(masks, after):
        held, token = gate(idx, [chunks[m] for m in masks], after)
        chunks.update(zip(masks, held))
        return token

    grad_other = swap(cotangent)
    singles = [1 << k for k in reversed(range(bits))]
    fetch(singles)

    orders = [list(range(bits)), [1, 0] + list(range(2, bits))]
    tile = pick(feats // PIECES, F_TILE)
    count = feats // PIECES // tile
    msgs, keeps = [], []
    token = []
    for p in range(PIECES):
        outs, t = backward(
            idx,
            cotangent,
            grad_other,
            weight,
            out_sketch if p == 0 else None,
            count,
            tile,
            p * count,
            rows,
            orders[p][0],
            token,
        )
        token = [t]
        msgs.append(partner(outs[0], orders[p][0]))
        keeps.append(outs[1])
        if p == 0:
            right = outs[2]
        if p == 0:
            token = hold(singles, token)
            fetch([m for m in evens if m.bit_count() == 2])
    ready = [m for m in evens if m in chunks]
    while len(ready) < len(evens):
        token = hold(ready, token)
        fetch([m for m in evens if m not in chunks and m & (m - 1) in chunks])
        ready = [m for m in evens if m in chunks]
    crossed, token = join(idx, [chunks[m] for m in evens], token)
    crossed = partner(crossed, 0)

    rights = [right] + [None] * (PIECES - 1)

    def folded(p, step, after):
        done, bit = orders[p][:step], orders[p][step]
        pos = sum(1 for k in range(bit) if k not in done)
        outs, t = fold(idx, keeps[p], msgs[p], rights[p], bit, pos, after)
        msgs[p], keeps[p] = partner(outs[0], bit), outs[1]
        if p == 0:
            rights[p] = outs[2]
        return [t]

    tiles = hidden // pick(hidden, H_TILE)

    def batch_forward(batch, lo, hi, after):
        if batch:
            parts = [(1, chunks[1], 0)] + [(m + 1, crossed, i) for i, m in enumerate(evens)]
        else:
            parts = [(m, chunks[m], 0) for m in [0] + evens]
        outs, t = forward(idx, parts, rows, weight, in_sketch, lo, hi, after)
        start = lo * (hidden // tiles)
        return (outs[1], swap(outs[0]), start, hidden, batch, rows), outs[2], [t]

    cut = -(-tiles // 2)
    token = folded(0, 1, token)
    first, left1, token = batch_forward(0, 0, tiles, token)
    token = folded(1, 1, token)
    token = folded(0, 2, token)
    second, left2, token = batch_forward(1, 0, cut, token)
    token = folded(1, 2, token)
    outputs, token = combine(idx, *first, [], token)
    third, _, token = batch_forward(1, cut, tiles, token)
    for step in range(3, bits):
        for p in range(PIECES):
            token = folded(p, step, token)
    right, token = last_right(idx, rights[0], msgs[0], token)
    right_got = swap(right)
    outputs, token = combine(idx, *second, [outputs], token)
    outputs, token = combine(idx, *third, [outputs], token)
    part, token = sketch_part(idx, [left1, left2], right, right_got, rows, token)
    input_grad = finish(idx, keeps, msgs, token)
    part = (part + swap(part)) * (1.0 / LEN**0.5)
    sketches = part.reshape(part.shape[0], -1)
    return (outputs, input_grad, sketches)


def solution(mesh):
    placed = (
        P(("groups", "outp"), "inp"),
        P(("groups", "inp"), "outp"),
        P("inp", "outp"),
        P(None, "inp"),
        P(None, "outp"),
    )
    return jax.shard_map(
        body,
        mesh=mesh,
        in_specs=placed,
        out_specs=(P(("groups", "inp"), "outp"), P(("groups", "outp"), "inp"), P("groups", None)),
        check_vma=False,
    )
```

```python
import jax
import jax.numpy as jnp
from jax import lax
from jax.experimental import pallas as pl
from jax.experimental.pallas import tpu as pltpu
from jax.sharding import PartitionSpec as P

LEN = 128
LANES = 128
BLK = 16
LN2 = 0.6931471805599453
SPAN = 248.0
SHIFT = 124.0
PIECES = 2
F_TILE = 512
H_TILE = 512
VMEM_MIB = {"backward": 36, "forward": 28}
MIB = 1 << 20
SLOTS = 3
RIGHT_ROWS = 16
RIGHT_PARTS = 2
TIMES = {"gate": 0, "backward_0": 19 * 10**9, "backward_4": 10 * 10**9, "forward": 1 << 34, "fold": 0, "combine": 1 << 34, "sketch_part": 1 << 34}
ANY = pl.BlockSpec(memory_space=pl.ANY)
HBM = pl.BlockSpec(memory_space=pltpu.HBM)


def pick(extent, cap):
    best = LANES
    for t in range(LANES, min(cap, extent) + 1, LANES):
        if extent % t == 0:
            best = t
    return best


def contract_last(a, b):
    return lax.dot_general(a, b, (((1,), (1,)), ((), ())), preferred_element_type=jnp.float32)


def whole(shape):
    return pl.BlockSpec(shape, lambda *_: (0,) * len(shape))


def call(
    kernel, idx, args, specs, out_shape, out_specs, name, grid, work, after, scratch=(), aliases=None
):
    token = jax.ShapeDtypeStruct((8, LANES), jnp.float32)
    n_args, n_after, n_out = len(args), len(after), len(out_shape)

    def with_token(idx, *refs):
        ins = refs[:n_args]
        outs = refs[n_args + n_after :]
        outs[n_out][...] = jnp.zeros((8, LANES), jnp.float32)
        kernel(idx, *ins, *outs[:n_out], *outs[n_out + 1 :])

    out = pl.pallas_call(
        with_token,
        out_shape=list(out_shape) + [token],
        grid_spec=pltpu.PrefetchScalarGridSpec(
            num_scalar_prefetch=1,
            grid=grid,
            in_specs=list(specs) + [ANY] * n_after,
            out_specs=list(out_specs) + [whole(token.shape)],
            scratch_shapes=list(scratch),
        ),
        compiler_params=pltpu.CompilerParams(vmem_limit_bytes=VMEM_MIB.get(name.split("_")[0], 14) * MIB),
        cost_estimate=pl.CostEstimate(
            flops=TIMES.get(name, work[0]), bytes_accessed=work[1], transcendentals=0
        ),
        input_output_aliases=aliases or {},
        name=name,
    )(idx, *args, *after)
    return out[:-1], out[-1]


def encode_rows(tiles, msg, at):
    top = jnp.abs(tiles[0])
    for v in tiles[1:]:
        top = jnp.maximum(top, jnp.abs(v))
    top = jnp.max(top, axis=1, keepdims=True)
    scale = jnp.maximum(top * 1.004, 2.0**-110).astype(jnp.bfloat16).astype(jnp.float32)
    gain = SPAN / scale
    col = 0
    for v in tiles:
        w = jnp.exp2(jnp.abs(v) * gain - SHIFT)
        msg[at, col : col + v.shape[1]] = jnp.where(v < 0, -w, w).astype(jnp.bfloat16)
        col += v.shape[1]
    msg[at, col : col + LANES] = jnp.broadcast_to(scale, (BLK, LANES)).astype(jnp.bfloat16)


def decode_rows(msg, at, tile, count):
    scale = msg[at, tile * count : tile * count + LANES].astype(jnp.float32)[:, :1]
    scale = scale * (1.0 / (SPAN * LN2))
    out = []
    for t in range(count):
        w = msg[at, t * tile : (t + 1) * tile].astype(jnp.float32)
        a = (lax.log(jnp.maximum(jnp.abs(w), 2.0**-SHIFT)) + SHIFT * LN2) * scale
        out.append(jnp.where(w < 0, -a, a))
    return out


def put_right(value, msg):
    base = msg.shape[0] - RIGHT_ROWS
    for q in range(value.shape[0] // RIGHT_ROWS):
        left_over = value[q * RIGHT_ROWS : (q + 1) * RIGHT_ROWS, :]
        for k in range(RIGHT_PARTS):
            part = left_over.astype(jnp.bfloat16)
            lo = (RIGHT_PARTS * q + k) * LANES
            msg[base:, lo : lo + LANES] = part
            left_over = left_over - part.astype(jnp.float32)


def add_right(value, msg):
    base = msg.shape[0] - RIGHT_ROWS
    out = []
    for q in range(value.shape[0] // RIGHT_ROWS):
        lo = RIGHT_PARTS * q * LANES
        parts = [
            msg[base:, lo + k * LANES : lo + (k + 1) * LANES].astype(jnp.float32)
            for k in range(RIGHT_PARTS)
        ]
        got = sum(parts)
        out.append(value[q * RIGHT_ROWS : (q + 1) * RIGHT_ROWS, :] + got)
    return jnp.concatenate(out, axis=0)


def with_bit(c, pos, value):
    low = c & ((1 << pos) - 1)
    return ((c >> pos) << (pos + 1)) + low + value * (1 << pos)


def rows_at(start):
    return pl.ds(pl.multiple_of(start, BLK), BLK)


def backward(idx, own, oth, w, sketch, count, tile, first, rows, bit, after):
    half, hidden = own.shape
    n = 2 * half // rows
    width = count * tile

    def kernel(idx, own, oth, w, *rest):
        if sketch is None:
            msg, keep, x, total, sems, tiles = rest
        else:
            sk, msg, keep, right, x, total, sems, tiles, sk_here = rest
        me, core = idx[0], idx[1]

        def fetch(j):
            at = pl.ds(pl.multiple_of((first + j) * tile, tile), tile)
            slot = lax.rem(j, SLOTS)
            return pltpu.make_async_copy(w.at[at], tiles.at[slot], sems.at[3 + slot])

        copies = [
            pltpu.make_async_copy(own, x.at[core], sems.at[0]),
            pltpu.make_async_copy(oth, x.at[1 - core], sems.at[1]),
        ]
        if sketch is not None:
            copies.append(pltpu.make_async_copy(sk, sk_here, sems.at[2]))
        for c in copies:
            c.start()
        for j in range(min(SLOTS - 1, count)):
            fetch(jnp.int32(j)).start()
        for c in copies:
            c.wait()
        if sketch is not None:
            low, high = jnp.zeros_like(sk_here[...]), sk_here[...]
            first_block = jnp.concatenate([high, low], axis=0)
            second_block = jnp.concatenate([low, high], axis=0)
            right[...] = contract_last(x[core, : half // 2, :], first_block) + contract_last(
                x[core, half // 2 :, :], second_block
            )
            put_right(right[...], msg)

        @pl.loop(0, count)
        def _(j):
            fetch(j).wait()

            @pl.when(j + SLOTS - 1 < count)
            def _():
                fetch(j + SLOTS - 1).start()

            xs = x[...].reshape(2 * half, hidden)
            total[j] = contract_last(xs, tiles[lax.rem(j, SLOTS)]).reshape(n, rows, tile)

        mine = (me >> bit) & 1
        for c in range(n // 2):
            away, here = with_bit(c, bit, 1 - mine), with_bit(c, bit, mine)

            @pl.loop(0, rows // BLK)
            def _(b):
                src = rows_at(b * BLK)
                encode_rows(
                    [total[t, away, src, :] for t in range(count)],
                    msg,
                    rows_at(c * rows + b * BLK),
                )
                for t in range(count):
                    keep[t, c, src, :] = total[t, here, src, :]

    extra = 0 if sketch is None else RIGHT_ROWS
    out = [
        jax.ShapeDtypeStruct((n // 2 * rows + extra, width + LANES), jnp.bfloat16),
        jax.ShapeDtypeStruct((count, n // 2, rows, tile), jnp.float32),
    ]
    args = [own, oth, w]
    specs = [HBM, ANY, HBM]
    scratch = [
        pltpu.VMEM((2, half, hidden), jnp.bfloat16),
        pltpu.VMEM((count, n, rows, tile), jnp.float32),
        pltpu.SemaphoreType.DMA((3 + SLOTS,)),
        pltpu.VMEM((SLOTS, tile, hidden), w.dtype),
    ]
    if sketch is not None:
        args.append(sketch)
        specs.append(HBM)
        out.append(jax.ShapeDtypeStruct((half // 2, 2 * sketch.shape[0]), jnp.float32))
        scratch.append(pltpu.VMEM(sketch.shape, sketch.dtype))
    return call(
        kernel,
        idx,
        args,
        specs,
        out,
        [whole(o.shape) for o in out],
        f"backward_{first}",
        (1,),
        (4 * half * hidden * width, 2 * hidden * width + 12 * half * width),
        after,
        scratch,
    )


def fold(idx, keep, got, right, bit, pos, after):
    count, m, rows, tile = keep.shape
    extra = 0 if right is None else RIGHT_ROWS

    def kernel(idx, keep, got, *refs):
        if extra:
            right, msg, rest, total = refs
            total[...] = add_right(right[...], got)
            put_right(total[...], msg)
        else:
            msg, rest = refs
        mine = (idx[0] >> bit) & 1
        for c in range(m // 2):
            away, here = with_bit(c, pos, 1 - mine), with_bit(c, pos, mine)

            @pl.loop(0, rows // BLK)
            def _(b):
                src = rows_at(b * BLK)
                plus = decode_rows(got, rows_at(away * rows + b * BLK), tile, count)
                encode_rows(
                    [keep[t, away, src, :] + plus[t] for t in range(count)],
                    msg,
                    rows_at(c * rows + b * BLK),
                )
                plus = decode_rows(got, rows_at(here * rows + b * BLK), tile, count)
                for t in range(count):
                    rest[t, c, src, :] = keep[t, here, src, :] + plus[t]

    args = [keep, got] + ([right] if extra else [])
    out = [
        jax.ShapeDtypeStruct((m // 2 * rows + extra, got.shape[1]), jnp.bfloat16),
        jax.ShapeDtypeStruct((count, m // 2, rows, tile), jnp.float32),
    ] + ([jax.ShapeDtypeStruct(right.shape, jnp.float32)] if extra else [])
    return call(
        kernel,
        idx,
        args,
        [whole(a.shape) for a in args],
        out,
        [whole(o.shape) for o in out],
        "fold",
        (1,),
        (0, 12 * keep.size),
        after,
    )


def finish(idx, keeps, gots, after):
    count, _, rows, tile = keeps[0].shape
    pieces = len(keeps)

    def kernel(idx, *refs):
        out = refs[-1]
        for p in range(pieces):

            @pl.loop(0, rows // BLK)
            def _(b):
                at = rows_at(b * BLK)
                plus = decode_rows(refs[pieces + p], at, tile, count)
                for t in range(count):
                    lo = (p * count + t) * tile
                    out[at, lo : lo + tile] = (refs[p][t, 0, at, :] + plus[t]).astype(
                        jnp.bfloat16
                    )

    args = list(keeps) + list(gots)
    out = [jax.ShapeDtypeStruct((rows, pieces * count * tile), jnp.bfloat16)]
    (grad,), _ = call(
        kernel,
        idx,
        args,
        [whole(a.shape) for a in args],
        out,
        [whole(out[0].shape)],
        "finish",
        (1,),
        (0, 16 * rows * count * tile),
        after,
    )
    return grad


def gate(idx, arrays, after):
    k = len(arrays)

    def kernel(idx, *refs):
        pass

    out, token = call(
        kernel,
        idx,
        arrays,
        [ANY] * k,
        [jax.ShapeDtypeStruct(a.shape, a.dtype) for a in arrays],
        [ANY] * k,
        "gate",
        (1,),
        (0, 0),
        after,
        aliases={1 + i: i for i in range(k)},
    )
    return list(out), [token]


def join(idx, arrays, after):
    rows, width = arrays[0].shape
    k = len(arrays)

    def kernel(idx, *refs):
        out, sems = refs[-2:]
        copies = [
            pltpu.make_async_copy(refs[i], out.at[pl.ds(i * rows, rows)], sems.at[i])
            for i in range(k)
        ]
        for c in copies:
            c.start()
        for c in copies:
            c.wait()

    (out,), token = call(
        kernel,
        idx,
        arrays,
        [ANY] * k,
        [jax.ShapeDtypeStruct((k * rows, width), arrays[0].dtype)],
        [ANY],
        "join",
        (1,),
        (0, 0),
        after,
        [pltpu.SemaphoreType.DMA((k,))],
    )
    return out, [token]


def last_right(idx, right, got, after):
    def kernel(idx, right, got, out):
        out[...] = add_right(right[...], got)

    out = [jax.ShapeDtypeStruct(right.shape, jnp.float32)]
    specs = [whole(right.shape), whole(got.shape)]
    work = (0, 2 * got.size)
    (total,), token = call(
        kernel, idx, [right, got], specs, out, specs[:1], "last_right", (1,), work, after
    )
    return total, [token]


def forward(idx, chunks, rows, w, sketch, lo, hi, after):
    feats = w.shape[0]
    m = len(chunks)
    tile = pick(w.shape[1], H_TILE)
    hidden = (hi - lo) * tile
    part = m // 2 * rows

    count = hi - lo

    def kernel(idx, *refs):
        if sketch is None:
            w, send, keep, x, sems, tiles, outs, out_sems = refs[m:]
        else:
            w, sk, send, keep, left, x, sems, tiles, outs, out_sems = refs[m:]
        me, core = idx[0], idx[1]

        def fetch(j):
            at = pl.ds(pl.multiple_of((lo + j) * tile, tile), tile)
            slot = lax.rem(j, SLOTS)
            return pltpu.make_async_copy(w.at[:, at], tiles.at[slot], sems.at[m + slot])

        def give(j):
            at = pl.ds(pl.multiple_of(j * tile, tile), tile)
            slot = lax.rem(j, 2)
            return [
                pltpu.make_async_copy(outs.at[slot, side], ref.at[:, at], out_sems.at[slot, side])
                for side, ref in enumerate((send, keep))
            ]

        copies = []
        for i, (mask, _, block) in enumerate(chunks):
            d = me ^ mask
            side = 1 - ((d // m) ^ core)
            to = pl.ds(pl.multiple_of(side * part + ((d % m) >> 1) * rows, BLK), rows)
            src = refs[i].at[pl.ds(block * rows, rows)]
            copies.append(pltpu.make_async_copy(src, x.at[to], sems.at[i]))
        for c in copies:
            c.start()
        for j in range(min(SLOTS - 1, count)):
            fetch(jnp.int32(j)).start()
        for c in copies:
            c.wait()
        if sketch is not None:
            left[...] = contract_last(x[...], sk[...])

        @pl.loop(0, count)
        def _(j):
            fetch(j).wait()

            @pl.when(j + SLOTS - 1 < count)
            def _():
                fetch(j + SLOTS - 1).start()

            t = jnp.dot(x[...], tiles[lax.rem(j, SLOTS)], preferred_element_type=jnp.float32)

            @pl.when(j >= 2)
            def _():
                for c in give(j - 2):
                    c.wait()

            outs[lax.rem(j, 2)] = t.reshape(2, part, tile)
            for c in give(j):
                c.start()

        for j in range(max(0, count - 2), count):
            for c in give(jnp.int32(j)):
                c.wait()

    args = [c[1] for c in chunks] + [w]
    specs = [ANY] * m + [HBM]
    out = [jax.ShapeDtypeStruct((part, hidden), jnp.float32)] * 2
    out_specs = [ANY, ANY]
    if sketch is not None:
        args.append(sketch)
        specs.append(whole(sketch.shape))
        out.append(jax.ShapeDtypeStruct((2 * part, sketch.shape[0]), jnp.float32))
        out_specs.append(whole(out[2].shape))
    return call(
        kernel,
        idx,
        args,
        specs,
        out,
        out_specs,
        "forward",
        (1,),
        (4 * part * feats * hidden, 2 * feats * hidden + 8 * part * hidden),
        after,
        [
            pltpu.VMEM((2 * part, feats), jnp.bfloat16),
            pltpu.SemaphoreType.DMA((m + SLOTS,)),
            pltpu.VMEM((SLOTS, feats, tile), w.dtype),
            pltpu.VMEM((2, 2, part, tile), jnp.float32),
            pltpu.SemaphoreType.DMA((2, 2)),
        ],
    )


def combine(idx, keep, got, lo, total, batch, rows, before, after):
    part, width = keep.shape
    m = part // rows

    def kernel(idx, keep, got, *refs):
        out, x, sems = refs[-3:]
        mine = (idx[0] & 1) ^ batch
        x[...] = (keep[...] + got[...]).astype(jnp.bfloat16)
        copies = []
        for i in range(m):
            to = pl.ds(pl.multiple_of((2 * i + mine) * rows, BLK), rows)
            copies.append(
                pltpu.make_async_copy(
                    x.at[pl.ds(i * rows, rows)], out.at[to, pl.ds(lo, width)], sems.at[i]
                )
            )
        for c in copies:
            c.start()
        for c in copies:
            c.wait()

    (out,), token = call(
        kernel,
        idx,
        [keep, got] + before,
        [whole(keep.shape)] * 2 + [HBM] * len(before),
        [jax.ShapeDtypeStruct((2 * part, total), jnp.bfloat16)],
        [HBM],
        "combine",
        (1,),
        (0, 10 * part * width),
        after,
        [pltpu.VMEM((part, width), jnp.bfloat16), pltpu.SemaphoreType.DMA((m,))],
        aliases={3: 0} if before else None,
    )
    return out, [token]


def sketch_part(idx, lefts, own, oth, rows, after):
    packed, lanes = own.shape
    width = lanes // 2
    half = 2 * packed
    part = half // 2
    examples = half // LEN

    def kernel(idx, first, second, own, oth, out):
        me, core = idx[0], idx[1]
        for side, right in ((0, oth), (1, own)):
            owner = 1 - (side ^ core)
            for e in range(examples):
                total = jnp.zeros((width, width), jnp.float32)
                for i in range(part // rows):
                    if 2 * i * rows // LEN != e:
                        continue
                    block, start = divmod(2 * i * rows, packed)
                    for batch, left in enumerate((first, second)):
                        at = start + ((me & 1) ^ batch) * rows
                        lo = side * part + i * rows
                        both = right[pl.ds(pl.multiple_of(at, BLK), rows), :]
                        total += lax.dot_general(
                            left[lo : lo + rows, :],
                            both[:, block * width : (block + 1) * width],
                            (((0,), (0,)), ((), ())),
                            precision=lax.Precision.HIGHEST,
                            preferred_element_type=jnp.float32,
                        )
                out[owner * examples + e] = total

    args = [*lefts, own, oth]
    out = [jax.ShapeDtypeStruct((2 * examples, width, width), jnp.float32)]
    (sketch,), token = call(
        kernel,
        idx,
        args,
        [whole(a.shape) for a in args],
        out,
        [whole(out[0].shape)],
        "sketch_part",
        (1,),
        (0, 16 * half * width),
        after,
    )
    return sketch, [token]


def body(inputs, cotangent, weight, in_sketch, out_sketch):
    n = lax.axis_size("outp")
    bits = n.bit_length() - 1
    rows, feats = inputs.shape
    hidden = weight.shape[1]
    idx = jnp.stack([lax.axis_index("outp"), lax.axis_index("inp")]).astype(jnp.int32)

    def partner(x, bit):
        return lax.ppermute(x, "outp", [(d, d ^ (1 << bit)) for d in range(n)])

    def swap(x):
        return lax.ppermute(x, "inp", [(0, 1), (1, 0)])

    evens = list(range(2, n, 2))
    chunks = {0: inputs}

    def fetch(masks):
        for mask in masks:
            bit = (mask & -mask).bit_length() - 1
            chunks[mask] = partner(chunks[mask ^ (1 << bit)], bit)

    def hold(masks, after):
        held, token = gate(idx, [chunks[m] for m in masks], after)
        chunks.update(zip(masks, held))
        return token

    grad_other = swap(cotangent)
    singles = [1 << k for k in reversed(range(bits))]
    fetch(singles)

    orders = [list(range(bits)), [1, 0] + list(range(2, bits))]
    tile = pick(feats // PIECES, F_TILE)
    count = feats // PIECES // tile
    msgs, keeps = [], []
    token = []
    for p in range(PIECES):
        outs, t = backward(
            idx,
            cotangent,
            grad_other,
            weight,
            out_sketch if p == 0 else None,
            count,
            tile,
            p * count,
            rows,
            orders[p][0],
            token,
        )
        token = [t]
        msgs.append(partner(outs[0], orders[p][0]))
        keeps.append(outs[1])
        if p == 0:
            right = outs[2]
        if p == 0:
            token = hold(singles, token)
            fetch([m for m in evens if m.bit_count() == 2])
    ready = [m for m in evens if m in chunks]
    while len(ready) < len(evens):
        token = hold(ready, token)
        fetch([m for m in evens if m not in chunks and m & (m - 1) in chunks])
        ready = [m for m in evens if m in chunks]
    crossed, token = join(idx, [chunks[m] for m in evens], token)
    crossed = partner(crossed, 0)

    rights = [right] + [None] * (PIECES - 1)

    def folded(p, step, after):
        done, bit = orders[p][:step], orders[p][step]
        pos = sum(1 for k in range(bit) if k not in done)
        outs, t = fold(idx, keeps[p], msgs[p], rights[p], bit, pos, after)
        msgs[p], keeps[p] = partner(outs[0], bit), outs[1]
        if p == 0:
            rights[p] = outs[2]
        return [t]

    tiles = hidden // pick(hidden, H_TILE)

    def batch_forward(batch, lo, hi, after):
        if batch:
            parts = [(1, chunks[1], 0)] + [(m + 1, crossed, i) for i, m in enumerate(evens)]
        else:
            parts = [(m, chunks[m], 0) for m in [0] + evens]
        outs, t = forward(idx, parts, rows, weight, None if lo else in_sketch, lo, hi, after)
        start = lo * (hidden // tiles)
        return (outs[1], swap(outs[0]), start, hidden, batch, rows), outs[-1], [t]

    cut = -(-tiles // 2)
    token = folded(0, 1, token)
    first, left1, token = batch_forward(0, 0, tiles, token)
    token = folded(1, 1, token)
    token = folded(0, 2, token)
    second, left2, token = batch_forward(1, 0, cut, token)
    token = folded(1, 2, token)
    outputs, token = combine(idx, *first, [], token)
    third, _, token = batch_forward(1, cut, tiles, token)
    for step in range(3, bits):
        for p in range(PIECES):
            token = folded(p, step, token)
    right, token = last_right(idx, rights[0], msgs[0], token)
    right_got = swap(right)
    outputs, token = combine(idx, *second, [outputs], token)
    outputs, token = combine(idx, *third, [outputs], token)
    part, token = sketch_part(idx, [left1, left2], right, right_got, rows, token)
    input_grad = finish(idx, keeps, msgs, token)
    part = (part + swap(part)) * (1.0 / LEN**0.5)
    sketches = part.reshape(part.shape[0], -1)
    return (outputs, input_grad, sketches)


def solution(mesh):
    placed = (
        P(("groups", "outp"), "inp"),
        P(("groups", "inp"), "outp"),
        P("inp", "outp"),
        P(None, "inp"),
        P(None, "outp"),
    )
    return jax.shard_map(
        body,
        mesh=mesh,
        in_specs=placed,
        out_specs=(P(("groups", "inp"), "outp"), P(("groups", "outp"), "inp"), P("groups", None)),
        check_vma=False,
    )
```

```python
import jax
import jax.numpy as jnp
from jax import lax
from jax.experimental import pallas as pl
from jax.experimental.pallas import tpu as pltpu
from jax.sharding import PartitionSpec as P

LEN = 128
LANES = 128
BLK = 16
LN2 = 0.6931471805599453
SPAN = 248.0
SHIFT = 124.0
PIECES = 2
F_TILE = 512
H_TILE = 512
VMEM_MIB = {"backward": 36, "forward": 28}
MIB = 1 << 20
SLOTS = 3
RIGHT_ROWS = 16
RIGHT_PARTS = 2
TIMES = {"gate": 0, "backward_0": 19 * 10**9, "backward_4": 10 * 10**9, "forward": 1 << 34, "fold": 0, "combine": 1 << 34, "sketch_part": 1 << 34}
ANY = pl.BlockSpec(memory_space=pl.ANY)
HBM = pl.BlockSpec(memory_space=pltpu.HBM)


def pick(extent, cap):
    best = LANES
    for t in range(LANES, min(cap, extent) + 1, LANES):
        if extent % t == 0:
            best = t
    return best


def contract_last(a, b):
    return lax.dot_general(a, b, (((1,), (1,)), ((), ())), preferred_element_type=jnp.float32)


def whole(shape):
    return pl.BlockSpec(shape, lambda *_: (0,) * len(shape))


def call(
    kernel, idx, args, specs, out_shape, out_specs, name, grid, work, after, scratch=(), aliases=None
):
    token = jax.ShapeDtypeStruct((8, LANES), jnp.float32)
    n_args, n_after, n_out = len(args), len(after), len(out_shape)

    def with_token(idx, *refs):
        ins = refs[:n_args]
        outs = refs[n_args + n_after :]
        outs[n_out][...] = jnp.zeros((8, LANES), jnp.float32)
        kernel(idx, *ins, *outs[:n_out], *outs[n_out + 1 :])

    out = pl.pallas_call(
        with_token,
        out_shape=list(out_shape) + [token],
        grid_spec=pltpu.PrefetchScalarGridSpec(
            num_scalar_prefetch=1,
            grid=grid,
            in_specs=list(specs) + [ANY] * n_after,
            out_specs=list(out_specs) + [whole(token.shape)],
            scratch_shapes=list(scratch),
        ),
        compiler_params=pltpu.CompilerParams(vmem_limit_bytes=VMEM_MIB.get(name.split("_")[0], 14) * MIB),
        cost_estimate=pl.CostEstimate(
            flops=TIMES.get(name, work[0]), bytes_accessed=work[1], transcendentals=0
        ),
        input_output_aliases=aliases or {},
        name=name,
    )(idx, *args, *after)
    return out[:-1], out[-1]


def encode_rows(tiles, msg, at):
    top = jnp.abs(tiles[0])
    for v in tiles[1:]:
        top = jnp.maximum(top, jnp.abs(v))
    top = jnp.max(top, axis=1, keepdims=True)
    scale = jnp.maximum(top * 1.004, 2.0**-110).astype(jnp.bfloat16).astype(jnp.float32)
    gain = SPAN / scale
    col = 0
    for v in tiles:
        w = jnp.exp2(jnp.abs(v) * gain - SHIFT)
        msg[at, col : col + v.shape[1]] = jnp.where(v < 0, -w, w).astype(jnp.bfloat16)
        col += v.shape[1]
    msg[at, col : col + LANES] = jnp.broadcast_to(scale, (BLK, LANES)).astype(jnp.bfloat16)


def decode_rows(msg, at, tile, count):
    scale = msg[at, tile * count : tile * count + LANES].astype(jnp.float32)[:, :1]
    scale = scale * (1.0 / (SPAN * LN2))
    out = []
    for t in range(count):
        w = msg[at, t * tile : (t + 1) * tile].astype(jnp.float32)
        a = (lax.log(jnp.maximum(jnp.abs(w), 2.0**-SHIFT)) + SHIFT * LN2) * scale
        out.append(jnp.where(w < 0, -a, a))
    return out


def put_right(value, msg):
    base = msg.shape[0] - RIGHT_ROWS
    for q in range(value.shape[0] // RIGHT_ROWS):
        left_over = value[q * RIGHT_ROWS : (q + 1) * RIGHT_ROWS, :]
        for k in range(RIGHT_PARTS):
            part = left_over.astype(jnp.bfloat16)
            lo = (RIGHT_PARTS * q + k) * LANES
            msg[base:, lo : lo + LANES] = part
            left_over = left_over - part.astype(jnp.float32)


def add_right(value, msg):
    base = msg.shape[0] - RIGHT_ROWS
    out = []
    for q in range(value.shape[0] // RIGHT_ROWS):
        lo = RIGHT_PARTS * q * LANES
        parts = [
            msg[base:, lo + k * LANES : lo + (k + 1) * LANES].astype(jnp.float32)
            for k in range(RIGHT_PARTS)
        ]
        got = sum(parts)
        out.append(value[q * RIGHT_ROWS : (q + 1) * RIGHT_ROWS, :] + got)
    return jnp.concatenate(out, axis=0)


def with_bit(c, pos, value):
    low = c & ((1 << pos) - 1)
    return ((c >> pos) << (pos + 1)) + low + value * (1 << pos)


def rows_at(start):
    return pl.ds(pl.multiple_of(start, BLK), BLK)


def backward(idx, own, oth, w, sketch, count, tile, first, rows, bit, after):
    half, hidden = own.shape
    n = 2 * half // rows
    width = count * tile

    def kernel(idx, own, oth, w, *rest):
        if sketch is None:
            msg, keep, x, total, sems, tiles = rest
        else:
            sk, msg, keep, right, x, total, sems, tiles, sk_here = rest
        me, core = idx[0], idx[1]

        def fetch(j):
            at = pl.ds(pl.multiple_of((first + j) * tile, tile), tile)
            slot = lax.rem(j, SLOTS)
            return pltpu.make_async_copy(w.at[at], tiles.at[slot], sems.at[3 + slot])

        copies = [
            pltpu.make_async_copy(own, x.at[core], sems.at[0]),
            pltpu.make_async_copy(oth, x.at[1 - core], sems.at[1]),
        ]
        if sketch is not None:
            copies.append(pltpu.make_async_copy(sk, sk_here, sems.at[2]))
        for c in copies:
            c.start()
        for j in range(min(SLOTS - 1, count)):
            fetch(jnp.int32(j)).start()
        for c in copies:
            c.wait()
        if sketch is not None:
            low, high = jnp.zeros_like(sk_here[...]), sk_here[...]
            first_block = jnp.concatenate([high, low], axis=0)
            second_block = jnp.concatenate([low, high], axis=0)
            right[...] = contract_last(x[core, : half // 2, :], first_block) + contract_last(
                x[core, half // 2 :, :], second_block
            )
            put_right(right[...], msg)

        @pl.loop(0, count)
        def _(j):
            fetch(j).wait()

            @pl.when(j + SLOTS - 1 < count)
            def _():
                fetch(j + SLOTS - 1).start()

            xs = x[...].reshape(2 * half, hidden)
            total[j] = contract_last(xs, tiles[lax.rem(j, SLOTS)]).reshape(n, rows, tile)

        mine = (me >> bit) & 1
        for c in range(n // 2):
            away, here = with_bit(c, bit, 1 - mine), with_bit(c, bit, mine)

            @pl.loop(0, rows // BLK)
            def _(b):
                src = rows_at(b * BLK)
                encode_rows(
                    [total[t, away, src, :] for t in range(count)],
                    msg,
                    rows_at(c * rows + b * BLK),
                )
                for t in range(count):
                    keep[t, c, src, :] = total[t, here, src, :]

    extra = 0 if sketch is None else RIGHT_ROWS
    out = [
        jax.ShapeDtypeStruct((n // 2 * rows + extra, width + LANES), jnp.bfloat16),
        jax.ShapeDtypeStruct((count, n // 2, rows, tile), jnp.float32),
    ]
    args = [own, oth, w]
    specs = [HBM, ANY, HBM]
    scratch = [
        pltpu.VMEM((2, half, hidden), jnp.bfloat16),
        pltpu.VMEM((count, n, rows, tile), jnp.float32),
        pltpu.SemaphoreType.DMA((3 + SLOTS,)),
        pltpu.VMEM((SLOTS, tile, hidden), w.dtype),
    ]
    if sketch is not None:
        args.append(sketch)
        specs.append(HBM)
        out.append(jax.ShapeDtypeStruct((half // 2, 2 * sketch.shape[0]), jnp.float32))
        scratch.append(pltpu.VMEM(sketch.shape, sketch.dtype))
    return call(
        kernel,
        idx,
        args,
        specs,
        out,
        [whole(o.shape) for o in out],
        f"backward_{first}",
        (1,),
        (4 * half * hidden * width, 2 * hidden * width + 12 * half * width),
        after,
        scratch,
    )


def fold(idx, keep, got, right, bit, pos, after):
    count, m, rows, tile = keep.shape
    extra = 0 if right is None else RIGHT_ROWS

    def kernel(idx, keep, got, *refs):
        if extra:
            right, msg, rest, total = refs
            total[...] = add_right(right[...], got)
            put_right(total[...], msg)
        else:
            msg, rest = refs
        mine = (idx[0] >> bit) & 1
        for c in range(m // 2):
            away, here = with_bit(c, pos, 1 - mine), with_bit(c, pos, mine)

            @pl.loop(0, rows // BLK)
            def _(b):
                src = rows_at(b * BLK)
                plus = decode_rows(got, rows_at(away * rows + b * BLK), tile, count)
                encode_rows(
                    [keep[t, away, src, :] + plus[t] for t in range(count)],
                    msg,
                    rows_at(c * rows + b * BLK),
                )
                plus = decode_rows(got, rows_at(here * rows + b * BLK), tile, count)
                for t in range(count):
                    rest[t, c, src, :] = keep[t, here, src, :] + plus[t]

    args = [keep, got] + ([right] if extra else [])
    out = [
        jax.ShapeDtypeStruct((m // 2 * rows + extra, got.shape[1]), jnp.bfloat16),
        jax.ShapeDtypeStruct((count, m // 2, rows, tile), jnp.float32),
    ] + ([jax.ShapeDtypeStruct(right.shape, jnp.float32)] if extra else [])
    return call(
        kernel,
        idx,
        args,
        [whole(a.shape) for a in args],
        out,
        [whole(o.shape) for o in out],
        "fold",
        (1,),
        (0, 12 * keep.size),
        after,
    )


def finish(idx, keeps, gots, after):
    count, _, rows, tile = keeps[0].shape
    pieces = len(keeps)

    def kernel(idx, *refs):
        out = refs[-1]
        for p in range(pieces):

            @pl.loop(0, rows // BLK)
            def _(b):
                at = rows_at(b * BLK)
                plus = decode_rows(refs[pieces + p], at, tile, count)
                for t in range(count):
                    lo = (p * count + t) * tile
                    out[at, lo : lo + tile] = (refs[p][t, 0, at, :] + plus[t]).astype(
                        jnp.bfloat16
                    )

    args = list(keeps) + list(gots)
    out = [jax.ShapeDtypeStruct((rows, pieces * count * tile), jnp.bfloat16)]
    (grad,), _ = call(
        kernel,
        idx,
        args,
        [whole(a.shape) for a in args],
        out,
        [whole(out[0].shape)],
        "finish",
        (1,),
        (0, 16 * rows * count * tile),
        after,
    )
    return grad


def gate(idx, arrays, after):
    k = len(arrays)

    def kernel(idx, *refs):
        pass

    out, token = call(
        kernel,
        idx,
        arrays,
        [ANY] * k,
        [jax.ShapeDtypeStruct(a.shape, a.dtype) for a in arrays],
        [ANY] * k,
        "gate",
        (1,),
        (0, 0),
        after,
        aliases={1 + i: i for i in range(k)},
    )
    return list(out), [token]


def join(idx, arrays, after):
    rows, width = arrays[0].shape
    k = len(arrays)

    def kernel(idx, *refs):
        out, sems = refs[-2:]
        copies = [
            pltpu.make_async_copy(refs[i], out.at[pl.ds(i * rows, rows)], sems.at[i])
            for i in range(k)
        ]
        for c in copies:
            c.start()
        for c in copies:
            c.wait()

    (out,), token = call(
        kernel,
        idx,
        arrays,
        [ANY] * k,
        [jax.ShapeDtypeStruct((k * rows, width), arrays[0].dtype)],
        [ANY],
        "join",
        (1,),
        (0, 0),
        after,
        [pltpu.SemaphoreType.DMA((k,))],
    )
    return out, [token]


def last_right(idx, right, got, after):
    def kernel(idx, right, got, out):
        out[...] = add_right(right[...], got)

    out = [jax.ShapeDtypeStruct(right.shape, jnp.float32)]
    specs = [whole(right.shape), whole(got.shape)]
    work = (0, 2 * got.size)
    (total,), token = call(
        kernel, idx, [right, got], specs, out, specs[:1], "last_right", (1,), work, after
    )
    return total, [token]


def forward(idx, chunks, rows, w, sketch, lo, hi, after):
    feats = w.shape[0]
    m = len(chunks)
    tile = pick(w.shape[1], H_TILE)
    hidden = (hi - lo) * tile
    part = m // 2 * rows

    count = hi - lo

    def kernel(idx, *refs):
        if sketch is None:
            w, send, keep, x, sems, tiles, outs, out_sems = refs[m:]
        else:
            w, sk, send, keep, left, x, sems, tiles, outs, out_sems = refs[m:]
        me, core = idx[0], idx[1]

        def fetch(j):
            at = pl.ds(pl.multiple_of((lo + j) * tile, tile), tile)
            slot = lax.rem(j, SLOTS)
            return pltpu.make_async_copy(w.at[:, at], tiles.at[slot], sems.at[m + slot])

        def give(j):
            at = pl.ds(pl.multiple_of(j * tile, tile), tile)
            slot = lax.rem(j, 2)
            return [
                pltpu.make_async_copy(outs.at[slot, side], ref.at[:, at], out_sems.at[slot, side])
                for side, ref in enumerate((send, keep))
            ]

        copies = []
        for i, (mask, _, block) in enumerate(chunks):
            d = me ^ mask
            side = 1 - ((d // m) ^ core)
            to = pl.ds(pl.multiple_of(side * part + ((d % m) >> 1) * rows, BLK), rows)
            src = refs[i].at[pl.ds(block * rows, rows)]
            copies.append(pltpu.make_async_copy(src, x.at[to], sems.at[i]))
        for c in copies:
            c.start()
        for j in range(min(SLOTS - 1, count)):
            fetch(jnp.int32(j)).start()
        for c in copies:
            c.wait()
        if sketch is not None:
            left[...] = contract_last(x[...], sk[...])

        @pl.loop(0, count)
        def _(j):
            fetch(j).wait()

            @pl.when(j + SLOTS - 1 < count)
            def _():
                fetch(j + SLOTS - 1).start()

            t = jnp.dot(x[...], tiles[lax.rem(j, SLOTS)], preferred_element_type=jnp.float32)

            @pl.when(j >= 2)
            def _():
                for c in give(j - 2):
                    c.wait()

            outs[lax.rem(j, 2)] = t.reshape(2, part, tile)
            for c in give(j):
                c.start()

        for j in range(max(0, count - 2), count):
            for c in give(jnp.int32(j)):
                c.wait()

    args = [c[1] for c in chunks] + [w]
    specs = [ANY] * m + [HBM]
    out = [jax.ShapeDtypeStruct((part, hidden), jnp.float32)] * 2
    out_specs = [ANY, ANY]
    if sketch is not None:
        args.append(sketch)
        specs.append(whole(sketch.shape))
        out.append(jax.ShapeDtypeStruct((2 * part, sketch.shape[0]), jnp.float32))
        out_specs.append(whole(out[2].shape))
    return call(
        kernel,
        idx,
        args,
        specs,
        out,
        out_specs,
        "forward",
        (1,),
        (4 * part * feats * hidden, 2 * feats * hidden + 8 * part * hidden),
        after,
        [
            pltpu.VMEM((2 * part, feats), jnp.bfloat16),
            pltpu.SemaphoreType.DMA((m + SLOTS,)),
            pltpu.VMEM((SLOTS, feats, tile), w.dtype),
            pltpu.VMEM((2, 2, part, tile), jnp.float32),
            pltpu.SemaphoreType.DMA((2, 2)),
        ],
    )


def combine(idx, keep, got, lo, total, batch, rows, before, after):
    part, width = keep.shape
    m = part // rows
    slices = max(k for k in (1, 2, 4) if width % (k * LANES) == 0)
    span = width // slices

    def kernel(idx, keep, got, *refs):
        out, a, b, x, in_sems, out_sems = refs[-6:]
        mine = (idx[0] & 1) ^ batch
        loads, stores = [], []
        for k in range(slices):
            cols = pl.ds(k * span, span)
            loads.append(
                [
                    pltpu.make_async_copy(keep.at[:, cols], a.at[k], in_sems.at[k, 0]),
                    pltpu.make_async_copy(got.at[:, cols], b.at[k], in_sems.at[k, 1]),
                ]
            )
            for c in loads[k]:
                c.start()
        for k in range(slices):
            for c in loads[k]:
                c.wait()
            x[k] = (a[k] + b[k]).astype(jnp.bfloat16)
            for i in range(m):
                to = pl.ds(pl.multiple_of((2 * i + mine) * rows, BLK), rows)
                dst = out.at[to, pl.ds(lo + k * span, span)]
                src = x.at[k, pl.ds(i * rows, rows)]
                stores.append(pltpu.make_async_copy(src, dst, out_sems.at[k, i]))
                stores[-1].start()
        for c in stores:
            c.wait()

    (out,), token = call(
        kernel,
        idx,
        [keep, got] + before,
        [ANY] * 2 + [HBM] * len(before),
        [jax.ShapeDtypeStruct((2 * part, total), jnp.bfloat16)],
        [HBM],
        "combine",
        (1,),
        (0, 10 * part * width),
        after,
        [
            pltpu.VMEM((slices, part, span), jnp.float32),
            pltpu.VMEM((slices, part, span), jnp.float32),
            pltpu.VMEM((slices, part, span), jnp.bfloat16),
            pltpu.SemaphoreType.DMA((slices, 2)),
            pltpu.SemaphoreType.DMA((slices, m)),
        ],
        aliases={3: 0} if before else None,
    )
    return out, [token]


def sketch_part(idx, lefts, own, oth, rows, after):
    packed, lanes = own.shape
    width = lanes // 2
    half = 2 * packed
    part = half // 2
    examples = half // LEN

    def kernel(idx, first, second, own, oth, out):
        me, core = idx[0], idx[1]
        for side, right in ((0, oth), (1, own)):
            owner = 1 - (side ^ core)
            for e in range(examples):
                total = jnp.zeros((width, width), jnp.float32)
                for i in range(part // rows):
                    if 2 * i * rows // LEN != e:
                        continue
                    block, start = divmod(2 * i * rows, packed)
                    for batch, left in enumerate((first, second)):
                        at = start + ((me & 1) ^ batch) * rows
                        lo = side * part + i * rows
                        both = right[pl.ds(pl.multiple_of(at, BLK), rows), :]
                        total += lax.dot_general(
                            left[lo : lo + rows, :],
                            both[:, block * width : (block + 1) * width],
                            (((0,), (0,)), ((), ())),
                            precision=lax.Precision.HIGHEST,
                            preferred_element_type=jnp.float32,
                        )
                out[owner * examples + e] = total

    args = [*lefts, own, oth]
    out = [jax.ShapeDtypeStruct((2 * examples, width, width), jnp.float32)]
    (sketch,), token = call(
        kernel,
        idx,
        args,
        [whole(a.shape) for a in args],
        out,
        [whole(out[0].shape)],
        "sketch_part",
        (1,),
        (0, 16 * half * width),
        after,
    )
    return sketch, [token]


def body(inputs, cotangent, weight, in_sketch, out_sketch):
    n = lax.axis_size("outp")
    bits = n.bit_length() - 1
    rows, feats = inputs.shape
    hidden = weight.shape[1]
    idx = jnp.stack([lax.axis_index("outp"), lax.axis_index("inp")]).astype(jnp.int32)

    def partner(x, bit):
        return lax.ppermute(x, "outp", [(d, d ^ (1 << bit)) for d in range(n)])

    def swap(x):
        return lax.ppermute(x, "inp", [(0, 1), (1, 0)])

    evens = list(range(2, n, 2))
    chunks = {0: inputs}

    def fetch(masks):
        for mask in masks:
            bit = (mask & -mask).bit_length() - 1
            chunks[mask] = partner(chunks[mask ^ (1 << bit)], bit)

    def hold(masks, after):
        held, token = gate(idx, [chunks[m] for m in masks], after)
        chunks.update(zip(masks, held))
        return token

    grad_other = swap(cotangent)
    singles = [1 << k for k in reversed(range(bits))]
    fetch(singles)

    orders = [list(range(bits)), [1, 0] + list(range(2, bits))]
    tile = pick(feats // PIECES, F_TILE)
    count = feats // PIECES // tile
    msgs, keeps = [], []
    token = []
    for p in range(PIECES):
        outs, t = backward(
            idx,
            cotangent,
            grad_other,
            weight,
            out_sketch if p == 0 else None,
            count,
            tile,
            p * count,
            rows,
            orders[p][0],
            token,
        )
        token = [t]
        msgs.append(partner(outs[0], orders[p][0]))
        keeps.append(outs[1])
        if p == 0:
            right = outs[2]
        if p == 0:
            token = hold(singles, token)
            fetch([m for m in evens if m.bit_count() == 2])
    ready = [m for m in evens if m in chunks]
    while len(ready) < len(evens):
        token = hold(ready, token)
        fetch([m for m in evens if m not in chunks and m & (m - 1) in chunks])
        ready = [m for m in evens if m in chunks]
    crossed, token = join(idx, [chunks[m] for m in evens], token)
    crossed = partner(crossed, 0)

    rights = [right] + [None] * (PIECES - 1)

    def folded(p, step, after):
        done, bit = orders[p][:step], orders[p][step]
        pos = sum(1 for k in range(bit) if k not in done)
        outs, t = fold(idx, keeps[p], msgs[p], rights[p], bit, pos, after)
        msgs[p], keeps[p] = partner(outs[0], bit), outs[1]
        if p == 0:
            rights[p] = outs[2]
        return [t]

    tiles = hidden // pick(hidden, H_TILE)

    def batch_forward(batch, lo, hi, after):
        if batch:
            parts = [(1, chunks[1], 0)] + [(m + 1, crossed, i) for i, m in enumerate(evens)]
        else:
            parts = [(m, chunks[m], 0) for m in [0] + evens]
        outs, t = forward(idx, parts, rows, weight, None if lo else in_sketch, lo, hi, after)
        start = lo * (hidden // tiles)
        return (outs[1], swap(outs[0]), start, hidden, batch, rows), outs[-1], [t]

    cut = -(-tiles // 2)
    token = folded(0, 1, token)
    first, left1, token = batch_forward(0, 0, tiles, token)
    token = folded(1, 1, token)
    token = folded(0, 2, token)
    second, left2, token = batch_forward(1, 0, cut, token)
    token = folded(1, 2, token)
    outputs, token = combine(idx, *first, [], token)
    right, token = last_right(idx, rights[0], msgs[0], token)
    right_got = swap(right)
    third, _, token = batch_forward(1, cut, tiles, token)
    for step in range(3, bits):
        for p in range(PIECES):
            token = folded(p, step, token)
    part, token = sketch_part(idx, [left1, left2], right, right_got, rows, token)
    outputs, token = combine(idx, *second, [outputs], token)
    outputs, token = combine(idx, *third, [outputs], token)
    input_grad = finish(idx, keeps, msgs, token)
    part = (part + swap(part)) * (1.0 / LEN**0.5)
    sketches = part.reshape(part.shape[0], -1)
    return (outputs, input_grad, sketches)


def solution(mesh):
    placed = (
        P(("groups", "outp"), "inp"),
        P(("groups", "inp"), "outp"),
        P("inp", "outp"),
        P(None, "inp"),
        P(None, "outp"),
    )
    return jax.shard_map(
        body,
        mesh=mesh,
        in_specs=placed,
        out_specs=(P(("groups", "inp"), "outp"), P(("groups", "outp"), "inp"), P("groups", None)),
        check_vma=False,
    )
```

```python
import jax
import jax.numpy as jnp
from jax import lax
from jax.experimental import pallas as pl
from jax.experimental.pallas import tpu as pltpu
from jax.sharding import PartitionSpec as P

LEN = 128
LANES = 128
BLK = 16
LN2 = 0.6931471805599453
SPAN = 248.0
SHIFT = 124.0
PIECES = 2
F_TILE = 512
H_TILE = 512
VMEM_MIB = {"backward": 36, "forward": 28}
MIB = 1 << 20
SLOTS = 3
RIGHT_ROWS = 16
RIGHT_PARTS = 2
TIMES = {"gate": 0, "backward_0": 19 * 10**9, "backward_4": 10 * 10**9, "forward": 1 << 34, "fold": 0, "combine": 1 << 34, "sketch_part": 1 << 36, "last_right": 1 << 34}
ANY = pl.BlockSpec(memory_space=pl.ANY)
HBM = pl.BlockSpec(memory_space=pltpu.HBM)


def pick(extent, cap):
    best = LANES
    for t in range(LANES, min(cap, extent) + 1, LANES):
        if extent % t == 0:
            best = t
    return best


def contract_last(a, b):
    return lax.dot_general(a, b, (((1,), (1,)), ((), ())), preferred_element_type=jnp.float32)


def whole(shape):
    return pl.BlockSpec(shape, lambda *_: (0,) * len(shape))


def call(
    kernel, idx, args, specs, out_shape, out_specs, name, grid, work, after, scratch=(), aliases=None
):
    token = jax.ShapeDtypeStruct((8, LANES), jnp.float32)
    n_args, n_after, n_out = len(args), len(after), len(out_shape)

    def with_token(idx, *refs):
        ins = refs[:n_args]
        outs = refs[n_args + n_after :]
        outs[n_out][...] = jnp.zeros((8, LANES), jnp.float32)
        kernel(idx, *ins, *outs[:n_out], *outs[n_out + 1 :])

    out = pl.pallas_call(
        with_token,
        out_shape=list(out_shape) + [token],
        grid_spec=pltpu.PrefetchScalarGridSpec(
            num_scalar_prefetch=1,
            grid=grid,
            in_specs=list(specs) + [ANY] * n_after,
            out_specs=list(out_specs) + [whole(token.shape)],
            scratch_shapes=list(scratch),
        ),
        compiler_params=pltpu.CompilerParams(vmem_limit_bytes=VMEM_MIB.get(name.split("_")[0], 14) * MIB),
        cost_estimate=pl.CostEstimate(
            flops=TIMES.get(name, work[0]), bytes_accessed=work[1], transcendentals=0
        ),
        input_output_aliases=aliases or {},
        name=name,
    )(idx, *args, *after)
    return out[:-1], out[-1]


def encode_rows(tiles, msg, at):
    top = jnp.abs(tiles[0])
    for v in tiles[1:]:
        top = jnp.maximum(top, jnp.abs(v))
    top = jnp.max(top, axis=1, keepdims=True)
    scale = jnp.maximum(top * 1.004, 2.0**-110).astype(jnp.bfloat16).astype(jnp.float32)
    gain = SPAN / scale
    col = 0
    for v in tiles:
        w = jnp.exp2(jnp.abs(v) * gain - SHIFT)
        msg[at, col : col + v.shape[1]] = jnp.where(v < 0, -w, w).astype(jnp.bfloat16)
        col += v.shape[1]
    msg[at, col : col + LANES] = jnp.broadcast_to(scale, (BLK, LANES)).astype(jnp.bfloat16)


def decode_rows(msg, at, tile, count):
    scale = msg[at, tile * count : tile * count + LANES].astype(jnp.float32)[:, :1]
    scale = scale * (1.0 / (SPAN * LN2))
    out = []
    for t in range(count):
        w = msg[at, t * tile : (t + 1) * tile].astype(jnp.float32)
        a = (lax.log(jnp.maximum(jnp.abs(w), 2.0**-SHIFT)) + SHIFT * LN2) * scale
        out.append(jnp.where(w < 0, -a, a))
    return out


def put_right(value, msg):
    base = msg.shape[0] - RIGHT_ROWS
    for q in range(value.shape[0] // RIGHT_ROWS):
        left_over = value[q * RIGHT_ROWS : (q + 1) * RIGHT_ROWS, :]
        for k in range(RIGHT_PARTS):
            part = left_over.astype(jnp.bfloat16)
            lo = (RIGHT_PARTS * q + k) * LANES
            msg[base:, lo : lo + LANES] = part
            left_over = left_over - part.astype(jnp.float32)


def add_right(value, msg):
    base = msg.shape[0] - RIGHT_ROWS
    out = []
    for q in range(value.shape[0] // RIGHT_ROWS):
        lo = RIGHT_PARTS * q * LANES
        parts = [
            msg[base:, lo + k * LANES : lo + (k + 1) * LANES].astype(jnp.float32)
            for k in range(RIGHT_PARTS)
        ]
        got = sum(parts)
        out.append(value[q * RIGHT_ROWS : (q + 1) * RIGHT_ROWS, :] + got)
    return jnp.concatenate(out, axis=0)


def with_bit(c, pos, value):
    low = c & ((1 << pos) - 1)
    return ((c >> pos) << (pos + 1)) + low + value * (1 << pos)


def rows_at(start):
    return pl.ds(pl.multiple_of(start, BLK), BLK)


def backward(idx, own, oth, w, sketch, count, tile, first, rows, bit, after):
    half, hidden = own.shape
    n = 2 * half // rows
    width = count * tile

    def kernel(idx, own, oth, w, *rest):
        if sketch is None:
            msg, keep, x, total, sems, tiles = rest
        else:
            sk, msg, keep, right, x, total, sems, tiles, sk_here = rest
        me, core = idx[0], idx[1]

        def fetch(j):
            at = pl.ds(pl.multiple_of((first + j) * tile, tile), tile)
            slot = lax.rem(j, SLOTS)
            return pltpu.make_async_copy(w.at[at], tiles.at[slot], sems.at[3 + slot])

        copies = [
            pltpu.make_async_copy(own, x.at[core], sems.at[0]),
            pltpu.make_async_copy(oth, x.at[1 - core], sems.at[1]),
        ]
        if sketch is not None:
            copies.append(pltpu.make_async_copy(sk, sk_here, sems.at[2]))
        for c in copies:
            c.start()
        for j in range(min(SLOTS - 1, count)):
            fetch(jnp.int32(j)).start()
        for c in copies:
            c.wait()
        if sketch is not None:
            low, high = jnp.zeros_like(sk_here[...]), sk_here[...]
            first_block = jnp.concatenate([high, low], axis=0)
            second_block = jnp.concatenate([low, high], axis=0)
            right[...] = contract_last(x[core, : half // 2, :], first_block) + contract_last(
                x[core, half // 2 :, :], second_block
            )
            put_right(right[...], msg)

        @pl.loop(0, count)
        def _(j):
            fetch(j).wait()

            @pl.when(j + SLOTS - 1 < count)
            def _():
                fetch(j + SLOTS - 1).start()

            xs = x[...].reshape(2 * half, hidden)
            total[j] = contract_last(xs, tiles[lax.rem(j, SLOTS)]).reshape(n, rows, tile)

        mine = (me >> bit) & 1
        for c in range(n // 2):
            away, here = with_bit(c, bit, 1 - mine), with_bit(c, bit, mine)

            @pl.loop(0, rows // BLK)
            def _(b):
                src = rows_at(b * BLK)
                encode_rows(
                    [total[t, away, src, :] for t in range(count)],
                    msg,
                    rows_at(c * rows + b * BLK),
                )
                for t in range(count):
                    keep[t, c, src, :] = total[t, here, src, :]

    extra = 0 if sketch is None else RIGHT_ROWS
    out = [
        jax.ShapeDtypeStruct((n // 2 * rows + extra, width + LANES), jnp.bfloat16),
        jax.ShapeDtypeStruct((count, n // 2, rows, tile), jnp.float32),
    ]
    args = [own, oth, w]
    specs = [HBM, ANY, HBM]
    scratch = [
        pltpu.VMEM((2, half, hidden), jnp.bfloat16),
        pltpu.VMEM((count, n, rows, tile), jnp.float32),
        pltpu.SemaphoreType.DMA((3 + SLOTS,)),
        pltpu.VMEM((SLOTS, tile, hidden), w.dtype),
    ]
    if sketch is not None:
        args.append(sketch)
        specs.append(HBM)
        out.append(jax.ShapeDtypeStruct((half // 2, 2 * sketch.shape[0]), jnp.float32))
        scratch.append(pltpu.VMEM(sketch.shape, sketch.dtype))
    return call(
        kernel,
        idx,
        args,
        specs,
        out,
        [whole(o.shape) for o in out],
        f"backward_{first}",
        (1,),
        (4 * half * hidden * width, 2 * hidden * width + 12 * half * width),
        after,
        scratch,
    )


def fold(idx, keep, got, right, bit, pos, after):
    count, m, rows, tile = keep.shape
    extra = 0 if right is None else RIGHT_ROWS

    def kernel(idx, keep, got, *refs):
        if extra:
            right, msg, rest, total = refs
            total[...] = add_right(right[...], got)
            put_right(total[...], msg)
        else:
            msg, rest = refs
        mine = (idx[0] >> bit) & 1
        for c in range(m // 2):
            away, here = with_bit(c, pos, 1 - mine), with_bit(c, pos, mine)

            @pl.loop(0, rows // BLK)
            def _(b):
                src = rows_at(b * BLK)
                plus = decode_rows(got, rows_at(away * rows + b * BLK), tile, count)
                encode_rows(
                    [keep[t, away, src, :] + plus[t] for t in range(count)],
                    msg,
                    rows_at(c * rows + b * BLK),
                )
                plus = decode_rows(got, rows_at(here * rows + b * BLK), tile, count)
                for t in range(count):
                    rest[t, c, src, :] = keep[t, here, src, :] + plus[t]

    args = [keep, got] + ([right] if extra else [])
    out = [
        jax.ShapeDtypeStruct((m // 2 * rows + extra, got.shape[1]), jnp.bfloat16),
        jax.ShapeDtypeStruct((count, m // 2, rows, tile), jnp.float32),
    ] + ([jax.ShapeDtypeStruct(right.shape, jnp.float32)] if extra else [])
    return call(
        kernel,
        idx,
        args,
        [whole(a.shape) for a in args],
        out,
        [whole(o.shape) for o in out],
        "fold",
        (1,),
        (0, 12 * keep.size),
        after,
    )


def finish(idx, keeps, gots, after):
    count, _, rows, tile = keeps[0].shape
    pieces = len(keeps)

    def kernel(idx, *refs):
        out = refs[-1]
        for p in range(pieces):

            @pl.loop(0, rows // BLK)
            def _(b):
                at = rows_at(b * BLK)
                plus = decode_rows(refs[pieces + p], at, tile, count)
                for t in range(count):
                    lo = (p * count + t) * tile
                    out[at, lo : lo + tile] = (refs[p][t, 0, at, :] + plus[t]).astype(
                        jnp.bfloat16
                    )

    args = list(keeps) + list(gots)
    out = [jax.ShapeDtypeStruct((rows, pieces * count * tile), jnp.bfloat16)]
    (grad,), _ = call(
        kernel,
        idx,
        args,
        [whole(a.shape) for a in args],
        out,
        [whole(out[0].shape)],
        "finish",
        (1,),
        (0, 16 * rows * count * tile),
        after,
    )
    return grad


def gate(idx, arrays, after):
    k = len(arrays)

    def kernel(idx, *refs):
        pass

    out, token = call(
        kernel,
        idx,
        arrays,
        [ANY] * k,
        [jax.ShapeDtypeStruct(a.shape, a.dtype) for a in arrays],
        [ANY] * k,
        "gate",
        (1,),
        (0, 0),
        after,
        aliases={1 + i: i for i in range(k)},
    )
    return list(out), [token]


def join(idx, arrays, after):
    rows, width = arrays[0].shape
    k = len(arrays)

    def kernel(idx, *refs):
        out, sems = refs[-2:]
        copies = [
            pltpu.make_async_copy(refs[i], out.at[pl.ds(i * rows, rows)], sems.at[i])
            for i in range(k)
        ]
        for c in copies:
            c.start()
        for c in copies:
            c.wait()

    (out,), token = call(
        kernel,
        idx,
        arrays,
        [ANY] * k,
        [jax.ShapeDtypeStruct((k * rows, width), arrays[0].dtype)],
        [ANY],
        "join",
        (1,),
        (0, 0),
        after,
        [pltpu.SemaphoreType.DMA((k,))],
    )
    return out, [token]


def last_right(idx, right, got, after):
    def kernel(idx, right, got, out):
        out[...] = add_right(right[...], got)

    out = [jax.ShapeDtypeStruct(right.shape, jnp.float32)]
    specs = [whole(right.shape), whole(got.shape)]
    work = (0, 2 * got.size)
    (total,), token = call(
        kernel, idx, [right, got], specs, out, specs[:1], "last_right", (1,), work, after
    )
    return total, [token]


def forward(idx, chunks, rows, w, sketch, lo, hi, after):
    feats = w.shape[0]
    m = len(chunks)
    tile = pick(w.shape[1], H_TILE)
    hidden = (hi - lo) * tile
    part = m // 2 * rows

    count = hi - lo

    def kernel(idx, *refs):
        if sketch is None:
            w, send, keep, x, sems, tiles, outs, out_sems = refs[m:]
        else:
            w, sk, send, keep, left, x, sems, tiles, outs, out_sems = refs[m:]
        me, core = idx[0], idx[1]

        def fetch(j):
            at = pl.ds(pl.multiple_of((lo + j) * tile, tile), tile)
            slot = lax.rem(j, SLOTS)
            return pltpu.make_async_copy(w.at[:, at], tiles.at[slot], sems.at[m + slot])

        def give(j):
            at = pl.ds(pl.multiple_of(j * tile, tile), tile)
            slot = lax.rem(j, 2)
            return [
                pltpu.make_async_copy(outs.at[slot, side], ref.at[:, at], out_sems.at[slot, side])
                for side, ref in enumerate((send, keep))
            ]

        copies = []
        for i, (mask, _, block) in enumerate(chunks):
            d = me ^ mask
            side = 1 - ((d // m) ^ core)
            to = pl.ds(pl.multiple_of(side * part + ((d % m) >> 1) * rows, BLK), rows)
            src = refs[i].at[pl.ds(block * rows, rows)]
            copies.append(pltpu.make_async_copy(src, x.at[to], sems.at[i]))
        for c in copies:
            c.start()
        for j in range(min(SLOTS - 1, count)):
            fetch(jnp.int32(j)).start()
        for c in copies:
            c.wait()
        if sketch is not None:
            left[...] = contract_last(x[...], sk[...])

        @pl.loop(0, count)
        def _(j):
            fetch(j).wait()

            @pl.when(j + SLOTS - 1 < count)
            def _():
                fetch(j + SLOTS - 1).start()

            t = jnp.dot(x[...], tiles[lax.rem(j, SLOTS)], preferred_element_type=jnp.float32)

            @pl.when(j >= 2)
            def _():
                for c in give(j - 2):
                    c.wait()

            outs[lax.rem(j, 2)] = t.reshape(2, part, tile)
            for c in give(j):
                c.start()

        for j in range(max(0, count - 2), count):
            for c in give(jnp.int32(j)):
                c.wait()

    args = [c[1] for c in chunks] + [w]
    specs = [ANY] * m + [HBM]
    out = [jax.ShapeDtypeStruct((part, hidden), jnp.float32)] * 2
    out_specs = [ANY, ANY]
    if sketch is not None:
        args.append(sketch)
        specs.append(whole(sketch.shape))
        out.append(jax.ShapeDtypeStruct((2 * part, sketch.shape[0]), jnp.float32))
        out_specs.append(whole(out[2].shape))
    return call(
        kernel,
        idx,
        args,
        specs,
        out,
        out_specs,
        "forward",
        (1,),
        (4 * part * feats * hidden, 2 * feats * hidden + 8 * part * hidden),
        after,
        [
            pltpu.VMEM((2 * part, feats), jnp.bfloat16),
            pltpu.SemaphoreType.DMA((m + SLOTS,)),
            pltpu.VMEM((SLOTS, feats, tile), w.dtype),
            pltpu.VMEM((2, 2, part, tile), jnp.float32),
            pltpu.SemaphoreType.DMA((2, 2)),
        ],
    )


def combine(idx, pieces, total, rows, batch, before, after):
    part = pieces[0][0].shape[0]
    m = part // rows

    def kernel(idx, *refs):
        out, sems = refs[-2 - len(pieces)], refs[-1]
        mine = (idx[0] & 1) ^ batch
        copies = []
        for k, (keep, _, lo) in enumerate(pieces):
            x = refs[k - 1 - len(pieces)]
            x[...] = (refs[2 * k][...] + refs[2 * k + 1][...]).astype(jnp.bfloat16)
            for i in range(m):
                to = pl.ds(pl.multiple_of((2 * i + mine) * rows, BLK), rows)
                dst = out.at[to, pl.ds(lo, keep.shape[1])]
                copies.append(
                    pltpu.make_async_copy(x.at[pl.ds(i * rows, rows)], dst, sems.at[k, i])
                )
                copies[-1].start()
        for c in copies:
            c.wait()

    flat = [a for keep, got, _ in pieces for a in (keep, got)]
    width = sum(keep.shape[1] for keep, _, _ in pieces)
    (out,), token = call(
        kernel,
        idx,
        flat + before,
        [whole(a.shape) for a in flat] + [HBM] * len(before),
        [jax.ShapeDtypeStruct((2 * part, total), jnp.bfloat16)],
        [HBM],
        "combine",
        (1,),
        (0, 10 * part * width),
        after,
        [pltpu.VMEM(keep.shape, jnp.bfloat16) for keep, _, _ in pieces]
        + [pltpu.SemaphoreType.DMA((len(pieces), m))],
        aliases={1 + len(flat): 0} if before else None,
    )
    return out, [token]


def sketch_part(idx, lefts, own, oth, rows, after):
    packed, lanes = own.shape
    width = lanes // 2
    half = 2 * packed
    part = half // 2
    examples = half // LEN

    def kernel(idx, first, second, own, oth, out):
        me, core = idx[0], idx[1]
        for side, right in ((0, oth), (1, own)):
            owner = 1 - (side ^ core)
            for e in range(examples):
                total = jnp.zeros((width, width), jnp.float32)
                for i in range(part // rows):
                    if 2 * i * rows // LEN != e:
                        continue
                    block, start = divmod(2 * i * rows, packed)
                    for batch, left in enumerate((first, second)):
                        at = start + ((me & 1) ^ batch) * rows
                        lo = side * part + i * rows
                        both = right[pl.ds(pl.multiple_of(at, BLK), rows), :]
                        total += lax.dot_general(
                            left[lo : lo + rows, :],
                            both[:, block * width : (block + 1) * width],
                            (((0,), (0,)), ((), ())),
                            precision=lax.Precision.HIGHEST,
                            preferred_element_type=jnp.float32,
                        )
                out[owner * examples + e] = total

    args = [*lefts, own, oth]
    out = [jax.ShapeDtypeStruct((2 * examples, width, width), jnp.float32)]
    (sketch,), token = call(
        kernel,
        idx,
        args,
        [whole(a.shape) for a in args],
        out,
        [whole(out[0].shape)],
        "sketch_part",
        (1,),
        (0, 16 * half * width),
        after,
    )
    return sketch, [token]


def body(inputs, cotangent, weight, in_sketch, out_sketch):
    n = lax.axis_size("outp")
    bits = n.bit_length() - 1
    rows, feats = inputs.shape
    hidden = weight.shape[1]
    idx = jnp.stack([lax.axis_index("outp"), lax.axis_index("inp")]).astype(jnp.int32)

    def partner(x, bit):
        return lax.ppermute(x, "outp", [(d, d ^ (1 << bit)) for d in range(n)])

    def swap(x):
        return lax.ppermute(x, "inp", [(0, 1), (1, 0)])

    evens = list(range(2, n, 2))
    chunks = {0: inputs}

    def fetch(masks):
        for mask in masks:
            bit = (mask & -mask).bit_length() - 1
            chunks[mask] = partner(chunks[mask ^ (1 << bit)], bit)

    def hold(masks, after):
        held, token = gate(idx, [chunks[m] for m in masks], after)
        chunks.update(zip(masks, held))
        return token

    grad_other = swap(cotangent)
    singles = [1 << k for k in reversed(range(bits))]
    fetch(singles)

    orders = [list(range(bits)), [1, 0] + list(range(2, bits))]
    tile = pick(feats // PIECES, F_TILE)
    count = feats // PIECES // tile
    msgs, keeps = [], []
    token = []
    for p in range(PIECES):
        outs, t = backward(
            idx,
            cotangent,
            grad_other,
            weight,
            out_sketch if p == 0 else None,
            count,
            tile,
            p * count,
            rows,
            orders[p][0],
            token,
        )
        token = [t]
        msgs.append(partner(outs[0], orders[p][0]))
        keeps.append(outs[1])
        if p == 0:
            right = outs[2]
        if p == 0:
            token = hold(singles, token)
            fetch([m for m in evens if m.bit_count() == 2])
    ready = [m for m in evens if m in chunks]
    while len(ready) < len(evens):
        token = hold(ready, token)
        fetch([m for m in evens if m not in chunks and m & (m - 1) in chunks])
        ready = [m for m in evens if m in chunks]
    crossed, token = join(idx, [chunks[m] for m in evens], token)
    crossed = partner(crossed, 0)

    rights = [right] + [None] * (PIECES - 1)

    def folded(p, step, after):
        done, bit = orders[p][:step], orders[p][step]
        pos = sum(1 for k in range(bit) if k not in done)
        outs, t = fold(idx, keeps[p], msgs[p], rights[p], bit, pos, after)
        msgs[p], keeps[p] = partner(outs[0], bit), outs[1]
        if p == 0:
            rights[p] = outs[2]
        return [t]

    tiles = hidden // pick(hidden, H_TILE)

    def batch_forward(batch, lo, hi, after):
        if batch:
            parts = [(1, chunks[1], 0)] + [(m + 1, crossed, i) for i, m in enumerate(evens)]
        else:
            parts = [(m, chunks[m], 0) for m in [0] + evens]
        outs, t = forward(idx, parts, rows, weight, None if lo else in_sketch, lo, hi, after)
        start = lo * (hidden // tiles)
        return (outs[1], swap(outs[0]), start), outs[-1], [t]

    cut = -(-tiles // 2)
    token = folded(0, 1, token)
    first, left1, token = batch_forward(0, 0, tiles, token)
    token = folded(1, 1, token)
    token = folded(0, 2, token)
    second, left2, token = batch_forward(1, 0, cut, token)
    token = folded(1, 2, token)
    outputs, token = combine(idx, [first], hidden, rows, 0, [], token)
    third, _, token = batch_forward(1, cut, tiles, token)
    for step in range(3, bits):
        for p in range(PIECES):
            token = folded(p, step, token)
    right, token = last_right(idx, rights[0], msgs[0], token)
    right_got = swap(right)
    outputs, token = combine(idx, [second, third], hidden, rows, 1, [outputs], token)
    part, token = sketch_part(idx, [left1, left2], right, right_got, rows, token)
    input_grad = finish(idx, keeps, msgs, token)
    part = (part + swap(part)) * (1.0 / LEN**0.5)
    sketches = part.reshape(part.shape[0], -1)
    return (outputs, input_grad, sketches)


def solution(mesh):
    placed = (
        P(("groups", "outp"), "inp"),
        P(("groups", "inp"), "outp"),
        P("inp", "outp"),
        P(None, "inp"),
        P(None, "outp"),
    )
    return jax.shard_map(
        body,
        mesh=mesh,
        in_specs=placed,
        out_specs=(P(("groups", "inp"), "outp"), P(("groups", "outp"), "inp"), P("groups", None)),
        check_vma=False,
    )
```

```python
import jax
import jax.numpy as jnp
from jax import lax
from jax.experimental import pallas as pl
from jax.experimental.pallas import tpu as pltpu
from jax.sharding import PartitionSpec as P

LEN = 128
LANES = 128
BLK = 16
LN2 = 0.6931471805599453
SPAN = 248.0
SHIFT = 124.0
PIECES = 2
F_TILE = 512
H_TILE = 512
VMEM_MIB = {"backward": 36, "forward": 28}
MIB = 1 << 20
SLOTS = 3
RIGHT_ROWS = 16
RIGHT_PARTS = 2
TIMES = {"gate": 6 * 10**9, "backward_0": 19 * 10**9, "backward_4": 8 * 10**9, "forward": 1 << 34, "fold": 0, "combine": 1 << 34, "sketch_part": 1 << 36, "last_right": 1 << 34}
ANY = pl.BlockSpec(memory_space=pl.ANY)
HBM = pl.BlockSpec(memory_space=pltpu.HBM)


def pick(extent, cap):
    best = LANES
    for t in range(LANES, min(cap, extent) + 1, LANES):
        if extent % t == 0:
            best = t
    return best


def contract_last(a, b):
    return lax.dot_general(a, b, (((1,), (1,)), ((), ())), preferred_element_type=jnp.float32)


def whole(shape):
    return pl.BlockSpec(shape, lambda *_: (0,) * len(shape))


def call(
    kernel, idx, args, specs, out_shape, out_specs, name, grid, work, after, scratch=(), aliases=None
):
    token = jax.ShapeDtypeStruct((8, LANES), jnp.float32)
    n_args, n_after, n_out = len(args), len(after), len(out_shape)

    def with_token(idx, *refs):
        ins = refs[:n_args]
        outs = refs[n_args + n_after :]
        outs[n_out][...] = jnp.zeros((8, LANES), jnp.float32)
        kernel(idx, *ins, *outs[:n_out], *outs[n_out + 1 :])

    out = pl.pallas_call(
        with_token,
        out_shape=list(out_shape) + [token],
        grid_spec=pltpu.PrefetchScalarGridSpec(
            num_scalar_prefetch=1,
            grid=grid,
            in_specs=list(specs) + [ANY] * n_after,
            out_specs=list(out_specs) + [whole(token.shape)],
            scratch_shapes=list(scratch),
        ),
        compiler_params=pltpu.CompilerParams(vmem_limit_bytes=VMEM_MIB.get(name.split("_")[0], 14) * MIB),
        cost_estimate=pl.CostEstimate(
            flops=TIMES.get(name, work[0]), bytes_accessed=work[1], transcendentals=0
        ),
        input_output_aliases=aliases or {},
        name=name,
    )(idx, *args, *after)
    return out[:-1], out[-1]


def encode_rows(tiles, msg, at):
    top = jnp.abs(tiles[0])
    for v in tiles[1:]:
        top = jnp.maximum(top, jnp.abs(v))
    top = jnp.max(top, axis=1, keepdims=True)
    scale = jnp.maximum(top * 1.004, 2.0**-110).astype(jnp.bfloat16).astype(jnp.float32)
    gain = SPAN / scale
    col = 0
    for v in tiles:
        w = jnp.exp2(jnp.abs(v) * gain - SHIFT)
        msg[at, col : col + v.shape[1]] = jnp.where(v < 0, -w, w).astype(jnp.bfloat16)
        col += v.shape[1]
    msg[at, col : col + LANES] = jnp.broadcast_to(scale, (BLK, LANES)).astype(jnp.bfloat16)


def decode_rows(msg, at, tile, count):
    scale = msg[at, tile * count : tile * count + LANES].astype(jnp.float32)[:, :1]
    scale = scale * (1.0 / (SPAN * LN2))
    out = []
    for t in range(count):
        w = msg[at, t * tile : (t + 1) * tile].astype(jnp.float32)
        a = (lax.log(jnp.maximum(jnp.abs(w), 2.0**-SHIFT)) + SHIFT * LN2) * scale
        out.append(jnp.where(w < 0, -a, a))
    return out


def put_right(value, msg):
    base = msg.shape[0] - RIGHT_ROWS
    for q in range(value.shape[0] // RIGHT_ROWS):
        left_over = value[q * RIGHT_ROWS : (q + 1) * RIGHT_ROWS, :]
        for k in range(RIGHT_PARTS):
            part = left_over.astype(jnp.bfloat16)
            lo = (RIGHT_PARTS * q + k) * LANES
            msg[base:, lo : lo + LANES] = part
            left_over = left_over - part.astype(jnp.float32)


def add_right(value, msg):
    base = msg.shape[0] - RIGHT_ROWS
    out = []
    for q in range(value.shape[0] // RIGHT_ROWS):
        lo = RIGHT_PARTS * q * LANES
        parts = [
            msg[base:, lo + k * LANES : lo + (k + 1) * LANES].astype(jnp.float32)
            for k in range(RIGHT_PARTS)
        ]
        got = sum(parts)
        out.append(value[q * RIGHT_ROWS : (q + 1) * RIGHT_ROWS, :] + got)
    return jnp.concatenate(out, axis=0)


def with_bit(c, pos, value):
    low = c & ((1 << pos) - 1)
    return ((c >> pos) << (pos + 1)) + low + value * (1 << pos)


def rows_at(start):
    return pl.ds(pl.multiple_of(start, BLK), BLK)


def backward(idx, own, oth, w, sketch, count, tile, first, rows, bit, after):
    half, hidden = own.shape
    n = 2 * half // rows
    width = count * tile

    def kernel(idx, own, oth, w, *rest):
        if sketch is None:
            msg, keep, x, total, sems, tiles = rest
        else:
            sk, msg, keep, right, x, total, sems, tiles, sk_here = rest
        me, core = idx[0], idx[1]

        def fetch(j):
            at = pl.ds(pl.multiple_of((first + j) * tile, tile), tile)
            slot = lax.rem(j, SLOTS)
            return pltpu.make_async_copy(w.at[at], tiles.at[slot], sems.at[3 + slot])

        copies = [
            pltpu.make_async_copy(own, x.at[core], sems.at[0]),
            pltpu.make_async_copy(oth, x.at[1 - core], sems.at[1]),
        ]
        if sketch is not None:
            copies.append(pltpu.make_async_copy(sk, sk_here, sems.at[2]))
        for c in copies:
            c.start()
        for j in range(min(SLOTS - 1, count)):
            fetch(jnp.int32(j)).start()
        for c in copies:
            c.wait()
        if sketch is not None:
            low, high = jnp.zeros_like(sk_here[...]), sk_here[...]
            first_block = jnp.concatenate([high, low], axis=0)
            second_block = jnp.concatenate([low, high], axis=0)
            right[...] = contract_last(x[core, : half // 2, :], first_block) + contract_last(
                x[core, half // 2 :, :], second_block
            )
            put_right(right[...], msg)

        @pl.loop(0, count)
        def _(j):
            fetch(j).wait()

            @pl.when(j + SLOTS - 1 < count)
            def _():
                fetch(j + SLOTS - 1).start()

            xs = x[...].reshape(2 * half, hidden)
            total[j] = contract_last(xs, tiles[lax.rem(j, SLOTS)]).reshape(n, rows, tile)

        mine = (me >> bit) & 1
        for c in range(n // 2):
            away, here = with_bit(c, bit, 1 - mine), with_bit(c, bit, mine)

            @pl.loop(0, rows // BLK)
            def _(b):
                src = rows_at(b * BLK)
                encode_rows(
                    [total[t, away, src, :] for t in range(count)],
                    msg,
                    rows_at(c * rows + b * BLK),
                )
                for t in range(count):
                    keep[t, c, src, :] = total[t, here, src, :]

    extra = 0 if sketch is None else RIGHT_ROWS
    out = [
        jax.ShapeDtypeStruct((n // 2 * rows + extra, width + LANES), jnp.bfloat16),
        jax.ShapeDtypeStruct((count, n // 2, rows, tile), jnp.float32),
    ]
    args = [own, oth, w]
    specs = [HBM, ANY, HBM]
    scratch = [
        pltpu.VMEM((2, half, hidden), jnp.bfloat16),
        pltpu.VMEM((count, n, rows, tile), jnp.float32),
        pltpu.SemaphoreType.DMA((3 + SLOTS,)),
        pltpu.VMEM((SLOTS, tile, hidden), w.dtype),
    ]
    if sketch is not None:
        args.append(sketch)
        specs.append(HBM)
        out.append(jax.ShapeDtypeStruct((half // 2, 2 * sketch.shape[0]), jnp.float32))
        scratch.append(pltpu.VMEM(sketch.shape, sketch.dtype))
    return call(
        kernel,
        idx,
        args,
        specs,
        out,
        [whole(o.shape) for o in out],
        f"backward_{first}",
        (1,),
        (4 * half * hidden * width, 2 * hidden * width + 12 * half * width),
        after,
        scratch,
    )


def fold(idx, keep, got, right, bit, pos, after):
    count, m, rows, tile = keep.shape
    extra = 0 if right is None else RIGHT_ROWS

    def kernel(idx, keep, got, *refs):
        if extra:
            right, msg, rest, total = refs
            total[...] = add_right(right[...], got)
            put_right(total[...], msg)
        else:
            msg, rest = refs
        mine = (idx[0] >> bit) & 1
        for c in range(m // 2):
            away, here = with_bit(c, pos, 1 - mine), with_bit(c, pos, mine)

            @pl.loop(0, rows // BLK)
            def _(b):
                src = rows_at(b * BLK)
                plus = decode_rows(got, rows_at(away * rows + b * BLK), tile, count)
                encode_rows(
                    [keep[t, away, src, :] + plus[t] for t in range(count)],
                    msg,
                    rows_at(c * rows + b * BLK),
                )
                plus = decode_rows(got, rows_at(here * rows + b * BLK), tile, count)
                for t in range(count):
                    rest[t, c, src, :] = keep[t, here, src, :] + plus[t]

    args = [keep, got] + ([right] if extra else [])
    out = [
        jax.ShapeDtypeStruct((m // 2 * rows + extra, got.shape[1]), jnp.bfloat16),
        jax.ShapeDtypeStruct((count, m // 2, rows, tile), jnp.float32),
    ] + ([jax.ShapeDtypeStruct(right.shape, jnp.float32)] if extra else [])
    return call(
        kernel,
        idx,
        args,
        [whole(a.shape) for a in args],
        out,
        [whole(o.shape) for o in out],
        "fold",
        (1,),
        (0, 12 * keep.size),
        after,
    )


def finish(idx, keeps, gots, after):
    count, _, rows, tile = keeps[0].shape
    pieces = len(keeps)

    def kernel(idx, *refs):
        out = refs[-1]
        for p in range(pieces):

            @pl.loop(0, rows // BLK)
            def _(b):
                at = rows_at(b * BLK)
                plus = decode_rows(refs[pieces + p], at, tile, count)
                for t in range(count):
                    lo = (p * count + t) * tile
                    out[at, lo : lo + tile] = (refs[p][t, 0, at, :] + plus[t]).astype(
                        jnp.bfloat16
                    )

    args = list(keeps) + list(gots)
    out = [jax.ShapeDtypeStruct((rows, pieces * count * tile), jnp.bfloat16)]
    (grad,), _ = call(
        kernel,
        idx,
        args,
        [whole(a.shape) for a in args],
        out,
        [whole(out[0].shape)],
        "finish",
        (1,),
        (0, 16 * rows * count * tile),
        after,
    )
    return grad


def gate(idx, arrays, after):
    k = len(arrays)

    def kernel(idx, *refs):
        pass

    out, token = call(
        kernel,
        idx,
        arrays,
        [ANY] * k,
        [jax.ShapeDtypeStruct(a.shape, a.dtype) for a in arrays],
        [ANY] * k,
        "gate",
        (1,),
        (0, 0),
        after,
        aliases={1 + i: i for i in range(k)},
    )
    return list(out), [token]


def join(idx, arrays, after):
    rows, width = arrays[0].shape
    k = len(arrays)

    def kernel(idx, *refs):
        out, sems = refs[-2:]
        copies = [
            pltpu.make_async_copy(refs[i], out.at[pl.ds(i * rows, rows)], sems.at[i])
            for i in range(k)
        ]
        for c in copies:
            c.start()
        for c in copies:
            c.wait()

    (out,), token = call(
        kernel,
        idx,
        arrays,
        [ANY] * k,
        [jax.ShapeDtypeStruct((k * rows, width), arrays[0].dtype)],
        [ANY],
        "join",
        (1,),
        (0, 0),
        after,
        [pltpu.SemaphoreType.DMA((k,))],
    )
    return out, [token]


def last_right(idx, right, got, after):
    def kernel(idx, right, got, out):
        out[...] = add_right(right[...], got)

    out = [jax.ShapeDtypeStruct(right.shape, jnp.float32)]
    specs = [whole(right.shape), whole(got.shape)]
    work = (0, 2 * got.size)
    (total,), token = call(
        kernel, idx, [right, got], specs, out, specs[:1], "last_right", (1,), work, after
    )
    return total, [token]


def forward(idx, chunks, rows, w, sketch, lo, hi, after):
    feats = w.shape[0]
    m = len(chunks)
    tile = pick(w.shape[1], H_TILE)
    hidden = (hi - lo) * tile
    part = m // 2 * rows

    count = hi - lo

    def kernel(idx, *refs):
        if sketch is None:
            w, send, keep, x, sems, tiles, outs, out_sems = refs[m:]
        else:
            w, sk, send, keep, left, x, sems, tiles, outs, out_sems = refs[m:]
        me, core = idx[0], idx[1]

        def fetch(j):
            at = pl.ds(pl.multiple_of((lo + j) * tile, tile), tile)
            slot = lax.rem(j, SLOTS)
            return pltpu.make_async_copy(w.at[:, at], tiles.at[slot], sems.at[m + slot])

        def give(j):
            at = pl.ds(pl.multiple_of(j * tile, tile), tile)
            slot = lax.rem(j, 2)
            return [
                pltpu.make_async_copy(outs.at[slot, side], ref.at[:, at], out_sems.at[slot, side])
                for side, ref in enumerate((send, keep))
            ]

        copies = []
        for i, (mask, _, block) in enumerate(chunks):
            d = me ^ mask
            side = 1 - ((d // m) ^ core)
            to = pl.ds(pl.multiple_of(side * part + ((d % m) >> 1) * rows, BLK), rows)
            src = refs[i].at[pl.ds(block * rows, rows)]
            copies.append(pltpu.make_async_copy(src, x.at[to], sems.at[i]))
        for c in copies:
            c.start()
        for j in range(min(SLOTS - 1, count)):
            fetch(jnp.int32(j)).start()
        for c in copies:
            c.wait()
        if sketch is not None:
            left[...] = contract_last(x[...], sk[...])

        @pl.loop(0, count)
        def _(j):
            fetch(j).wait()

            @pl.when(j + SLOTS - 1 < count)
            def _():
                fetch(j + SLOTS - 1).start()

            t = jnp.dot(x[...], tiles[lax.rem(j, SLOTS)], preferred_element_type=jnp.float32)

            @pl.when(j >= 2)
            def _():
                for c in give(j - 2):
                    c.wait()

            outs[lax.rem(j, 2)] = t.reshape(2, part, tile)
            for c in give(j):
                c.start()

        for j in range(max(0, count - 2), count):
            for c in give(jnp.int32(j)):
                c.wait()

    args = [c[1] for c in chunks] + [w]
    specs = [ANY] * m + [HBM]
    out = [jax.ShapeDtypeStruct((part, hidden), jnp.float32)] * 2
    out_specs = [ANY, ANY]
    if sketch is not None:
        args.append(sketch)
        specs.append(whole(sketch.shape))
        out.append(jax.ShapeDtypeStruct((2 * part, sketch.shape[0]), jnp.float32))
        out_specs.append(whole(out[2].shape))
    return call(
        kernel,
        idx,
        args,
        specs,
        out,
        out_specs,
        "forward",
        (1,),
        (4 * part * feats * hidden, 2 * feats * hidden + 8 * part * hidden),
        after,
        [
            pltpu.VMEM((2 * part, feats), jnp.bfloat16),
            pltpu.SemaphoreType.DMA((m + SLOTS,)),
            pltpu.VMEM((SLOTS, feats, tile), w.dtype),
            pltpu.VMEM((2, 2, part, tile), jnp.float32),
            pltpu.SemaphoreType.DMA((2, 2)),
        ],
    )


def combine(idx, pieces, total, rows, batch, before, after):
    part = pieces[0][0].shape[0]
    m = part // rows

    def kernel(idx, *refs):
        out, sems = refs[-2 - len(pieces)], refs[-1]
        mine = (idx[0] & 1) ^ batch
        copies = []
        for k, (keep, _, lo) in enumerate(pieces):
            x = refs[k - 1 - len(pieces)]
            x[...] = (refs[2 * k][...] + refs[2 * k + 1][...]).astype(jnp.bfloat16)
            for i in range(m):
                to = pl.ds(pl.multiple_of((2 * i + mine) * rows, BLK), rows)
                dst = out.at[to, pl.ds(lo, keep.shape[1])]
                copies.append(
                    pltpu.make_async_copy(x.at[pl.ds(i * rows, rows)], dst, sems.at[k, i])
                )
                copies[-1].start()
        for c in copies:
            c.wait()

    flat = [a for keep, got, _ in pieces for a in (keep, got)]
    width = sum(keep.shape[1] for keep, _, _ in pieces)
    (out,), token = call(
        kernel,
        idx,
        flat + before,
        [whole(a.shape) for a in flat] + [HBM] * len(before),
        [jax.ShapeDtypeStruct((2 * part, total), jnp.bfloat16)],
        [HBM],
        "combine",
        (1,),
        (0, 10 * part * width),
        after,
        [pltpu.VMEM(keep.shape, jnp.bfloat16) for keep, _, _ in pieces]
        + [pltpu.SemaphoreType.DMA((len(pieces), m))],
        aliases={1 + len(flat): 0} if before else None,
    )
    return out, [token]


def sketch_part(idx, lefts, own, oth, rows, after):
    packed, lanes = own.shape
    width = lanes // 2
    half = 2 * packed
    part = half // 2
    examples = half // LEN

    def kernel(idx, first, second, own, oth, out):
        me, core = idx[0], idx[1]
        for side, right in ((0, oth), (1, own)):
            owner = 1 - (side ^ core)
            for e in range(examples):
                total = jnp.zeros((width, width), jnp.float32)
                for i in range(part // rows):
                    if 2 * i * rows // LEN != e:
                        continue
                    block, start = divmod(2 * i * rows, packed)
                    for batch, left in enumerate((first, second)):
                        at = start + ((me & 1) ^ batch) * rows
                        lo = side * part + i * rows
                        both = right[pl.ds(pl.multiple_of(at, BLK), rows), :]
                        total += lax.dot_general(
                            left[lo : lo + rows, :],
                            both[:, block * width : (block + 1) * width],
                            (((0,), (0,)), ((), ())),
                            precision=lax.Precision.HIGHEST,
                            preferred_element_type=jnp.float32,
                        )
                out[owner * examples + e] = total

    args = [*lefts, own, oth]
    out = [jax.ShapeDtypeStruct((2 * examples, width, width), jnp.float32)]
    (sketch,), token = call(
        kernel,
        idx,
        args,
        [whole(a.shape) for a in args],
        out,
        [whole(out[0].shape)],
        "sketch_part",
        (1,),
        (0, 16 * half * width),
        after,
    )
    return sketch, [token]


def body(inputs, cotangent, weight, in_sketch, out_sketch):
    n = lax.axis_size("outp")
    bits = n.bit_length() - 1
    rows, feats = inputs.shape
    hidden = weight.shape[1]
    idx = jnp.stack([lax.axis_index("outp"), lax.axis_index("inp")]).astype(jnp.int32)

    def partner(x, bit):
        return lax.ppermute(x, "outp", [(d, d ^ (1 << bit)) for d in range(n)])

    def swap(x):
        return lax.ppermute(x, "inp", [(0, 1), (1, 0)])

    evens = list(range(2, n, 2))
    chunks = {0: inputs}

    def fetch(masks):
        for mask in masks:
            bit = (mask & -mask).bit_length() - 1
            chunks[mask] = partner(chunks[mask ^ (1 << bit)], bit)

    def hold(masks, after):
        held, token = gate(idx, [chunks[m] for m in masks], after)
        chunks.update(zip(masks, held))
        return token

    grad_other = swap(cotangent)
    singles = [1 << k for k in reversed(range(bits))]
    fetch(singles)

    orders = [list(range(bits)), [1, 0] + list(range(2, bits))]
    tile = pick(feats // PIECES, F_TILE)
    count = feats // PIECES // tile
    msgs, keeps = [], []
    token = []
    for p in range(PIECES):
        outs, t = backward(
            idx,
            cotangent,
            grad_other,
            weight,
            out_sketch if p == 0 else None,
            count,
            tile,
            p * count,
            rows,
            orders[p][0],
            token,
        )
        token = [t]
        msgs.append(partner(outs[0], orders[p][0]))
        keeps.append(outs[1])
        if p == 0:
            right = outs[2]
        if p == 0:
            token = hold([singles[0], 1], token)
            fetch([m for m in evens if m.bit_count() == 2])
    ready = [m for m in evens if m in chunks]
    while len(ready) < len(evens):
        token = hold(ready, token)
        fetch([m for m in evens if m not in chunks and m & (m - 1) in chunks])
        ready = [m for m in evens if m in chunks]
    crossed, token = join(idx, [chunks[m] for m in evens], token)
    crossed = partner(crossed, 0)

    rights = [right] + [None] * (PIECES - 1)

    def folded(p, step, after):
        done, bit = orders[p][:step], orders[p][step]
        pos = sum(1 for k in range(bit) if k not in done)
        outs, t = fold(idx, keeps[p], msgs[p], rights[p], bit, pos, after)
        msgs[p], keeps[p] = partner(outs[0], bit), outs[1]
        if p == 0:
            rights[p] = outs[2]
        return [t]

    tiles = hidden // pick(hidden, H_TILE)

    def batch_forward(batch, lo, hi, after):
        if batch:
            parts = [(1, chunks[1], 0)] + [(m + 1, crossed, i) for i, m in enumerate(evens)]
        else:
            parts = [(m, chunks[m], 0) for m in [0] + evens]
        outs, t = forward(idx, parts, rows, weight, None if lo else in_sketch, lo, hi, after)
        start = lo * (hidden // tiles)
        return (outs[1], swap(outs[0]), start), outs[-1], [t]

    cut = -(-tiles // 2)
    token = folded(0, 1, token)
    first, left1, token = batch_forward(0, 0, tiles, token)
    token = folded(1, 1, token)
    token = folded(0, 2, token)
    second, left2, token = batch_forward(1, 0, cut, token)
    token = folded(1, 2, token)
    outputs, token = combine(idx, [first], hidden, rows, 0, [], token)
    third, _, token = batch_forward(1, cut, tiles, token)
    for step in range(3, bits):
        for p in range(PIECES):
            token = folded(p, step, token)
    right, token = last_right(idx, rights[0], msgs[0], token)
    right_got = swap(right)
    outputs, token = combine(idx, [second, third], hidden, rows, 1, [outputs], token)
    part, token = sketch_part(idx, [left1, left2], right, right_got, rows, token)
    input_grad = finish(idx, keeps, msgs, token)
    part = (part + swap(part)) * (1.0 / LEN**0.5)
    sketches = part.reshape(part.shape[0], -1)
    return (outputs, input_grad, sketches)


def solution(mesh):
    placed = (
        P(("groups", "outp"), "inp"),
        P(("groups", "inp"), "outp"),
        P("inp", "outp"),
        P(None, "inp"),
        P(None, "outp"),
    )
    return jax.shard_map(
        body,
        mesh=mesh,
        in_specs=placed,
        out_specs=(P(("groups", "inp"), "outp"), P(("groups", "outp"), "inp"), P("groups", None)),
        check_vma=False,
    )
```
